32 devices in a mesh: hst: 8 (over z, y), grp: 4 (over x, core).
Axes of the slice: x: 2, y: 2, z: 4, core: 2. Of those that a mesh axis runs over, the one named last changes fastest.
Arguments:
- queries: bfloat16 [16384, 1536], P(('hst', 'grp')), may hold values from -5 to 5
- keys_values: bfloat16 [2, 16384, 1536], P(None, ('hst', 'grp')), may hold values from -5 to 5
- token_ids: int32 [16384], replicated, may hold values from 0 to 4095
- lengths: int32 [32], replicated, may hold values from 1 to 512, 12288 in all
- suffix_queries: bfloat16 [1024, 1536], P('hst', 'grp'), may hold values from -5 to 5
- suffix_kv: bfloat16 [2, 1024, 1536], P(None, 'hst', 'grp'), may hold values from -5 to 5
Outputs:
- context_out: bfloat16 [16384, 1536], P(('hst', 'grp'))
- suffix_out: bfloat16 [1024, 1536], P('hst', 'grp')
The draws below stay inside these ranges and needn't reach their ends.
All inputs are finite; a program needn't handle non-finite values.
Results may differ from the reference program's by a relative error of at most 0.0029.
Values may be sent and summed in bfloat16 or wider, within the bound.
No kernel may reach another device: no remote copies, remote signals or barrier semaphores. Data moves between devices by JAX's collectives and lax.ppermute only.
A program may use at most 128 MiB of HBM per device.

```python
import math
import jax
import jax.numpy as jnp
import numpy as np
from jax import lax

HEADS = 12
HSZ = 128
VOC = 4096
BLK = 512
QS = 1024
HD = 1536
NAMB = 512
NBLK = 32
NTOK = 16384
N_HST = 8
N_GRP = 4


def query_law(key, rows):
    return jnp.clip(1.7 * jax.random.normal(key, (rows, HD)), -5.0, 5.0)


def key_law(key, rows):
    values = jnp.clip(jax.random.normal(jax.random.fold_in(key, 7), (rows, HD)), -5.0, 5.0)
    keys = jnp.clip(1.7 * jax.random.normal(key, (rows, HD)), -5.0, 5.0)
    return jnp.stack([keys, values]).astype(jnp.bfloat16)


def draw_queries(key, part):
    key = jax.random.fold_in(key, 1)
    return query_law(key, NTOK).astype(jnp.bfloat16)


def draw_keys_values(key, part):
    key = jax.random.fold_in(key, 2)
    return key_law(key, NTOK)


def draw_suffix_queries(key, part):
    key = jax.random.fold_in(key, 3)
    return query_law(key, QS).astype(jnp.bfloat16)


def draw_suffix_kv(key, part):
    key = jax.random.fold_in(key, 4)
    return key_law(key, QS)


def plant(array, rng, least, top_value):
    longest = array.shape.index(max(array.shape))
    spots = []
    for shift in (0, 1):
        where = [jax.random.randint(jax.random.fold_in(rng, axis), (), 0, length) for axis, length in enumerate(array.shape)]
        where[longest] = (where[longest] + shift) % array.shape[longest]
        spots.append(tuple(where))
    return array.at[spots[0]].set(least).at[spots[1]].set(top_value)


def profile(count, total, bound, lean):
    loads = [(1 << 20) // math.isqrt(grade ** lean) + 1 for grade in range(2, count + 1)]
    surplus, holding = total - bound - (count - 1), [1] * (count - 1)
    while surplus > 0:
        movable = [i for i in range(count - 1) if holding[i] < bound]
        whole, left = sum([loads[i] for i in movable]), surplus
        for i in movable:
            extra = min(bound - holding[i], max(1, left * loads[i] // whole), surplus)
            holding[i] = holding[i] + extra
            surplus = surplus - extra
    return np.array([bound] + holding)


def uneven_parts(own_key, number_of, total, reach, skew):
    if number_of == 2:
        one = jax.random.randint(own_key, (), max(1, total - reach), min(reach, total - 1) + 1)
        return jnp.stack([one, total - one])
    tallies = jnp.asarray(profile(number_of, total, reach, skew), jnp.int32)
    couples = (number_of - 1) // 2
    donor, sink = tallies[1:1 + 2 * couples:2], tallies[2:2 + 2 * couples:2]
    room = jnp.minimum(donor - 1, reach - sink)
    shifted = jax.random.randint(jax.random.fold_in(own_key, 1), (couples,), 0, 1 << 20) % (room + 1)
    tallies = tallies.at[1:1 + 2 * couples:2].set(donor - shifted).at[2:2 + 2 * couples:2].set(sink + shifted)
    return tallies[jax.random.permutation(jax.random.fold_in(own_key, 2), number_of)]


def setup_inputs(seed: int = 0) -> dict:
    streams_of = jax.random.split(jax.random.key(seed), 7)
    queries = draw_queries(jax.random.fold_in(streams_of[6], 71), 0)
    keys_values = draw_keys_values(jax.random.fold_in(streams_of[6], 71), 0)
    token_ids = plant(jax.random.randint(streams_of[2], (NTOK,), 0, VOC), jax.random.fold_in(streams_of[2], 1), 0, VOC - 1).astype(jnp.int32)
    lengths = uneven_parts(streams_of[3], NBLK, 3 * NBLK * BLK // 4, BLK, 2).astype(jnp.int32)
    suffix_queries = draw_suffix_queries(jax.random.fold_in(streams_of[6], 71), 0)
    suffix_kv = draw_suffix_kv(jax.random.fold_in(streams_of[6], 71), 0)
    return dict(queries=queries, keys_values=keys_values, token_ids=token_ids, lengths=lengths, suffix_queries=suffix_queries, suffix_kv=suffix_kv)


NEG = -1e+30

def attend(q, keys, values, valid):
    scale = 1.0 / math.sqrt(HSZ)
    s = jnp.einsum('qhd,khd->hqk', q, keys) * scale
    masked = jnp.where(valid[None], s, NEG)
    top = lax.optimization_barrier(jnp.max(masked, axis=-1))
    weights = jnp.where(valid[None], jnp.exp(masked - top[..., None]), 0.0)
    total = lax.optimization_barrier(jnp.sum(weights, axis=-1))
    rounded = lax.optimization_barrier(weights.astype(jnp.bfloat16))
    mixed = jnp.einsum('hqk,khd->qhd', rounded.astype(jnp.float32), values)
    return (top.T, total.T, mixed)

def reference(queries, keys_values, token_ids, lengths, suffix_queries, suffix_kv):
    clear = token_ids >= NAMB
    places = jnp.arange(BLK)
    anchor = keys_values[:, :BLK]
    anchor_ok = clear[:BLK] & (places < lengths[0])

    def context_block(block):
        start = block * BLK
        q = lax.dynamic_slice_in_dim(queries, start, BLK, 0).astype(jnp.float32).reshape(BLK, HEADS, HSZ)
        own = lax.dynamic_slice_in_dim(keys_values, start, BLK, 1)
        both = jnp.concatenate([anchor, own], axis=1).astype(jnp.float32).reshape(2, 2 * BLK, HEADS, HSZ)
        own_len = lengths[block]
        own_ok = lax.dynamic_slice_in_dim(clear, start, BLK, 0) & (places < own_len)
        causal = places[None, :] <= places[:, None]
        own_valid = causal & (own_ok[None, :] | (places[None, :] == places[:, None]))
        anchor_valid = jnp.broadcast_to((anchor_ok & (block > 0))[None, :], (BLK, BLK))
        valid = jnp.concatenate([anchor_valid, own_valid], axis=1)
        top, total, mixed = attend(q, both[0], both[1], valid)
        out = mixed / total[:, :, None]
        out = jnp.where((places < own_len)[:, None, None], out, 0.0)
        return out.astype(jnp.bfloat16).reshape(BLK, HD)
    context_out = lax.map(context_block, jnp.arange(N_HST * N_GRP)).reshape(NTOK, HD)
    span = N_GRP * BLK
    share = QS // N_HST
    width_q = min(512, QS)

    def group_step(carry, group):
        first = group * span
        ctx = lax.dynamic_slice_in_dim(keys_values, first, span, 1)
        suf = lax.dynamic_slice_in_dim(suffix_kv, group * share, share, 1)
        both = jnp.concatenate([ctx, suf], axis=1).astype(jnp.float32).reshape(2, span + share, HEADS, HSZ)
        lens = lax.dynamic_slice_in_dim(lengths, group * N_GRP, N_GRP, 0)
        ctx_ok = lax.dynamic_slice_in_dim(clear, first, span, 0) & (jnp.arange(span) % BLK < jnp.repeat(lens, BLK, total_repeat_length=span))
        spos = group * share + jnp.arange(share)

        def piece(index):
            q = lax.dynamic_slice_in_dim(suffix_queries, index * width_q, width_q, 0).astype(jnp.float32).reshape(width_q, HEADS, HSZ)
            qpos = index * width_q + jnp.arange(width_q)
            valid = jnp.concatenate([jnp.broadcast_to(ctx_ok[None, :], (width_q, span)), spos[None, :] <= qpos[:, None]], axis=1)
            return attend(q, both[0], both[1], valid)
        tops, totals, mixed = lax.map(piece, jnp.arange(QS // width_q))
        tops = tops.reshape(QS, HEADS)
        totals = totals.reshape(QS, HEADS)
        mixed = mixed.reshape(QS, HEADS, HSZ)
        best, summed, acc = carry
        upper = jnp.maximum(best, tops)
        old_factor = jnp.exp(best - upper)
        new_factor = jnp.exp(tops - upper)
        summed = summed * old_factor + totals * new_factor
        acc = acc * old_factor[..., None] + mixed * new_factor[..., None]
        return ((upper, summed, acc), None)
    start_state = (jnp.full((QS, HEADS), NEG, jnp.float32), jnp.zeros((QS, HEADS), jnp.float32), jnp.zeros((QS, HEADS, HSZ), jnp.float32))
    final, unused = lax.scan(group_step, start_state, jnp.arange(N_HST))
    suffix_out = (final[2] / final[1][..., None]).astype(jnp.bfloat16).reshape(QS, HD)
    return (context_out, suffix_out)
```

```python
import functools
import math

import jax
import jax.numpy as jnp
from jax import lax
from jax.experimental import pallas as pl
from jax.experimental.pallas import tpu as pltpu
from jax.sharding import PartitionSpec as P

HSZ = 128
NAMB = 512
NEG = -1e30
FLOOR = -1e4
SCALE = 1.0 / math.sqrt(HSZ)
C2 = SCALE * math.log2(math.e)
BOTH = ("hst", "grp")


def dot_t(a, b):
    return lax.dot_general(a, b, (((1,), (1,)), ((), ())), preferred_element_type=jnp.float32)


def dot(a, b):
    return lax.dot_general(a, b, (((1,), (0,)), ((), ())), preferred_element_type=jnp.float32)


def softmax_mix(scores, values):
    top = functools.reduce(jnp.maximum, [jnp.max(s, axis=-1, keepdims=True) for s in scores])
    base = top * C2
    total = 0.0
    mixed = 0.0
    for s, v in zip(scores, values):
        w = jnp.exp2(s * C2 - base)
        total = total + jnp.sum(w, axis=-1, keepdims=True)
        mixed = mixed + dot(w.astype(jnp.bfloat16), v)
    return top, total, mixed


def pack_kernel(kv_ref, out_ref):
    out_ref[0, 0] = kv_ref[0]


def pack(kv, groups):
    _, rows, width = kv.shape
    part = width // groups
    return pl.pallas_call(
        pack_kernel,
        grid=(groups, 2),
        in_specs=[pl.BlockSpec((1, rows, part), lambda g, s: (s, 0, g))],
        out_specs=pl.BlockSpec((1, 1, rows, part), lambda g, s: (g, s, 0, 0)),
        out_shape=jax.ShapeDtypeStruct((groups, 2, rows, part), kv.dtype),
        cost_estimate=pl.CostEstimate(flops=0, bytes_accessed=4 * kv.size, transcendentals=0),
        name="pack_heads",
    )(kv)


def suffix_kernel(groups, sub, share, at_ref, q_ref, kv_ref, sk_ref, bias_ref, n_ref, st_ref):
    host = at_ref[0]
    step, head = pl.program_id(0), pl.program_id(1)
    tile = q_ref.shape[0]

    @pl.when(head == 0)
    def _():
        st_ref[...] = jnp.zeros_like(st_ref)

    for first in range(0, tile, sub):
        q = q_ref[first : first + sub, :]
        scores = []
        values = []
        for g in range(groups):
            bias = bias_ref[pl.ds(host * groups + g, 1), :]
            scores.append(dot_t(q, kv_ref[g, 0]) + bias)
            values.append(kv_ref[g, 1])
        s = dot_t(q, sk_ref[0])
        qpos = step * tile + first + lax.broadcasted_iota(jnp.int32, s.shape, 0)
        spos = host * share + lax.broadcasted_iota(jnp.int32, s.shape, 1)
        scores.append(jnp.where(spos <= qpos, s, NEG))
        values.append(sk_ref[1])
        top, total, mixed = softmax_mix(scores, values)
        n = mixed / total
        size = jnp.max(jnp.abs(n), axis=-1, keepdims=True)
        size = jnp.where(size > 0.0, size, 1.0)
        n_ref[first : first + sub, :] = n / size
        lse = jnp.maximum(top * SCALE + jnp.log(total), FLOOR)
        lane = lax.broadcasted_iota(jnp.int32, (sub, 128), 1)
        turned = jnp.where(lane == 0, lse, size).T
        for c in range(sub // share):
            chunk = first // share + c
            st_ref[chunk, pl.ds(2 * head, 2), :] = turned[0:2, c * share : (c + 1) * share]


def suffix_attend(at, q, kv, sk, bias):
    groups, _, rows, width = kv.shape
    total_q = q.shape[0]
    share = sk.shape[1]
    heads = width // HSZ
    tile, sub = min(512, total_q), min(256, total_q)
    seen = groups * rows + share
    return pl.pallas_call(
        functools.partial(suffix_kernel, groups, sub, share),
        grid_spec=pltpu.PrefetchScalarGridSpec(
            num_scalar_prefetch=1,
            grid=(total_q // tile, heads),
            in_specs=[
                pl.BlockSpec((tile, HSZ), lambda i, h, at: (i, h)),
                pl.BlockSpec((groups, 2, rows, HSZ), lambda i, h, at: (0, 0, 0, h)),
                pl.BlockSpec((2, share, HSZ), lambda i, h, at: (0, 0, h)),
                pl.BlockSpec(bias.shape, lambda i, h, at: (0, 0)),
            ],
            out_specs=[
                pl.BlockSpec((tile, HSZ), lambda i, h, at: (i, h)),
                pl.BlockSpec((tile // share, 8, share), lambda i, h, at: (i, 0, 0)),
            ],
        ),
        out_shape=[
            jax.ShapeDtypeStruct((total_q, width), jnp.float32),
            jax.ShapeDtypeStruct((total_q // share, 8, share), jnp.float32),
        ],
        compiler_params=pltpu.CompilerParams(vmem_limit_bytes=48 * 1024 * 1024),
        cost_estimate=pl.CostEstimate(
            flops=8 * total_q * seen * width,
            bytes_accessed=2 * kv.size + 2 * q.size + 4 * q.size,
            transcendentals=total_q * seen * heads,
        ),
        name="suffix_attend",
    )(at, q, kv, sk, bias)


def context_kernel(pieces, at_ref, len_ref, q_ref, kv_ref, bias_ref, *rest):
    piece_refs, (out_ref, diag_ref, anchor_ref) = rest[:pieces], rest[pieces:]
    block, mine = at_ref[2], at_ref[3]
    rows = q_ref.shape[0]
    half = rows // 2
    part = rows // pieces
    own = bias_ref[pl.ds(block, 1), :]

    @pl.when(pl.program_id(0) == 0)
    def _():
        row = lax.broadcasted_iota(jnp.int32, (half, half), 0)
        col = lax.broadcasted_iota(jnp.int32, (half, half), 1)
        for t in range(2):
            ok = own[:, t * half : (t + 1) * half]
            diag_ref[t] = jnp.where(col == row, 0.0, jnp.where(col < row, ok, NEG))

    for k in range(pieces):
        place = pl.multiple_of(jnp.bitwise_xor(mine, k) * part, part)
        anchor_ref[:, pl.ds(place, part), :] = piece_refs[k][...]
    anchor_bias = jnp.where(block > 0, bias_ref[0:1, :], NEG)
    keys, values = kv_ref[0], kv_ref[1]
    for t in range(2):
        q = q_ref[t * half : (t + 1) * half, :]
        scores = [dot_t(q, anchor_ref[0]) + anchor_bias]
        mix = [anchor_ref[1]]
        if t == 1:
            scores.append(dot_t(q, keys[:half]) + own[:, :half])
            mix.append(values[:half])
        scores.append(dot_t(q, keys[t * half : (t + 1) * half]) + diag_ref[t])
        mix.append(values[t * half : (t + 1) * half])
        _, total, mixed = softmax_mix(scores, mix)
        place = t * half + lax.broadcasted_iota(jnp.int32, mixed.shape, 0)
        out = jnp.where(place < len_ref[block], mixed / total, 0.0)
        out_ref[t * half : (t + 1) * half, :] = out.astype(out_ref.dtype)


def context_attend(at, lengths, q, kv, bias, anchor):
    rows, width = q.shape
    heads = width // HSZ
    pieces = len(anchor)
    part = rows // pieces
    half = rows // 2
    column = lambda h, *_: (0, h)
    return pl.pallas_call(
        functools.partial(context_kernel, pieces),
        grid_spec=pltpu.PrefetchScalarGridSpec(
            num_scalar_prefetch=2,
            grid=(heads,),
            in_specs=[
                pl.BlockSpec((rows, HSZ), column),
                pl.BlockSpec((2, rows, HSZ), lambda h, *_: (0, 0, h)),
                pl.BlockSpec(bias.shape, lambda h, *_: (0, 0)),
            ]
            + [pl.BlockSpec((2, part, HSZ), lambda h, *_: (0, 0, h))] * pieces,
            out_specs=pl.BlockSpec((rows, HSZ), column),
            scratch_shapes=[
                pltpu.VMEM((2, half, half), jnp.float32),
                pltpu.VMEM((2, rows, HSZ), jnp.bfloat16),
            ],
        ),
        out_shape=jax.ShapeDtypeStruct((rows, width), q.dtype),
        compiler_params=pltpu.CompilerParams(vmem_limit_bytes=48 * 1024 * 1024),
        cost_estimate=pl.CostEstimate(
            flops=8 * rows * rows * width,
            bytes_accessed=12 * q.size,
            transcendentals=2 * rows * rows * heads,
        ),
        name="context_attend",
    )(at, lengths, q, kv, bias, *anchor)


def spread_anchor(kv, hosts, groups):
    count = 2 * groups
    part = kv.shape[1] // count
    first = (lax.axis_index("hst") == 0) & (lax.axis_index("grp") == 0)
    piece = jnp.where(first, kv[:, :part], 0.0)
    for p in range(1, count):
        piece = piece + lax.ppermute(kv[:, p * part : (p + 1) * part], BOTH, [(0, p)])
    far = hosts // 2
    while far >= 2:
        pairs = [(h, h + far) for h in range(hosts) if h % (2 * far) < 2]
        piece = piece + lax.ppermute(piece, "hst", pairs)
        far //= 2
    swap = lambda x, axis, n, k: lax.ppermute(x, axis, [(i, i ^ k) for i in range(n)])
    held = {0: piece}
    held[groups] = swap(piece, "hst", hosts, 1)
    k = groups // 2
    while k >= 1:
        for have in list(held):
            held[have ^ k] = swap(held[have], "grp", groups, k)
        k //= 2
    return [held[k] for k in range(count)]


def combine(parts, stats, share):
    hosts, _, width = parts.shape
    heads = width // HSZ
    lse, size = stats[:, 0 : 2 * heads : 2, :], stats[:, 1 : 2 * heads : 2, :]
    factor = jnp.exp(lse - jnp.max(lse, axis=0, keepdims=True))
    factor = factor / jnp.sum(factor, axis=0, keepdims=True) * size
    factor = factor.transpose(0, 2, 1)[..., None]
    out = jnp.sum(parts.astype(jnp.float32).reshape(hosts, share, heads, HSZ) * factor, axis=0)
    return out.astype(jnp.bfloat16).reshape(share, width)


def per_device(queries, keys_values, token_ids, lengths, suffix_queries, suffix_kv):
    hosts, groups = lax.axis_size("hst"), lax.axis_size("grp")
    host, group = lax.axis_index("hst"), lax.axis_index("grp")
    rows = queries.shape[0]
    share = suffix_queries.shape[0]
    at = jnp.stack([host, group, host * groups + group, (host % 2) * groups + group]).astype(jnp.int32)
    swapped = lax.all_to_all(pack(keys_values, groups), "grp", split_axis=0, concat_axis=0, tiled=True)
    gathered = lax.all_gather(suffix_queries, "hst", axis=0, tiled=True)
    anchor = spread_anchor(keys_values, hosts, groups)
    seen = (token_ids.reshape(-1, rows) >= NAMB) & (jnp.arange(rows)[None, :] < lengths[:, None])
    bias = jnp.where(seen, 0.0, NEG).astype(jnp.float32)
    parts, stats = suffix_attend(at, gathered, swapped, suffix_kv, bias)
    parts = parts.astype(jnp.float16).reshape(hosts, share, -1)
    parts = lax.all_to_all(parts, "hst", split_axis=0, concat_axis=0, tiled=True)
    stats = lax.all_to_all(stats, "hst", split_axis=0, concat_axis=0, tiled=True)
    context_out = context_attend(at, lengths, queries, keys_values, bias, anchor)
    return (context_out, combine(parts, stats, share))


def solution(mesh):
    return jax.shard_map(
        per_device,
        mesh=mesh,
        in_specs=(
            P(("hst", "grp"), None),
            P(None, ("hst", "grp"), None),
            P(),
            P(),
            P("hst", "grp"),
            P(None, "hst", "grp"),
        ),
        out_specs=(P(("hst", "grp"), None), P("hst", "grp")),
        check_vma=False,
    )
```

```python
import functools
import math

import jax
import jax.numpy as jnp
from jax import lax
from jax.experimental import pallas as pl
from jax.experimental.pallas import tpu as pltpu
from jax.sharding import PartitionSpec as P

HSZ = 128
NAMB = 512
NEG = -1e30
FLOOR = -2000.0
EXTRA = 16
C2 = math.log2(math.e) / math.sqrt(HSZ)
BOTH = ("hst", "grp")


def dot_t(a, b):
    return lax.dot_general(a, b, (((1,), (1,)), ((), ())), preferred_element_type=jnp.float32)


def dot(a, b):
    return lax.dot_general(a, b, (((1,), (0,)), ((), ())), preferred_element_type=jnp.float32)


def softmax_mix(tiles):
    results = []
    for scores, values in tiles:
        top = functools.reduce(jnp.maximum, [jnp.max(s, axis=-1, keepdims=True) for s in scores])
        base = top * C2
        weights = [jnp.exp2(s * C2 - base) for s in scores]
        total = functools.reduce(jnp.add, [jnp.sum(w, axis=-1, keepdims=True) for w in weights])
        mixed = functools.reduce(jnp.add, [dot(w.astype(jnp.bfloat16), v) for w, v in zip(weights, values)])
        results.append((base, total, mixed))
    return results


def pack_kernel(groups, kv_ref, out_ref, sems):
    part = out_ref.shape[3]
    copies = [
        pltpu.make_async_copy(kv_ref.at[s, :, pl.ds(g * part, part)], out_ref.at[g, s], sems.at[g, s])
        for g in range(groups)
        for s in range(2)
    ]
    for copy in copies:
        copy.start()
    for copy in copies:
        copy.wait()


def pack(kv, groups):
    _, rows, width = kv.shape
    return pl.pallas_call(
        functools.partial(pack_kernel, groups),
        in_specs=[pl.BlockSpec(memory_space=pl.ANY)],
        out_specs=pl.BlockSpec(memory_space=pl.ANY),
        out_shape=jax.ShapeDtypeStruct((groups, 2, rows, width // groups), kv.dtype),
        scratch_shapes=[pltpu.SemaphoreType.DMA((groups, 2))],
        cost_estimate=pl.CostEstimate(flops=0, bytes_accessed=4 * kv.size, transcendentals=0),
        name="pack_heads",
    )(kv)


def suffix_kernel(groups, sub, share, at_ref, q_ref, kv_ref, sk_ref, bias_ref, out_ref):
    host = at_ref[0]
    step = pl.program_id(0)
    tile = q_ref.shape[0]
    bias = [bias_ref[pl.ds(host * groups + g, 1), :] for g in range(groups)]
    tiles = []
    for first in range(0, tile, sub):
        q = q_ref[first : first + sub, :]
        scores = [dot_t(q, kv_ref[g, 0]) + bias[g] for g in range(groups)]
        s = dot_t(q, sk_ref[0])
        qpos = step * tile + first + lax.broadcasted_iota(jnp.int32, s.shape, 0)
        spos = host * share + lax.broadcasted_iota(jnp.int32, s.shape, 1)
        scores.append(jnp.where(spos <= qpos, s, NEG))
        tiles.append((scores, [kv_ref[g, 1] for g in range(groups)] + [sk_ref[1]]))
    for number, (base, total, mixed) in enumerate(softmax_mix(tiles)):
        first = number * sub
        n = mixed / total
        size = jnp.max(jnp.abs(n), axis=-1, keepdims=True)
        shift = jnp.clip(jnp.floor(jnp.log2(size)), -100.0, 100.0)
        n = n * jnp.exp2(-shift)
        level = jnp.maximum(base + jnp.log2(total), FLOOR)
        whole = jnp.floor(level)
        rest = jnp.exp2(level - whole)
        coarse = jnp.round(rest * 512.0) * (1.0 / 512.0)
        fine = (rest - coarse) * 1024.0
        lane = lax.broadcasted_iota(jnp.int32, (sub, HSZ), 1)
        stats = jnp.where(lane == 0, whole, jnp.where(lane == 1, coarse, jnp.where(lane == 2, fine, shift)))
        turned = stats.T
        for c in range(sub // share):
            chunk = first // share + c
            out_ref[chunk, :share, :] = n[c * share : (c + 1) * share, :]
            out_ref[chunk, share : share + EXTRA, :share] = turned[:EXTRA, c * share : (c + 1) * share]


def suffix_attend(at, q, kv, sk, bias):
    groups, _, rows, width = kv.shape
    total_q = q.shape[0]
    share = sk.shape[1]
    heads = width // HSZ
    tile, sub = min(512, total_q), min(256, total_q)
    seen = groups * rows + share
    return pl.pallas_call(
        functools.partial(suffix_kernel, groups, sub, share),
        grid_spec=pltpu.PrefetchScalarGridSpec(
            num_scalar_prefetch=1,
            grid=(total_q // tile, heads),
            in_specs=[
                pl.BlockSpec((tile, HSZ), lambda i, h, at: (i, h)),
                pl.BlockSpec((groups, 2, rows, HSZ), lambda i, h, at: (0, 0, 0, h)),
                pl.BlockSpec((2, share, HSZ), lambda i, h, at: (0, 0, h)),
                pl.BlockSpec(bias.shape, lambda i, h, at: (0, 0)),
            ],
            out_specs=pl.BlockSpec((tile // share, share + EXTRA, HSZ), lambda i, h, at: (i, 0, h)),
        ),
        out_shape=jax.ShapeDtypeStruct((total_q // share, share + EXTRA, width), jnp.float32),
        compiler_params=pltpu.CompilerParams(vmem_limit_bytes=48 * 1024 * 1024),
        cost_estimate=pl.CostEstimate(
            flops=8 * total_q * seen * width,
            bytes_accessed=2 * kv.size + 2 * q.size + 4 * q.size,
            transcendentals=total_q * seen * heads,
        ),
        name="suffix_attend",
    )(at, q, kv, sk, bias)


def combine_kernel(in_ref, out_ref):
    hosts, tall, _ = in_ref.shape
    share = tall - EXTRA
    stats = in_ref[:, share:, :].reshape(hosts * EXTRA, HSZ).T[:share, :]
    column = lambda g, k: stats[:, g * EXTRA + k : g * EXTRA + k + 1]
    highest = functools.reduce(jnp.maximum, [column(g, 0) for g in range(hosts)])
    total = 0.0
    mixed = 0.0
    for g in range(hosts):
        weight = jnp.exp2(column(g, 0) - highest) * (column(g, 1) + column(g, 2) * (1.0 / 1024.0))
        total = total + weight
        mixed = mixed + (weight * jnp.exp2(column(g, 3))) * in_ref[g, :share, :]
    out_ref[...] = (mixed / total).astype(out_ref.dtype)


def combine(parts):
    hosts, tall, width = parts.shape
    return pl.pallas_call(
        combine_kernel,
        grid=(width // HSZ,),
        in_specs=[pl.BlockSpec((hosts, tall, HSZ), lambda h: (0, 0, h))],
        out_specs=pl.BlockSpec((tall - EXTRA, HSZ), lambda h: (0, h)),
        out_shape=jax.ShapeDtypeStruct((tall - EXTRA, width), jnp.bfloat16),
        cost_estimate=pl.CostEstimate(flops=2 * parts.size, bytes_accessed=4 * parts.size, transcendentals=0),
        name="combine_groups",
    )(parts)


def context_kernel(at_ref, len_ref, q_ref, kv_ref, bias_ref, anchor_ref, *rest):
    out_ref, diag_ref = rest[-2:]
    block = at_ref[0]
    rows = q_ref.shape[0]
    half = rows // 2
    own = bias_ref[pl.ds(block, 1), :]

    @pl.when(pl.program_id(0) == 0)
    def _():
        row = lax.broadcasted_iota(jnp.int32, (half, half), 0)
        col = lax.broadcasted_iota(jnp.int32, (half, half), 1)
        for t in range(2):
            ok = own[:, t * half : (t + 1) * half]
            diag_ref[t] = jnp.where(col == row, 0.0, jnp.where(col < row, ok, NEG))

    anchor_keys = anchor_ref[:, 0].reshape(rows, HSZ)
    anchor_values = anchor_ref[:, 1].reshape(rows, HSZ)
    anchor_bias = jnp.where(block > 0, bias_ref[0:1, :], NEG)
    keys, values = kv_ref[0], kv_ref[1]
    tiles = []
    for t in range(2):
        q = q_ref[t * half : (t + 1) * half, :]
        scores = [dot_t(q, anchor_keys) + anchor_bias]
        mix = [anchor_values]
        if t == 1:
            scores.append(dot_t(q, keys[:half]) + own[:, :half])
            mix.append(values[:half])
        scores.append(dot_t(q, keys[t * half : (t + 1) * half]) + diag_ref[t])
        mix.append(values[t * half : (t + 1) * half])
        tiles.append((scores, mix))
    for t, (_, total, mixed) in enumerate(softmax_mix(tiles)):
        place = t * half + lax.broadcasted_iota(jnp.int32, mixed.shape, 0)
        out = jnp.where(place < len_ref[block], mixed / total, 0.0)
        out_ref[t * half : (t + 1) * half, :] = out.astype(out_ref.dtype)


def context_attend(at, lengths, q, kv, bias, anchor, before):
    rows, width = q.shape
    hosts, _, part, group_width = anchor.shape
    heads = group_width // HSZ
    half = rows // 2
    column = lambda h, at, n: (0, at[1] * heads + h)
    both = lambda h, at, n: (0, 0, at[1] * heads + h)
    more = [] if before is None else [before]
    return pl.pallas_call(
        context_kernel,
        grid_spec=pltpu.PrefetchScalarGridSpec(
            num_scalar_prefetch=2,
            grid=(heads,),
            in_specs=[
                pl.BlockSpec((rows, HSZ), column),
                pl.BlockSpec((2, rows, HSZ), both),
                pl.BlockSpec(bias.shape, lambda h, *_: (0, 0)),
                pl.BlockSpec((hosts, 2, part, HSZ), lambda h, *_: (0, 0, 0, h)),
            ]
            + [pl.BlockSpec(memory_space=pl.ANY) for _ in more],
            out_specs=pl.BlockSpec((rows, HSZ), column),
            scratch_shapes=[pltpu.VMEM((2, half, half), jnp.float32)],
        ),
        out_shape=jax.ShapeDtypeStruct((rows, width), q.dtype),
        input_output_aliases={6: 0} if more else {},
        compiler_params=pltpu.CompilerParams(vmem_limit_bytes=48 * 1024 * 1024),
        cost_estimate=pl.CostEstimate(
            flops=8 * rows * rows * group_width,
            bytes_accessed=12 * rows * group_width,
            transcendentals=2 * rows * rows * heads,
        ),
        name="context_attend",
    )(at, lengths, q, kv, bias, anchor, *more)


def gather_rows(x, axis, n):
    return lax.all_to_all(jnp.broadcast_to(x[None], (n, *x.shape)), axis, split_axis=0, concat_axis=0, tiled=True)


def spread_anchor(kv, hosts, groups):
    _, rows, width = kv.shape
    part, wide = rows // hosts, width // groups
    first = (lax.axis_index("hst") == 0) & (lax.axis_index("grp") == 0)
    slab = jnp.where(first, kv[:, :part], 0.0)
    for h in range(1, hosts):
        slab = slab + lax.ppermute(kv[:, h * part : (h + 1) * part], BOTH, [(0, h * groups)])
    piece = slab[:, :, :wide]
    for g in range(1, groups):
        piece = piece + lax.ppermute(slab[:, :, g * wide : (g + 1) * wide], "grp", [(0, g)])
    return gather_rows(piece, "hst", hosts)


def per_device(queries, keys_values, token_ids, lengths, suffix_queries, suffix_kv):
    hosts, groups = lax.axis_size("hst"), lax.axis_size("grp")
    host, group = lax.axis_index("hst"), lax.axis_index("grp")
    rows = queries.shape[0]
    swapped = lax.all_to_all(pack(keys_values, groups), "grp", split_axis=0, concat_axis=0, tiled=True)
    gathered = gather_rows(suffix_queries, "hst", hosts).reshape(-1, suffix_queries.shape[1])
    held = {0: spread_anchor(keys_values, hosts, groups)}
    k = groups // 2
    while k >= 1:
        for have in list(held):
            held[have ^ k] = lax.ppermute(held[have], "grp", [(g, g ^ k) for g in range(groups)])
        k //= 2
    seen = (token_ids.reshape(-1, rows) >= NAMB) & (jnp.arange(rows)[None, :] < lengths[:, None])
    bias = jnp.where(seen, 0.0, NEG).astype(jnp.float32)
    parts = suffix_attend(jnp.stack([host]).astype(jnp.int32), gathered, swapped, suffix_kv, bias)
    parts = lax.all_to_all(parts.astype(jnp.float16), "hst", split_axis=0, concat_axis=0, tiled=True)
    context_out = None
    for k in range(groups):
        at = jnp.stack([host * groups + group, group ^ k]).astype(jnp.int32)
        context_out = context_attend(at, lengths, queries, keys_values, bias, held[k], context_out)
    return (context_out, combine(parts.astype(jnp.float32)))


def solution(mesh):
    return jax.shard_map(
        per_device,
        mesh=mesh,
        in_specs=(
            P(("hst", "grp"), None),
            P(None, ("hst", "grp"), None),
            P(),
            P(),
            P("hst", "grp"),
            P(None, "hst", "grp"),
        ),
        out_specs=(P(("hst", "grp"), None), P("hst", "grp")),
        check_vma=False,
    )
```

```python
import functools
import math

import jax
import jax.numpy as jnp
from jax import lax
from jax.experimental import pallas as pl
from jax.experimental.pallas import tpu as pltpu
from jax.sharding import PartitionSpec as P

HSZ = 128
NAMB = 512
NEG = -1e30
FLOOR = -2000.0
EXTRA = 16
C2 = math.log2(math.e) / math.sqrt(HSZ)
BOTH = ("hst", "grp")


def dot_t(a, b):
    return lax.dot_general(a, b, (((1,), (1,)), ((), ())), preferred_element_type=jnp.float32)


def dot(a, b):
    return lax.dot_general(a, b, (((1,), (0,)), ((), ())), preferred_element_type=jnp.float32)


def softmax(scores):
    top = functools.reduce(jnp.maximum, [jnp.max(s, axis=-1, keepdims=True) for s in scores])
    base = top * C2
    weights = [jnp.exp2(s * C2 - base) for s in scores]
    total = functools.reduce(jnp.add, [jnp.sum(w, axis=-1, keepdims=True) for w in weights])
    return base, total, [w.astype(jnp.bfloat16) for w in weights]


def pack_kernel(kv_ref, out_ref):
    out_ref[0] = kv_ref[...]


def pack(kv, groups):
    _, rows, width = kv.shape
    part = width // groups
    return pl.pallas_call(
        pack_kernel,
        grid=(groups, 2),
        in_specs=[pl.BlockSpec((1, rows, part), lambda g, s: (s, 0, g))],
        out_specs=pl.BlockSpec((1, 1, rows, part), lambda g, s: (g, s, 0, 0)),
        out_shape=jax.ShapeDtypeStruct((groups, 2, rows, part), kv.dtype),
        cost_estimate=pl.CostEstimate(flops=0, bytes_accessed=4 * kv.size, transcendentals=0),
        name="pack_heads",
    )(kv)


def suffix_kernel(at_ref, q_ref, kv_ref, sk_ref, bias_ref, *rest):
    out_ref = rest[-1]
    host = at_ref[0]
    groups = kv_ref.shape[0]
    chunks, share, _ = q_ref.shape
    odd = pl.program_id(0)
    bias = [bias_ref[pl.ds(host * groups + g, 1), :] for g in range(groups)]
    values = [kv_ref[g, 1] for g in range(groups)] + [sk_ref[1]]

    def score(k):
        q = q_ref[k]
        s = dot_t(q, sk_ref[0])
        qpos = jnp.bitwise_xor(host, 2 * k + odd) * share + lax.broadcasted_iota(jnp.int32, s.shape, 0)
        spos = host * share + lax.broadcasted_iota(jnp.int32, s.shape, 1)
        return [dot_t(q, kv_ref[g, 0]) + bias[g] for g in range(groups)] + [jnp.where(spos <= qpos, s, NEG)]

    ahead = score(0)
    for k in range(chunks):
        scores = ahead
        if k + 1 < chunks:
            ahead = score(k + 1)
        base, total, weights = softmax(scores)
        mixed = functools.reduce(jnp.add, [dot(w, v) for w, v in zip(weights, values)])
        n = mixed / total
        size = jnp.max(jnp.abs(n), axis=-1, keepdims=True)
        shift = jnp.clip(jnp.floor(jnp.log2(size)), -100.0, 100.0)
        level = jnp.maximum(base + jnp.log2(total), FLOOR)
        whole = jnp.floor(level)
        rest = jnp.exp2(level - whole)
        coarse = jnp.round(rest * 512.0) * (1.0 / 512.0)
        fine = (rest - coarse) * 1024.0
        lane = lax.broadcasted_iota(jnp.int32, (share, HSZ), 1)
        stats = jnp.where(lane == 0, whole, jnp.where(lane == 1, coarse, jnp.where(lane == 2, fine, shift)))
        to = jnp.bitwise_xor(host, 2 * k + odd)
        out_ref[to, :share, :] = n * jnp.exp2(-shift)
        out_ref[to, share : share + EXTRA, :share] = stats.T[:EXTRA, :]


def suffix_attend(host, q, kv, sk, bias, head, before):
    hosts, share, width = q.shape
    groups, _, rows, _ = kv.shape
    seen = groups * rows + share
    more = [] if before is None else [before]
    chunks = hosts // 2
    return pl.pallas_call(
        suffix_kernel,
        grid_spec=pltpu.PrefetchScalarGridSpec(
            num_scalar_prefetch=1,
            grid=(2,),
            in_specs=[
                pl.BlockSpec((chunks, share, HSZ), lambda i, at: (i, 0, head)),
                pl.BlockSpec((groups, 2, rows, HSZ), lambda i, at: (0, 0, 0, head)),
                pl.BlockSpec((2, share, HSZ), lambda i, at: (0, 0, head)),
                pl.BlockSpec(bias.shape, lambda i, at: (0, 0)),
            ]
            + [pl.BlockSpec(memory_space=pl.ANY) for _ in more],
            out_specs=pl.BlockSpec((hosts, share + EXTRA, HSZ), lambda i, at: (0, 0, head)),
        ),
        out_shape=jax.ShapeDtypeStruct((hosts, share + EXTRA, width), jnp.float32),
        input_output_aliases={5: 0} if more else {},
        compiler_params=pltpu.CompilerParams(vmem_limit_bytes=48 * 1024 * 1024),
        cost_estimate=pl.CostEstimate(
            flops=8 * hosts * share * seen * HSZ,
            bytes_accessed=4 * (groups * rows + 3 * hosts * share) * HSZ,
            transcendentals=hosts * share * seen,
        ),
        name="suffix_attend",
    )(host, q, kv, sk, bias, *more)


def combine_kernel(in_ref, out_ref):
    hosts, tall, _ = in_ref.shape
    share = tall - EXTRA
    whole, coarse, fine, shift = [in_ref[:, share + k, :] for k in range(4)]
    weight = jnp.exp2(whole - jnp.max(whole, axis=0, keepdims=True)) * (coarse + fine * (1.0 / 1024.0))
    factor = weight * jnp.exp2(shift) / jnp.sum(weight, axis=0, keepdims=True)
    factor = jnp.concatenate([factor, jnp.zeros((HSZ - hosts, HSZ), jnp.float32)], axis=0).T[:share, :]
    mixed = 0.0
    for g in range(hosts):
        mixed = mixed + factor[:, g : g + 1] * in_ref[g, :share, :]
    out_ref[...] = mixed.astype(out_ref.dtype)


def combine(parts):
    hosts, tall, width = parts.shape
    return pl.pallas_call(
        combine_kernel,
        grid=(width // HSZ,),
        in_specs=[pl.BlockSpec((hosts, tall, HSZ), lambda h: (0, 0, h))],
        out_specs=pl.BlockSpec((tall - EXTRA, HSZ), lambda h: (0, h)),
        out_shape=jax.ShapeDtypeStruct((tall - EXTRA, width), jnp.bfloat16),
        cost_estimate=pl.CostEstimate(flops=2 * parts.size, bytes_accessed=4 * parts.size, transcendentals=0),
        name="combine_groups",
    )(parts)


def context_kernel(at_ref, len_ref, q_ref, kv_ref, bias_ref, anchor_ref, *rest):
    out_ref, diag_ref = rest[-2:]
    block = at_ref[0]
    rows = q_ref.shape[0]
    half = rows // 2
    own = bias_ref[pl.ds(block, 1), :]

    @pl.when(pl.program_id(0) == 0)
    def _():
        row = lax.broadcasted_iota(jnp.int32, (half, half), 0)
        col = lax.broadcasted_iota(jnp.int32, (half, half), 1)
        for t in range(2):
            ok = own[:, t * half : (t + 1) * half]
            diag_ref[t] = jnp.where(col == row, 0.0, jnp.where(col < row, ok, NEG))

    hosts = anchor_ref.shape[0]
    apart = [jnp.bitwise_xor(at_ref[2], h) for h in range(hosts)]
    order = [jnp.bitwise_and(k, 1) * (hosts // 2) + lax.shift_right_logical(k, 1) for k in apart]
    anchor_keys = jnp.concatenate([anchor_ref[k, 0] for k in order], axis=0)
    anchor_values = jnp.concatenate([anchor_ref[k, 1] for k in order], axis=0)
    anchor_bias = jnp.where(block > 0, bias_ref[0:1, :], NEG)
    keys, values = kv_ref[0], kv_ref[1]
    tiles = []
    for t in range(2):
        q = q_ref[t * half : (t + 1) * half, :]
        scores = [dot_t(q, anchor_keys) + anchor_bias]
        mix = [anchor_values]
        if t == 1:
            scores.append(dot_t(q, keys[:half]) + own[:, :half])
            mix.append(values[:half])
        scores.append(dot_t(q, keys[t * half : (t + 1) * half]) + diag_ref[t])
        mix.append(values[t * half : (t + 1) * half])
        tiles.append((scores, mix))
    for t, (scores, mix) in enumerate(tiles):
        _, total, weights = softmax(scores)
        mixed = functools.reduce(jnp.add, [dot(w, v) for w, v in zip(weights, mix)])
        place = t * half + lax.broadcasted_iota(jnp.int32, mixed.shape, 0)
        out = jnp.where(place < len_ref[block], mixed / total, 0.0)
        out_ref[t * half : (t + 1) * half, :] = out.astype(out_ref.dtype)


def context_attend(at, lengths, q, kv, bias, anchor, before):
    rows, width = q.shape
    hosts, _, part, group_width = anchor.shape
    heads = group_width // HSZ
    half = rows // 2
    column = lambda h, at, n: (0, at[1] * heads + h)
    both = lambda h, at, n: (0, 0, at[1] * heads + h)
    more = [] if before is None else [before]
    return pl.pallas_call(
        context_kernel,
        grid_spec=pltpu.PrefetchScalarGridSpec(
            num_scalar_prefetch=2,
            grid=(heads,),
            in_specs=[
                pl.BlockSpec((rows, HSZ), column),
                pl.BlockSpec((2, rows, HSZ), both),
                pl.BlockSpec(bias.shape, lambda h, *_: (0, 0)),
                pl.BlockSpec((hosts, 2, part, HSZ), lambda h, *_: (0, 0, 0, h)),
            ]
            + [pl.BlockSpec(memory_space=pl.ANY) for _ in more],
            out_specs=pl.BlockSpec((rows, HSZ), column),
            scratch_shapes=[pltpu.VMEM((2, half, half), jnp.float32)],
        ),
        out_shape=jax.ShapeDtypeStruct((rows, width), q.dtype),
        input_output_aliases={6: 0} if more else {},
        compiler_params=pltpu.CompilerParams(vmem_limit_bytes=48 * 1024 * 1024),
        cost_estimate=pl.CostEstimate(
            flops=8 * rows * rows * group_width,
            bytes_accessed=12 * rows * group_width,
            transcendentals=2 * rows * rows * heads,
        ),
        name="context_attend",
    )(at, lengths, q, kv, bias, anchor, *more)


def swap(x, axis, k):
    return lax.ppermute(x, axis, [(i, i ^ k) for i in range(lax.axis_size(axis))])


def scatter_rows(kv, hosts, groups):
    part = kv.shape[1] // hosts
    rows = lambda h: kv[:, h * part : (h + 1) * part]
    send = lambda x, a, b: lax.ppermute(x, BOTH, [(a * groups, b * groups)])
    first = (lax.axis_index("hst") == 0) & (lax.axis_index("grp") == 0)
    pieces = [jnp.where(first, rows(0), 0.0)]
    for h in range(hosts - 1, 0, -2):
        near = send(rows(h), 0, 1)
        pieces.append(near if h == 1 else send(near, 1, h))
        if h > 1:
            pieces.append(send(rows(h - 1), 0, h - 1))
    return functools.reduce(jnp.add, pieces)


def gather_hosts(x, hosts):
    near = jnp.stack([x] + [swap(x, "hst", k) for k in range(2, hosts, 2)], axis=0)
    far = swap(near, "hst", 1)
    return jnp.concatenate([near, far], axis=0)


def spread_anchor(kv, hosts, groups):
    wide = kv.shape[2] // groups
    slab = scatter_rows(kv, hosts, groups)
    piece = slab[:, :, :wide]
    for g in range(1, groups):
        piece = piece + lax.ppermute(slab[:, :, g * wide : (g + 1) * wide], "grp", [(0, g)])
    return gather_hosts(piece, hosts)


def per_device(queries, keys_values, token_ids, lengths, suffix_queries, suffix_kv):
    hosts, groups = lax.axis_size("hst"), lax.axis_size("grp")
    host, group = lax.axis_index("hst"), lax.axis_index("grp")
    rows = queries.shape[0]
    packed, keys_values = lax.optimization_barrier((pack(keys_values, groups), keys_values))
    swapped = lax.all_to_all(packed, "grp", split_axis=0, concat_axis=0, tiled=True)
    gathered = gather_hosts(suffix_queries, hosts)
    held = {0: spread_anchor(keys_values, hosts, groups)}
    k = groups // 2
    while k >= 1:
        for have in list(held):
            held[have ^ k] = swap(held[have], "grp", k)
        k //= 2
    seen = (token_ids.reshape(-1, rows) >= NAMB) & (jnp.arange(rows)[None, :] < lengths[:, None])
    bias = jnp.where(seen, 0.0, NEG).astype(jnp.float32)
    parts = None
    for head in range(suffix_queries.shape[1] // HSZ):
        parts = suffix_attend(jnp.stack([host]), gathered, swapped, suffix_kv, bias, head, parts)
    coded = lax.all_to_all(parts.astype(jnp.float16), "hst", split_axis=0, concat_axis=0, tiled=True)
    context_out = None
    for k in range(groups):
        at = jnp.stack([host * groups + group, group ^ k, host])
        context_out = context_attend(at, lengths, queries, keys_values, bias, held[k], context_out)
    return (context_out, combine(coded.astype(jnp.float32)))


def solution(mesh):
    return jax.shard_map(
        per_device,
        mesh=mesh,
        in_specs=(
            P(("hst", "grp"), None),
            P(None, ("hst", "grp"), None),
            P(),
            P(),
            P("hst", "grp"),
            P(None, "hst", "grp"),
        ),
        out_specs=(P(("hst", "grp"), None), P("hst", "grp")),
        check_vma=False,
    )
```

```python
import functools
import math

import jax
import jax.numpy as jnp
from jax import lax
from jax.experimental import pallas as pl
from jax.experimental.pallas import tpu as pltpu
from jax.sharding import PartitionSpec as P

HSZ = 128
NAMB = 512
NEG = -1e30
FLOOR = -2000.0
EXTRA = 16
TILE = 256
C2 = math.log2(math.e) / math.sqrt(HSZ)
BOTH = ("hst", "grp")


def dot_t(a, b):
    return lax.dot_general(a, b, (((1,), (1,)), ((), ())), preferred_element_type=jnp.float32)


def dot(a, b):
    return lax.dot_general(a, b, (((1,), (0,)), ((), ())), preferred_element_type=jnp.float32)


def softmax(scores):
    top = functools.reduce(jnp.maximum, [jnp.max(s, axis=-1, keepdims=True) for s in scores])
    base = top * C2
    weights = [jnp.exp2(s * C2 - base) for s in scores]
    total = functools.reduce(jnp.add, [jnp.sum(w, axis=-1, keepdims=True) for w in weights])
    return base, total, [w.astype(jnp.bfloat16) for w in weights]


def pack_kernel(kv_ref, out_ref):
    groups, _, _, part = out_ref.shape
    for g in range(groups):
        out_ref[g, 0] = kv_ref[0, :, g * part : (g + 1) * part]


def pack(kv, groups):
    _, rows, width = kv.shape
    part = width // groups
    few = rows // 4
    return pl.pallas_call(
        pack_kernel,
        grid=(2, 4),
        in_specs=[pl.BlockSpec((1, few, width), lambda s, i: (s, i, 0))],
        out_specs=pl.BlockSpec((groups, 1, few, part), lambda s, i: (0, s, i, 0)),
        out_shape=jax.ShapeDtypeStruct((groups, 2, rows, part), kv.dtype),
        cost_estimate=pl.CostEstimate(flops=0, bytes_accessed=4 * kv.size, transcendentals=0),
        name="pack_heads",
    )(kv)


def pipelined(tasks, score, finish):
    ahead = score(tasks[0])
    for n, task in enumerate(tasks):
        scores = ahead
        if n + 1 < len(tasks):
            ahead = score(tasks[n + 1])
        finish(task, scores)


def suffix_kernel(at_ref, q_ref, kv_ref, sk_ref, bias_ref, *rest):
    out_ref = rest[-1]
    host = at_ref[0]
    groups = kv_ref.shape[0]
    hosts, share, _ = q_ref.shape
    apart = list(range(0, hosts, 2)) + list(range(1, hosts, 2))
    chunks = min(hosts, max(1, TILE // share))
    bias = [bias_ref[pl.ds(host * groups + g, 1), :] for g in range(groups)]
    values = [kv_ref[g, 1] for g in range(groups)] + [sk_ref[1]]

    def score(first):
        q = jnp.concatenate([q_ref[first + c] for c in range(chunks)], axis=0)
        s = dot_t(q, sk_ref[0])
        row = lax.broadcasted_iota(jnp.int32, (share, share), 0)
        spos = host * share + lax.broadcasted_iota(jnp.int32, (share, share), 1)
        late = []
        for c in range(chunks):
            qpos = jnp.bitwise_xor(host, apart[first + c]) * share + row
            late.append(jnp.where(spos <= qpos, s[c * share : (c + 1) * share], NEG))
        return [dot_t(q, kv_ref[g, 0]) + bias[g] for g in range(groups)] + [jnp.concatenate(late, axis=0)]

    def finish(first, scores):
        base, total, weights = softmax(scores)
        mixed = functools.reduce(jnp.add, [dot(w, v) for w, v in zip(weights, values)])
        n = mixed / total
        size = jnp.max(jnp.abs(n), axis=-1, keepdims=True)
        shift = jnp.clip(jnp.floor(jnp.log2(size)), -100.0, 100.0)
        level = jnp.maximum(base + jnp.log2(total), FLOOR)
        whole = jnp.floor(level)
        rest = jnp.exp2(level - whole)
        coarse = jnp.round(rest * 512.0) * (1.0 / 512.0)
        fine = (rest - coarse) * 1024.0
        lane = lax.broadcasted_iota(jnp.int32, (chunks * share, HSZ), 1)
        stats = jnp.where(lane == 0, whole, jnp.where(lane == 1, coarse, jnp.where(lane == 2, fine, shift)))
        turned = stats.T
        n = n * jnp.exp2(-shift)
        for c in range(chunks):
            to = jnp.bitwise_xor(host, apart[first + c])
            out_ref[to, :share, :] = n[c * share : (c + 1) * share]
            out_ref[to, share : share + EXTRA, :share] = turned[:EXTRA, c * share : (c + 1) * share]

    pipelined(list(range(0, hosts, chunks)), score, finish)


def suffix_attend(host, q, kv, sk, bias, head, before):
    hosts, share, width = q.shape
    groups, _, rows, _ = kv.shape
    seen = groups * rows + share
    more = [] if before is None else [before]
    return pl.pallas_call(
        suffix_kernel,
        grid_spec=pltpu.PrefetchScalarGridSpec(
            num_scalar_prefetch=1,
            grid=(1,),
            in_specs=[
                pl.BlockSpec((hosts, share, HSZ), lambda i, at: (0, 0, head)),
                pl.BlockSpec((groups, 2, rows, HSZ), lambda i, at: (0, 0, 0, head)),
                pl.BlockSpec((2, share, HSZ), lambda i, at: (0, 0, head)),
                pl.BlockSpec(bias.shape, lambda i, at: (0, 0)),
            ]
            + [pl.BlockSpec(memory_space=pl.ANY) for _ in more],
            out_specs=pl.BlockSpec((hosts, share + EXTRA, HSZ), lambda i, at: (0, 0, head)),
        ),
        out_shape=jax.ShapeDtypeStruct((hosts, share + EXTRA, width), jnp.float32),
        input_output_aliases={5: 0} if more else {},
        compiler_params=pltpu.CompilerParams(vmem_limit_bytes=48 * 1024 * 1024),
        cost_estimate=pl.CostEstimate(
            flops=8 * hosts * share * seen * HSZ,
            bytes_accessed=4 * (groups * rows + 3 * hosts * share) * HSZ,
            transcendentals=hosts * share * seen,
        ),
        name="suffix_attend",
    )(host, q, kv, sk, bias, *more)


def combine_kernel(in_ref, out_ref):
    hosts, tall, _ = in_ref.shape
    share = tall - EXTRA
    whole, coarse, fine, shift = [in_ref[:, share + k, :] for k in range(4)]
    weight = jnp.exp2(whole - jnp.max(whole, axis=0, keepdims=True)) * (coarse + fine * (1.0 / 1024.0))
    factor = weight * jnp.exp2(shift) / jnp.sum(weight, axis=0, keepdims=True)
    factor = jnp.concatenate([factor, jnp.zeros((HSZ - hosts, HSZ), jnp.float32)], axis=0).T[:share, :]
    mixed = 0.0
    for g in range(hosts):
        mixed = mixed + factor[:, g : g + 1] * in_ref[g, :share, :]
    out_ref[...] = mixed.astype(out_ref.dtype)


def combine(parts):
    hosts, tall, width = parts.shape
    return pl.pallas_call(
        combine_kernel,
        grid=(width // HSZ,),
        in_specs=[pl.BlockSpec((hosts, tall, HSZ), lambda h: (0, 0, h))],
        out_specs=pl.BlockSpec((tall - EXTRA, HSZ), lambda h: (0, h)),
        out_shape=jax.ShapeDtypeStruct((tall - EXTRA, width), jnp.bfloat16),
        cost_estimate=pl.CostEstimate(flops=2 * parts.size, bytes_accessed=4 * parts.size, transcendentals=0),
        name="combine_groups",
    )(parts)


def context_kernel(at_ref, len_ref, q_ref, kv_ref, bias_ref, near_ref, far_ref, *rest):
    out_ref, diag_ref = rest[-2:]
    block, odd = at_ref[0], at_ref[2]
    rows, width = q_ref.shape
    half = rows // 2
    own = bias_ref[pl.ds(block, 1), :]
    row = lax.broadcasted_iota(jnp.int32, (half, half), 0)
    col = lax.broadcasted_iota(jnp.int32, (half, half), 1)
    for t in range(2):
        ok = own[:, t * half : (t + 1) * half]
        diag_ref[t] = jnp.where(col == row, 0.0, jnp.where(col < row, ok, NEG))
    low, high = bias_ref[0:1, :half], bias_ref[0:1, half:]
    near_bias = jnp.where(block > 0, jnp.where(odd == 0, low, high), NEG)
    far_bias = jnp.where(block > 0, jnp.where(odd == 0, high, low), NEG)

    def score(task):
        first, t = task
        head = slice(first, first + HSZ)
        q = q_ref[t * half : (t + 1) * half, head]
        scores = [dot_t(q, near_ref[0, :, head]) + near_bias, dot_t(q, far_ref[0, :, head]) + far_bias]
        if t == 1:
            scores.append(dot_t(q, kv_ref[0, :half, head]) + own[:, :half])
        scores.append(dot_t(q, kv_ref[0, t * half : (t + 1) * half, head]) + diag_ref[t])
        return scores

    def finish(task, scores):
        first, t = task
        head = slice(first, first + HSZ)
        _, total, weights = softmax(scores)
        values = [near_ref[1, :, head], far_ref[1, :, head]]
        values += [kv_ref[1, u * half : (u + 1) * half, head] for u in range(t + 1)]
        mixed = functools.reduce(jnp.add, [dot(w, v) for w, v in zip(weights, values)])
        place = t * half + lax.broadcasted_iota(jnp.int32, mixed.shape, 0)
        out = jnp.where(place < len_ref[block], mixed / total, 0.0)
        out_ref[t * half : (t + 1) * half, head] = out.astype(out_ref.dtype)

    pipelined([(first, t) for first in range(0, width, HSZ) for t in range(2)], score, finish)


def context_attend(at, lengths, q, kv, bias, near, far, before):
    rows, width = q.shape
    _, half, wide = near.shape
    heads = wide // HSZ
    both = lambda i, at, n: (0, 0, at[1])
    more = [] if before is None else [before]
    return pl.pallas_call(
        context_kernel,
        grid_spec=pltpu.PrefetchScalarGridSpec(
            num_scalar_prefetch=2,
            grid=(1,),
            in_specs=[
                pl.BlockSpec((rows, wide), lambda i, at, n: (0, at[1])),
                pl.BlockSpec((2, rows, wide), both),
                pl.BlockSpec(bias.shape, lambda i, *_: (0, 0)),
                pl.BlockSpec((2, half, wide), lambda i, *_: (0, 0, 0)),
                pl.BlockSpec((2, half, wide), lambda i, *_: (0, 0, 0)),
            ]
            + [pl.BlockSpec(memory_space=pl.ANY) for _ in more],
            out_specs=pl.BlockSpec((rows, wide), lambda i, at, n: (0, at[1])),
            scratch_shapes=[pltpu.VMEM((2, half, half), jnp.float32)],
        ),
        out_shape=jax.ShapeDtypeStruct((rows, width), q.dtype),
        input_output_aliases={7: 0} if more else {},
        compiler_params=pltpu.CompilerParams(vmem_limit_bytes=48 * 1024 * 1024),
        cost_estimate=pl.CostEstimate(
            flops=8 * rows * rows * wide,
            bytes_accessed=12 * rows * wide,
            transcendentals=2 * rows * rows * heads,
        ),
        name="context_attend",
    )(at, lengths, q, kv, bias, near, far, *more)


def swap(x, axis, k):
    return lax.ppermute(x, axis, [(i, i ^ k) for i in range(lax.axis_size(axis))])


def gather_hosts(x, hosts):
    near = jnp.stack([x] + [swap(x, "hst", k) for k in range(2, hosts, 2)], axis=0)
    far = swap(near, "hst", 1)
    return jnp.concatenate([near, far], axis=0)


def after(x, done):
    return lax.optimization_barrier((x, done))[0]


def anchor_quarters(kv):
    _, rows, width = kv.shape
    tall, wide = rows // 2, width // 2
    quarter = lambda y, x: kv[:, y * tall : (y + 1) * tall, x * wide : (x + 1) * wide]
    return [quarter(1, 1), quarter(0, 1), quarter(1, 0), quarter(0, 0)]


def spread_anchor(quarters, hosts, groups):
    cores = groups // 2
    first = (lax.axis_index("hst") == 0) & (lax.axis_index("grp") == 0)
    slab = jnp.where(first, quarters[3], 0.0)
    for quarter, to in zip(quarters, [groups + cores, cores, groups]):
        slab = slab + lax.ppermute(quarter, BOTH, [(0, to)])
    wide = slab.shape[2] // cores
    piece = slab[:, :, :wide]
    for c in range(1, cores):
        pairs = [(x, x + c) for x in (0, cores)]
        piece = piece + lax.ppermute(slab[:, :, c * wide : (c + 1) * wide], "grp", pairs)
    far = hosts // 2
    while far >= 2:
        pairs = [(h, h + far) for h in range(hosts) if h % (2 * far) < 2]
        piece = piece + lax.ppermute(piece, "hst", pairs)
        far //= 2
    return piece


def per_device(queries, keys_values, token_ids, lengths, suffix_queries, suffix_kv):
    hosts, groups = lax.axis_size("hst"), lax.axis_size("grp")
    host, group = lax.axis_index("hst"), lax.axis_index("grp")
    rows = queries.shape[0]
    heads = suffix_queries.shape[1] // HSZ
    quarters, keys_values = lax.optimization_barrier((anchor_quarters(keys_values), keys_values))
    swapped = lax.all_to_all(pack(keys_values, groups), "grp", split_axis=0, concat_axis=0, tiled=True)
    near = spread_anchor(quarters, hosts, groups)
    gathered = gather_hosts(suffix_queries, hosts)
    seen = (token_ids.reshape(-1, rows) >= NAMB) & (jnp.arange(rows)[None, :] < lengths[:, None])
    bias = jnp.where(seen, 0.0, NEG).astype(jnp.float32)
    cores = groups // 2
    far = swap(near, "hst", 1)
    other_near = swap(near, "grp", cores)
    parts = None
    for head in range(heads):
        parts = suffix_attend(jnp.stack([host]), gathered, swapped, suffix_kv, bias, head, parts)
        if head == 0:
            far = after(far, parts)
    held = {0: [near, far], cores: [other_near, swap(far, "grp", cores)]}
    for k in range(1, cores):
        held[k] = [swap(x, "grp", k) for x in held[0]]
    for k in range(1, cores):
        held[cores ^ k] = [swap(after(x, parts), "grp", k) for x in held[cores]]
    coded = lax.all_to_all(parts.astype(jnp.float16), "hst", split_axis=0, concat_axis=0, tiled=True)
    context_out = None
    for k in range(groups):
        at = jnp.stack([host * groups + group, group ^ k, host % 2])
        context_out = context_attend(at, lengths, queries, keys_values, bias, *held[k], context_out)
    return (context_out, combine(coded.astype(jnp.float32)))


def solution(mesh):
    return jax.shard_map(
        per_device,
        mesh=mesh,
        in_specs=(
            P(("hst", "grp"), None),
            P(None, ("hst", "grp"), None),
            P(),
            P(),
            P("hst", "grp"),
            P(None, "hst", "grp"),
        ),
        out_specs=(P(("hst", "grp"), None), P("hst", "grp")),
        check_vma=False,
    )
```

```python
import functools
import math

import jax
import jax.numpy as jnp
from jax import lax
from jax.experimental import pallas as pl
from jax.experimental.pallas import tpu as pltpu
from jax.sharding import PartitionSpec as P

HSZ = 128
NAMB = 512
NEG = -1e30
FLOOR = -2000.0
EXTRA = 16
TILE = 256
C2 = math.log2(math.e) / math.sqrt(HSZ)
BOTH = ("hst", "grp")


def dot_t(a, b):
    return lax.dot_general(a, b, (((1,), (1,)), ((), ())), preferred_element_type=jnp.float32)


def dot(a, b):
    return lax.dot_general(a, b, (((1,), (0,)), ((), ())), preferred_element_type=jnp.float32)


def softmax(scores):
    top = functools.reduce(jnp.maximum, [jnp.max(s, axis=-1, keepdims=True) for s in scores])
    base = top * C2
    weights = [jnp.exp2(s * C2 - base) for s in scores]
    total = functools.reduce(jnp.add, [jnp.sum(w, axis=-1, keepdims=True) for w in weights])
    return base, total, [w.astype(jnp.bfloat16) for w in weights]


def pack_kernel(kv_ref, out_ref):
    groups, _, _, part = out_ref.shape
    for g in range(groups):
        out_ref[g, 0] = kv_ref[0, :, g * part : (g + 1) * part]


def pack(kv, groups):
    _, rows, width = kv.shape
    part = width // groups
    few = rows // 4
    return pl.pallas_call(
        pack_kernel,
        grid=(2, 4),
        in_specs=[pl.BlockSpec((1, few, width), lambda s, i: (s, i, 0))],
        out_specs=pl.BlockSpec((groups, 1, few, part), lambda s, i: (0, s, i, 0)),
        out_shape=jax.ShapeDtypeStruct((groups, 2, rows, part), kv.dtype),
        cost_estimate=pl.CostEstimate(flops=0, bytes_accessed=4 * kv.size, transcendentals=0),
        name="pack_heads",
    )(kv)


def pipelined(tasks, score, finish):
    ahead = score(tasks[0])
    for n, task in enumerate(tasks):
        scores = ahead
        if n + 1 < len(tasks):
            ahead = score(tasks[n + 1])
        finish(task, scores)


def suffix_kernel(at_ref, q_ref, kv_ref, sk_ref, bias_ref, *rest):
    out_ref = rest[-1]
    host = at_ref[0]
    groups = kv_ref.shape[0]
    hosts, share, _ = q_ref.shape
    apart = list(range(0, hosts, 2)) + list(range(1, hosts, 2))
    chunks = min(hosts, max(1, TILE // share))
    bias = [bias_ref[pl.ds(host * groups + g, 1), :] for g in range(groups)]
    values = [kv_ref[g, 1] for g in range(groups)] + [sk_ref[1]]

    def score(first):
        q = jnp.concatenate([q_ref[first + c] for c in range(chunks)], axis=0)
        s = dot_t(q, sk_ref[0])
        row = lax.broadcasted_iota(jnp.int32, (share, share), 0)
        spos = host * share + lax.broadcasted_iota(jnp.int32, (share, share), 1)
        late = []
        for c in range(chunks):
            qpos = jnp.bitwise_xor(host, apart[first + c]) * share + row
            late.append(jnp.where(spos <= qpos, s[c * share : (c + 1) * share], NEG))
        return [dot_t(q, kv_ref[g, 0]) + bias[g] for g in range(groups)] + [jnp.concatenate(late, axis=0)]

    def finish(first, scores):
        base, total, weights = softmax(scores)
        mixed = functools.reduce(jnp.add, [dot(w, v) for w, v in zip(weights, values)])
        n = mixed / total
        size = jnp.max(jnp.abs(n), axis=-1, keepdims=True)
        shift = jnp.clip(jnp.floor(jnp.log2(size)), -100.0, 100.0)
        level = jnp.maximum(base + jnp.log2(total), FLOOR)
        whole = jnp.floor(level)
        rest = jnp.exp2(level - whole)
        coarse = jnp.round(rest * 512.0) * (1.0 / 512.0)
        fine = (rest - coarse) * 1024.0
        lane = lax.broadcasted_iota(jnp.int32, (chunks * share, HSZ), 1)
        stats = jnp.where(lane == 0, whole, jnp.where(lane == 1, coarse, jnp.where(lane == 2, fine, shift)))
        turned = stats.T
        n = n * jnp.exp2(-shift)
        for c in range(chunks):
            to = jnp.bitwise_xor(host, apart[first + c])
            out_ref[to, :share, :] = n[c * share : (c + 1) * share]
            out_ref[to, share : share + EXTRA, :share] = turned[:EXTRA, c * share : (c + 1) * share]

    pipelined(list(range(0, hosts, chunks)), score, finish)


def suffix_attend(host, q, kv, sk, bias, first, count, before):
    hosts, share, width = q.shape
    groups, _, rows, _ = kv.shape
    seen = groups * rows + share
    more = [] if before is None else [before]
    return pl.pallas_call(
        suffix_kernel,
        grid_spec=pltpu.PrefetchScalarGridSpec(
            num_scalar_prefetch=1,
            grid=(count,),
            in_specs=[
                pl.BlockSpec((hosts, share, HSZ), lambda i, at: (0, 0, first + i)),
                pl.BlockSpec((groups, 2, rows, HSZ), lambda i, at: (0, 0, 0, first + i)),
                pl.BlockSpec((2, share, HSZ), lambda i, at: (0, 0, first + i)),
                pl.BlockSpec(bias.shape, lambda i, at: (0, 0)),
            ]
            + [pl.BlockSpec(memory_space=pl.ANY) for _ in more],
            out_specs=pl.BlockSpec((hosts, share + EXTRA, HSZ), lambda i, at: (0, 0, first + i)),
        ),
        out_shape=jax.ShapeDtypeStruct((hosts, share + EXTRA, width), jnp.float32),
        input_output_aliases={5: 0} if more else {},
        compiler_params=pltpu.CompilerParams(vmem_limit_bytes=48 * 1024 * 1024),
        cost_estimate=pl.CostEstimate(
            flops=8 * count * hosts * share * seen * HSZ,
            bytes_accessed=4 * count * (groups * rows + 3 * hosts * share) * HSZ,
            transcendentals=count * hosts * share * seen,
        ),
        name="suffix_attend",
    )(host, q, kv, sk, bias, *more)


def combine_kernel(in_ref, out_ref):
    hosts, tall, _ = in_ref.shape
    share = tall - EXTRA
    whole, coarse, fine, shift = [in_ref[:, share + k, :] for k in range(4)]
    weight = jnp.exp2(whole - jnp.max(whole, axis=0, keepdims=True)) * (coarse + fine * (1.0 / 1024.0))
    factor = weight * jnp.exp2(shift) / jnp.sum(weight, axis=0, keepdims=True)
    factor = jnp.concatenate([factor, jnp.zeros((HSZ - hosts, HSZ), jnp.float32)], axis=0).T[:share, :]
    mixed = 0.0
    for g in range(hosts):
        mixed = mixed + factor[:, g : g + 1] * in_ref[g, :share, :]
    out_ref[...] = mixed.astype(out_ref.dtype)


def combine(parts):
    hosts, tall, width = parts.shape
    return pl.pallas_call(
        combine_kernel,
        grid=(width // HSZ,),
        in_specs=[pl.BlockSpec((hosts, tall, HSZ), lambda h: (0, 0, h))],
        out_specs=pl.BlockSpec((tall - EXTRA, HSZ), lambda h: (0, h)),
        out_shape=jax.ShapeDtypeStruct((tall - EXTRA, width), jnp.bfloat16),
        cost_estimate=pl.CostEstimate(flops=2 * parts.size, bytes_accessed=4 * parts.size, transcendentals=0),
        name="combine_groups",
    )(parts)


def context_kernel(at_ref, len_ref, q_ref, kv_ref, bias_ref, near_ref, far_ref, *rest):
    out_ref, diag_ref = rest[-2:]
    block, odd = at_ref[0], at_ref[2]
    rows, width = q_ref.shape
    half = rows // 2
    own = bias_ref[pl.ds(block, 1), :]
    row = lax.broadcasted_iota(jnp.int32, (half, half), 0)
    col = lax.broadcasted_iota(jnp.int32, (half, half), 1)
    for t in range(2):
        ok = own[:, t * half : (t + 1) * half]
        diag_ref[t] = jnp.where(col == row, 0.0, jnp.where(col < row, ok, NEG))
    low, high = bias_ref[0:1, :half], bias_ref[0:1, half:]
    near_bias = jnp.where(block > 0, jnp.where(odd == 0, low, high), NEG)
    far_bias = jnp.where(block > 0, jnp.where(odd == 0, high, low), NEG)

    def score(task):
        first, t = task
        head = slice(first, first + HSZ)
        q = q_ref[t * half : (t + 1) * half, head]
        scores = [dot_t(q, near_ref[0, :, head]) + near_bias, dot_t(q, far_ref[0, :, head]) + far_bias]
        if t == 1:
            scores.append(dot_t(q, kv_ref[0, :half, head]) + own[:, :half])
        scores.append(dot_t(q, kv_ref[0, t * half : (t + 1) * half, head]) + diag_ref[t])
        return scores

    def finish(task, scores):
        first, t = task
        head = slice(first, first + HSZ)
        _, total, weights = softmax(scores)
        values = [near_ref[1, :, head], far_ref[1, :, head]]
        values += [kv_ref[1, u * half : (u + 1) * half, head] for u in range(t + 1)]
        mixed = functools.reduce(jnp.add, [dot(w, v) for w, v in zip(weights, values)])
        place = t * half + lax.broadcasted_iota(jnp.int32, mixed.shape, 0)
        out = jnp.where(place < len_ref[block], mixed / total, 0.0)
        out_ref[t * half : (t + 1) * half, head] = out.astype(out_ref.dtype)

    pipelined([(first, t) for first in range(0, width, HSZ) for t in range(2)], score, finish)


def context_attend(at, lengths, q, kv, bias, near, far, before):
    rows, width = q.shape
    _, half, wide = near.shape
    heads = wide // HSZ
    both = lambda i, at, n: (0, 0, at[1])
    more = [] if before is None else [before]
    return pl.pallas_call(
        context_kernel,
        grid_spec=pltpu.PrefetchScalarGridSpec(
            num_scalar_prefetch=2,
            grid=(1,),
            in_specs=[
                pl.BlockSpec((rows, wide), lambda i, at, n: (0, at[1])),
                pl.BlockSpec((2, rows, wide), both),
                pl.BlockSpec(bias.shape, lambda i, *_: (0, 0)),
                pl.BlockSpec((2, half, wide), lambda i, *_: (0, 0, 0)),
                pl.BlockSpec((2, half, wide), lambda i, *_: (0, 0, 0)),
            ]
            + [pl.BlockSpec(memory_space=pl.ANY) for _ in more],
            out_specs=pl.BlockSpec((rows, wide), lambda i, at, n: (0, at[1])),
            scratch_shapes=[pltpu.VMEM((2, half, half), jnp.float32)],
        ),
        out_shape=jax.ShapeDtypeStruct((rows, width), q.dtype),
        input_output_aliases={7: 0} if more else {},
        compiler_params=pltpu.CompilerParams(vmem_limit_bytes=48 * 1024 * 1024),
        cost_estimate=pl.CostEstimate(
            flops=8 * rows * rows * wide,
            bytes_accessed=12 * rows * wide,
            transcendentals=2 * rows * rows * heads,
        ),
        name="context_attend",
    )(at, lengths, q, kv, bias, near, far, *more)


def swap(x, axis, k):
    return lax.ppermute(x, axis, [(i, i ^ k) for i in range(lax.axis_size(axis))])


def gather_hosts(x, hosts):
    near = jnp.stack([x] + [swap(x, "hst", k) for k in range(2, hosts, 2)], axis=0)
    far = swap(near, "hst", 1)
    return jnp.concatenate([near, far], axis=0)


def anchor_quarters(block):
    rows, width = block.shape
    tall, wide = rows // 2, width // 2
    quarter = lambda y, x: block[y * tall : (y + 1) * tall, x * wide : (x + 1) * wide]
    return [quarter(1, 1), quarter(0, 1), quarter(1, 0), quarter(0, 0)]


def spread_anchor(quarters, hosts, groups):
    cores = groups // 2
    first = (lax.axis_index("hst") == 0) & (lax.axis_index("grp") == 0)
    slab = jnp.where(first, quarters[3], 0.0)
    for quarter, to in zip(quarters, [groups + cores, cores, groups]):
        slab = slab + lax.ppermute(quarter, BOTH, [(0, to)])
    wide = slab.shape[1] // cores
    piece = slab[:, :wide]
    for c in range(1, cores):
        pairs = [(x, x + c) for x in (0, cores)]
        piece = piece + lax.ppermute(slab[:, c * wide : (c + 1) * wide], "grp", pairs)
    far = hosts // 2
    while far >= 2:
        pairs = [(h, h + far) for h in range(hosts) if h % (2 * far) < 2]
        piece = piece + lax.ppermute(piece, "hst", pairs)
        far //= 2
    return piece


def per_device(queries, keys_values, token_ids, lengths, suffix_queries, suffix_kv):
    hosts, groups = lax.axis_size("hst"), lax.axis_size("grp")
    host, group = lax.axis_index("hst"), lax.axis_index("grp")
    rows = queries.shape[0]
    heads = suffix_queries.shape[1] // HSZ
    quarters, keys_values = lax.optimization_barrier(([anchor_quarters(x) for x in keys_values], keys_values))
    packed, suffix_queries = lax.optimization_barrier((pack(keys_values, groups), suffix_queries))
    swapped = lax.all_to_all(packed, "grp", split_axis=0, concat_axis=0, tiled=True)
    near = jnp.stack([spread_anchor(x, hosts, groups) for x in quarters])
    gathered = gather_hosts(suffix_queries, hosts)
    seen = (token_ids.reshape(-1, rows) >= NAMB) & (jnp.arange(rows)[None, :] < lengths[:, None])
    bias = jnp.where(seen, 0.0, NEG).astype(jnp.float32)
    cores = groups // 2
    suffix = functools.partial(suffix_attend, jnp.stack([host]), gathered, swapped, suffix_kv, bias)
    parts = suffix(0, 1, None)
    held = {0: [near, swap(near, "hst", 1)], cores: [swap(near, "grp", cores)]}
    held, parts = lax.optimization_barrier((held, parts))
    held[cores].append(swap(held[0][1], "grp", cores))
    for k in range(1, cores):
        held[k] = [swap(x, "grp", k) for x in held[0]]
        held[cores ^ k] = [swap(held[cores][0], "grp", k)]
    if heads > 1:
        parts = suffix(1, heads - 1, parts)
    held, parts = lax.optimization_barrier((held, parts))
    for k in range(1, cores):
        held[cores ^ k].append(swap(held[cores][1], "grp", k))
    coded = lax.all_to_all(parts.astype(jnp.float16), "hst", split_axis=0, concat_axis=0, tiled=True)
    context_out = None
    for k in range(groups):
        at = jnp.stack([host * groups + group, group ^ k, host % 2])
        context_out = context_attend(at, lengths, queries, keys_values, bias, *held[k], context_out)
    return (context_out, combine(coded.astype(jnp.float32)))


def solution(mesh):
    return jax.shard_map(
        per_device,
        mesh=mesh,
        in_specs=(
            P(("hst", "grp"), None),
            P(None, ("hst", "grp"), None),
            P(),
            P(),
            P("hst", "grp"),
            P(None, "hst", "grp"),
        ),
        out_specs=(P(("hst", "grp"), None), P("hst", "grp")),
        check_vma=False,
    )
```

```python
import functools
import math

import jax
import jax.numpy as jnp
from jax import lax
from jax.experimental import pallas as pl
from jax.experimental.pallas import tpu as pltpu
from jax.sharding import PartitionSpec as P

HSZ = 128
NAMB = 512
NEG = -1e30
FLOOR = -2000.0
EXTRA = 16
TILE = 256
C2 = math.log2(math.e) / math.sqrt(HSZ)
BOTH = ("hst", "grp")


def dot_t(a, b):
    return lax.dot_general(a, b, (((1,), (1,)), ((), ())), preferred_element_type=jnp.float32)


def dot(a, b):
    return lax.dot_general(a, b, (((1,), (0,)), ((), ())), preferred_element_type=jnp.float32)


def softmax(scores):
    top = functools.reduce(jnp.maximum, [jnp.max(s, axis=-1, keepdims=True) for s in scores])
    base = top * C2
    weights = [jnp.exp2(s * C2 - base) for s in scores]
    total = functools.reduce(jnp.add, [jnp.sum(w, axis=-1, keepdims=True) for w in weights])
    return base, total, [w.astype(jnp.bfloat16) for w in weights]


def pack_kernel(kv_ref, out_ref):
    groups, _, _, part = out_ref.shape
    for g in range(groups):
        out_ref[g, 0] = kv_ref[0, :, g * part : (g + 1) * part]


def pack(kv, groups):
    _, rows, width = kv.shape
    part = width // groups
    few = rows // 4
    return pl.pallas_call(
        pack_kernel,
        grid=(2, 4),
        in_specs=[pl.BlockSpec((1, few, width), lambda s, i: (s, i, 0))],
        out_specs=pl.BlockSpec((groups, 1, few, part), lambda s, i: (0, s, i, 0)),
        out_shape=jax.ShapeDtypeStruct((groups, 2, rows, part), kv.dtype),
        cost_estimate=pl.CostEstimate(flops=0, bytes_accessed=4 * kv.size, transcendentals=0),
        name="pack_heads",
    )(kv)


def pipelined(tasks, score, finish):
    ahead = score(tasks[0])
    for n, task in enumerate(tasks):
        scores = ahead
        if n + 1 < len(tasks):
            ahead = score(tasks[n + 1])
        finish(task, scores)


def suffix_kernel(at_ref, q_ref, kv_ref, sk_ref, bias_ref, *rest):
    out_ref = rest[-1]
    host = at_ref[0]
    groups = kv_ref.shape[0]
    hosts, share, _ = q_ref.shape
    apart = list(range(0, hosts, 2)) + list(range(1, hosts, 2))
    chunks = min(hosts, max(1, TILE // share))
    bias = [bias_ref[pl.ds(host * groups + g, 1), :] for g in range(groups)]
    values = [kv_ref[g, 1] for g in range(groups)] + [sk_ref[1]]

    def score(first):
        q = jnp.concatenate([q_ref[first + c] for c in range(chunks)], axis=0)
        s = dot_t(q, sk_ref[0])
        row = lax.broadcasted_iota(jnp.int32, (share, share), 0)
        spos = host * share + lax.broadcasted_iota(jnp.int32, (share, share), 1)
        late = []
        for c in range(chunks):
            qpos = jnp.bitwise_xor(host, apart[first + c]) * share + row
            late.append(jnp.where(spos <= qpos, s[c * share : (c + 1) * share], NEG))
        return [dot_t(q, kv_ref[g, 0]) + bias[g] for g in range(groups)] + [jnp.concatenate(late, axis=0)]

    def finish(first, scores):
        base, total, weights = softmax(scores)
        mixed = functools.reduce(jnp.add, [dot(w, v) for w, v in zip(weights, values)])
        n = mixed / total
        size = jnp.max(jnp.abs(n), axis=-1, keepdims=True)
        shift = jnp.clip(jnp.floor(jnp.log2(size)), -100.0, 100.0)
        level = jnp.maximum(base + jnp.log2(total), FLOOR)
        whole = jnp.floor(level)
        rest = jnp.exp2(level - whole)
        coarse = jnp.round(rest * 512.0) * (1.0 / 512.0)
        fine = (rest - coarse) * 1024.0
        lane = lax.broadcasted_iota(jnp.int32, (chunks * share, HSZ), 1)
        stats = jnp.where(lane == 0, whole, jnp.where(lane == 1, coarse, jnp.where(lane == 2, fine, shift)))
        turned = stats.T
        n = n * jnp.exp2(-shift)
        for c in range(chunks):
            to = jnp.bitwise_xor(host, apart[first + c])
            out_ref[to, :share, :] = n[c * share : (c + 1) * share]
            out_ref[to, share : share + EXTRA, :share] = turned[:EXTRA, c * share : (c + 1) * share]

    pipelined(list(range(0, hosts, chunks)), score, finish)


def suffix_attend(host, q, kv, sk, bias, first, count, before):
    hosts, share, width = q.shape
    groups, _, rows, _ = kv.shape
    seen = groups * rows + share
    more = [] if before is None else [before]
    return pl.pallas_call(
        suffix_kernel,
        grid_spec=pltpu.PrefetchScalarGridSpec(
            num_scalar_prefetch=1,
            grid=(count,),
            in_specs=[
                pl.BlockSpec((hosts, share, HSZ), lambda i, at: (0, 0, first + i)),
                pl.BlockSpec((groups, 2, rows, HSZ), lambda i, at: (0, 0, 0, first + i)),
                pl.BlockSpec((2, share, HSZ), lambda i, at: (0, 0, first + i)),
                pl.BlockSpec(bias.shape, lambda i, at: (0, 0)),
            ]
            + [pl.BlockSpec(memory_space=pl.ANY) for _ in more],
            out_specs=pl.BlockSpec((hosts, share + EXTRA, HSZ), lambda i, at: (0, 0, first + i)),
        ),
        out_shape=jax.ShapeDtypeStruct((hosts, share + EXTRA, width), jnp.float32),
        input_output_aliases={5: 0} if more else {},
        compiler_params=pltpu.CompilerParams(vmem_limit_bytes=24 * 1024 * 1024),
        cost_estimate=pl.CostEstimate(
            flops=8 * count * hosts * share * seen * HSZ,
            bytes_accessed=4 * count * (groups * rows + 3 * hosts * share) * HSZ,
            transcendentals=count * hosts * share * seen,
        ),
        name="suffix_attend",
    )(host, q, kv, sk, bias, *more)


def combine_kernel(in_ref, out_ref):
    hosts, tall, _ = in_ref.shape
    share = tall - EXTRA
    whole, coarse, fine, shift = [in_ref[:, share + k, :] for k in range(4)]
    weight = jnp.exp2(whole - jnp.max(whole, axis=0, keepdims=True)) * (coarse + fine * (1.0 / 1024.0))
    factor = weight * jnp.exp2(shift) / jnp.sum(weight, axis=0, keepdims=True)
    factor = jnp.concatenate([factor, jnp.zeros((HSZ - hosts, HSZ), jnp.float32)], axis=0).T[:share, :]
    mixed = 0.0
    for g in range(hosts):
        mixed = mixed + factor[:, g : g + 1] * in_ref[g, :share, :]
    out_ref[...] = mixed.astype(out_ref.dtype)


def combine(parts):
    hosts, tall, width = parts.shape
    return pl.pallas_call(
        combine_kernel,
        grid=(width // HSZ,),
        in_specs=[pl.BlockSpec((hosts, tall, HSZ), lambda h: (0, 0, h))],
        out_specs=pl.BlockSpec((tall - EXTRA, HSZ), lambda h: (0, h)),
        out_shape=jax.ShapeDtypeStruct((tall - EXTRA, width), jnp.bfloat16),
        cost_estimate=pl.CostEstimate(flops=2 * parts.size, bytes_accessed=4 * parts.size, transcendentals=0),
        name="combine_groups",
    )(parts)


def context_kernel(at_ref, len_ref, q_ref, kv_ref, bias_ref, near_ref, far_ref, *rest):
    out_ref, diag_ref = rest[-2:]
    block, odd = at_ref[0], at_ref[2]
    rows, width = q_ref.shape
    half = rows // 2
    own = bias_ref[pl.ds(block, 1), :]
    row = lax.broadcasted_iota(jnp.int32, (half, half), 0)
    col = lax.broadcasted_iota(jnp.int32, (half, half), 1)
    for t in range(2):
        ok = own[:, t * half : (t + 1) * half]
        diag_ref[t] = jnp.where(col == row, 0.0, jnp.where(col < row, ok, NEG))
    low, high = bias_ref[0:1, :half], bias_ref[0:1, half:]
    near_bias = jnp.where(block > 0, jnp.where(odd == 0, low, high), NEG)
    far_bias = jnp.where(block > 0, jnp.where(odd == 0, high, low), NEG)

    def score(task):
        first, t = task
        head = slice(first, first + HSZ)
        q = q_ref[t * half : (t + 1) * half, head]
        scores = [dot_t(q, near_ref[0, :, head]) + near_bias, dot_t(q, far_ref[0, :, head]) + far_bias]
        if t == 1:
            scores.append(dot_t(q, kv_ref[0, :half, head]) + own[:, :half])
        scores.append(dot_t(q, kv_ref[0, t * half : (t + 1) * half, head]) + diag_ref[t])
        return scores

    def finish(task, scores):
        first, t = task
        head = slice(first, first + HSZ)
        _, total, weights = softmax(scores)
        values = [near_ref[1, :, head], far_ref[1, :, head]]
        values += [kv_ref[1, u * half : (u + 1) * half, head] for u in range(t + 1)]
        mixed = functools.reduce(jnp.add, [dot(w, v) for w, v in zip(weights, values)])
        place = t * half + lax.broadcasted_iota(jnp.int32, mixed.shape, 0)
        out = jnp.where(place < len_ref[block], mixed / total, 0.0)
        out_ref[t * half : (t + 1) * half, head] = out.astype(out_ref.dtype)

    pipelined([(first, t) for first in range(0, width, HSZ) for t in range(2)], score, finish)


def context_attend(at, lengths, q, kv, bias, near, far, before):
    rows, width = q.shape
    _, half, wide = near.shape
    heads = wide // HSZ
    both = lambda i, at, n: (0, 0, at[1])
    more = [] if before is None else [before]
    return pl.pallas_call(
        context_kernel,
        grid_spec=pltpu.PrefetchScalarGridSpec(
            num_scalar_prefetch=2,
            grid=(1,),
            in_specs=[
                pl.BlockSpec((rows, wide), lambda i, at, n: (0, at[1])),
                pl.BlockSpec((2, rows, wide), both),
                pl.BlockSpec(bias.shape, lambda i, *_: (0, 0)),
                pl.BlockSpec((2, half, wide), lambda i, *_: (0, 0, 0)),
                pl.BlockSpec((2, half, wide), lambda i, *_: (0, 0, 0)),
            ]
            + [pl.BlockSpec(memory_space=pl.ANY) for _ in more],
            out_specs=pl.BlockSpec((rows, wide), lambda i, at, n: (0, at[1])),
            scratch_shapes=[pltpu.VMEM((2, half, half), jnp.float32)],
        ),
        out_shape=jax.ShapeDtypeStruct((rows, width), q.dtype),
        input_output_aliases={7: 0} if more else {},
        compiler_params=pltpu.CompilerParams(vmem_limit_bytes=24 * 1024 * 1024),
        cost_estimate=pl.CostEstimate(
            flops=8 * rows * rows * wide,
            bytes_accessed=12 * rows * wide,
            transcendentals=2 * rows * rows * heads,
        ),
        name="context_attend",
    )(at, lengths, q, kv, bias, near, far, *more)


def swap(x, axis, k):
    return lax.ppermute(x, axis, [(i, i ^ k) for i in range(lax.axis_size(axis))])


def gather_hosts(x, hosts):
    near = jnp.stack([x] + [swap(x, "hst", k) for k in range(2, hosts, 2)], axis=0)
    far = swap(near, "hst", 1)
    return jnp.concatenate([near, far], axis=0)


def after(x, done):
    return lax.optimization_barrier((x, done))[0]


def quarter(kv, y, x):
    _, rows, width = kv.shape
    tall, wide = rows // 2, width // 2
    return kv[:, y * tall : (y + 1) * tall, x * wide : (x + 1) * wide]


def scatter_anchor(mine, across, diagonal, below, groups):
    cores = groups // 2
    first = (lax.axis_index("hst") == 0) & (lax.axis_index("grp") == 0)
    send = lambda x, to: lax.ppermute(x, BOTH, [(0, to)])
    down = send(below, groups)
    slabs = []
    for s in range(2):
        slab = jnp.where(first, mine[s], 0.0) + send(diagonal[s], groups + cores) + send(across[s], cores)
        slabs.append(slab + (after(down[s], slabs[0]) if s else down[s]))
    return slabs


def spread_anchor(slab, hosts, groups):
    cores = groups // 2
    wide = slab.shape[1] // cores
    piece = slab[:, :wide]
    for c in range(1, cores):
        pairs = [(x, x + c) for x in (0, cores)]
        piece = piece + lax.ppermute(slab[:, c * wide : (c + 1) * wide], "grp", pairs)
    far = hosts // 2
    while far >= 2:
        pairs = [(h, h + far) for h in range(hosts) if h % (2 * far) < 2]
        piece = piece + lax.ppermute(piece, "hst", pairs)
        far //= 2
    return piece


def per_device(queries, keys_values, token_ids, lengths, suffix_queries, suffix_kv):
    hosts, groups = lax.axis_size("hst"), lax.axis_size("grp")
    host, group = lax.axis_index("hst"), lax.axis_index("grp")
    rows = queries.shape[0]
    heads = suffix_queries.shape[1] // HSZ
    quarters = [quarter(keys_values, y, x) for y, x in ((0, 0), (0, 1), (1, 1), (1, 0))]
    quarters, keys_values = lax.optimization_barrier((quarters, keys_values))
    swapped = lax.all_to_all(pack(keys_values, groups), "grp", split_axis=0, concat_axis=0, tiled=True)
    slabs = scatter_anchor(*quarters, groups)
    near = jnp.stack([spread_anchor(x, hosts, groups) for x in slabs])
    suffix_queries = after(suffix_queries, slabs[0])
    gathered = gather_hosts(suffix_queries, hosts)
    seen = (token_ids.reshape(-1, rows) >= NAMB) & (jnp.arange(rows)[None, :] < lengths[:, None])
    bias = jnp.where(seen, 0.0, NEG).astype(jnp.float32)
    cores = groups // 2
    suffix = functools.partial(suffix_attend, jnp.stack([host]), gathered, swapped, suffix_kv, bias)
    parts = suffix(0, 1, None)
    held = {0: [near, swap(near, "hst", 1)], cores: [swap(near, "grp", cores)]}
    held, parts = lax.optimization_barrier((held, parts))
    held[cores].append(swap(held[0][1], "grp", cores))
    for k in range(1, cores):
        held[k] = [swap(x, "grp", k) for x in held[0]]
        held[cores ^ k] = [swap(held[cores][0], "grp", k)]
    if heads > 1:
        parts = suffix(1, heads - 1, parts)
    held, parts = lax.optimization_barrier((held, parts))
    for k in range(1, cores):
        held[cores ^ k].append(swap(held[cores][1], "grp", k))
    coded = lax.all_to_all(parts.astype(jnp.float16), "hst", split_axis=0, concat_axis=0, tiled=True)
    context_out = None
    for k in range(groups):
        at = jnp.stack([host * groups + group, group ^ k, host % 2])
        context_out = context_attend(at, lengths, queries, keys_values, bias, *held[k], context_out)
    return (context_out, combine(coded.astype(jnp.float32)))


def solution(mesh):
    return jax.shard_map(
        per_device,
        mesh=mesh,
        in_specs=(
            P(("hst", "grp"), None),
            P(None, ("hst", "grp"), None),
            P(),
            P(),
            P("hst", "grp"),
            P(None, "hst", "grp"),
        ),
        out_specs=(P(("hst", "grp"), None), P("hst", "grp")),
        check_vma=False,
    )
```

```python
import functools
import math

import jax
import jax.numpy as jnp
from jax import lax
from jax.experimental import pallas as pl
from jax.experimental.pallas import tpu as pltpu
from jax.sharding import PartitionSpec as P

HSZ = 128
NAMB = 512
NEG = -1e30
FLOOR = -2000.0
EXTRA = 16
TILE = 256
C2 = math.log2(math.e) / math.sqrt(HSZ)
BOTH = ("hst", "grp")


def dot_t(a, b):
    return lax.dot_general(a, b, (((1,), (1,)), ((), ())), preferred_element_type=jnp.float32)


def dot(a, b):
    return lax.dot_general(a, b, (((1,), (0,)), ((), ())), preferred_element_type=jnp.float32)


def softmax(scores):
    top = functools.reduce(jnp.maximum, [jnp.max(s, axis=-1, keepdims=True) for s in scores])
    base = top * C2
    weights = [jnp.exp2(s * C2 - base) for s in scores]
    total = functools.reduce(jnp.add, [jnp.sum(w, axis=-1, keepdims=True) for w in weights])
    return base, total, [w.astype(jnp.bfloat16) for w in weights]


def pack_kernel(kv_ref, out_ref):
    groups, _, _, part = out_ref.shape
    for g in range(groups):
        out_ref[g, 0] = kv_ref[0, :, g * part : (g + 1) * part]


def pack(kv, groups):
    _, rows, width = kv.shape
    part = width // groups
    few = rows // 4
    return pl.pallas_call(
        pack_kernel,
        grid=(2, 4),
        in_specs=[pl.BlockSpec((1, few, width), lambda s, i: (s, i, 0))],
        out_specs=pl.BlockSpec((groups, 1, few, part), lambda s, i: (0, s, i, 0)),
        out_shape=jax.ShapeDtypeStruct((groups, 2, rows, part), kv.dtype),
        cost_estimate=pl.CostEstimate(flops=0, bytes_accessed=4 * kv.size, transcendentals=0),
        name="pack_heads",
    )(kv)


def pipelined(tasks, score, finish):
    ahead = score(tasks[0])
    for n, task in enumerate(tasks):
        scores = ahead
        if n + 1 < len(tasks):
            ahead = score(tasks[n + 1])
        finish(task, scores)


def suffix_kernel(at_ref, q_ref, kv_ref, sk_ref, bias_ref, *rest):
    out_ref = rest[-1]
    host = at_ref[0]
    groups = kv_ref.shape[0]
    hosts, share, _ = q_ref.shape
    apart = list(range(0, hosts, 2)) + list(range(1, hosts, 2))
    chunks = min(hosts, max(1, TILE // share))
    bias = [bias_ref[pl.ds(host * groups + g, 1), :] for g in range(groups)]
    values = [kv_ref[g, 1] for g in range(groups)] + [sk_ref[1]]

    def score(first):
        q = jnp.concatenate([q_ref[first + c] for c in range(chunks)], axis=0)
        s = dot_t(q, sk_ref[0])
        row = lax.broadcasted_iota(jnp.int32, (share, share), 0)
        spos = host * share + lax.broadcasted_iota(jnp.int32, (share, share), 1)
        late = []
        for c in range(chunks):
            qpos = jnp.bitwise_xor(host, apart[first + c]) * share + row
            late.append(jnp.where(spos <= qpos, s[c * share : (c + 1) * share], NEG))
        return [dot_t(q, kv_ref[g, 0]) + bias[g] for g in range(groups)] + [jnp.concatenate(late, axis=0)]

    def finish(first, scores):
        base, total, weights = softmax(scores)
        mixed = functools.reduce(jnp.add, [dot(w, v) for w, v in zip(weights, values)])
        n = mixed / total
        size = jnp.max(jnp.abs(n), axis=-1, keepdims=True)
        shift = jnp.clip(jnp.floor(jnp.log2(size)), -100.0, 100.0)
        level = jnp.maximum(base + jnp.log2(total), FLOOR)
        whole = jnp.floor(level)
        rest = jnp.exp2(level - whole)
        coarse = jnp.round(rest * 512.0) * (1.0 / 512.0)
        fine = (rest - coarse) * 1024.0
        lane = lax.broadcasted_iota(jnp.int32, (chunks * share, HSZ), 1)
        stats = jnp.where(lane == 0, whole, jnp.where(lane == 1, coarse, jnp.where(lane == 2, fine, shift)))
        turned = stats.T
        n = n * jnp.exp2(-shift)
        for c in range(chunks):
            to = jnp.bitwise_xor(host, apart[first + c])
            out_ref[to, :share, :] = n[c * share : (c + 1) * share]
            out_ref[to, share : share + EXTRA, :share] = turned[:EXTRA, c * share : (c + 1) * share]

    pipelined(list(range(0, hosts, chunks)), score, finish)


def suffix_attend(host, q, kv, sk, bias, first, count, before):
    hosts, share, width = q.shape
    groups, _, rows, _ = kv.shape
    seen = groups * rows + share
    more = [] if before is None else [before]
    return pl.pallas_call(
        suffix_kernel,
        grid_spec=pltpu.PrefetchScalarGridSpec(
            num_scalar_prefetch=1,
            grid=(count,),
            in_specs=[
                pl.BlockSpec((hosts, share, HSZ), lambda i, at: (0, 0, first + i)),
                pl.BlockSpec((groups, 2, rows, HSZ), lambda i, at: (0, 0, 0, first + i)),
                pl.BlockSpec((2, share, HSZ), lambda i, at: (0, 0, first + i)),
                pl.BlockSpec(bias.shape, lambda i, at: (0, 0)),
            ]
            + [pl.BlockSpec(memory_space=pl.ANY) for _ in more],
            out_specs=pl.BlockSpec((hosts, share + EXTRA, HSZ), lambda i, at: (0, 0, first + i)),
        ),
        out_shape=jax.ShapeDtypeStruct((hosts, share + EXTRA, width), jnp.float32),
        input_output_aliases={5: 0} if more else {},
        compiler_params=pltpu.CompilerParams(vmem_limit_bytes=24 * 1024 * 1024),
        cost_estimate=pl.CostEstimate(
            flops=8 * count * hosts * share * seen * HSZ,
            bytes_accessed=4 * count * (groups * rows + 3 * hosts * share) * HSZ,
            transcendentals=count * hosts * share * seen,
        ),
        name="suffix_attend",
    )(host, q, kv, sk, bias, *more)


def combine_kernel(in_ref, out_ref):
    hosts, tall, _ = in_ref.shape
    share = tall - EXTRA
    whole, coarse, fine, shift = [in_ref[:, share + k, :] for k in range(4)]
    weight = jnp.exp2(whole - jnp.max(whole, axis=0, keepdims=True)) * (coarse + fine * (1.0 / 1024.0))
    factor = weight * jnp.exp2(shift) / jnp.sum(weight, axis=0, keepdims=True)
    factor = jnp.concatenate([factor, jnp.zeros((HSZ - hosts, HSZ), jnp.float32)], axis=0).T[:share, :]
    mixed = 0.0
    for g in range(hosts):
        mixed = mixed + factor[:, g : g + 1] * in_ref[g, :share, :]
    out_ref[...] = mixed.astype(out_ref.dtype)


def combine(parts):
    hosts, tall, width = parts.shape
    return pl.pallas_call(
        combine_kernel,
        grid=(width // HSZ,),
        in_specs=[pl.BlockSpec((hosts, tall, HSZ), lambda h: (0, 0, h))],
        out_specs=pl.BlockSpec((tall - EXTRA, HSZ), lambda h: (0, h)),
        out_shape=jax.ShapeDtypeStruct((tall - EXTRA, width), jnp.bfloat16),
        cost_estimate=pl.CostEstimate(flops=2 * parts.size, bytes_accessed=4 * parts.size, transcendentals=0),
        name="combine_groups",
    )(parts)


def context_kernel(at_ref, len_ref, q_ref, kv_ref, bias_ref, near_ref, far_ref, *rest):
    out_ref, diag_ref = rest[-2:]
    block, odd, level = at_ref[0], at_ref[2], at_ref[3]
    rows, width = q_ref.shape
    half = rows // 2
    own = bias_ref[pl.ds(block, 1), :]
    row = lax.broadcasted_iota(jnp.int32, (half, half), 0)
    col = lax.broadcasted_iota(jnp.int32, (half, half), 1)
    for t in range(2):
        ok = own[:, t * half : (t + 1) * half]
        diag_ref[t] = jnp.where(col == row, 0.0, jnp.where(col < row, ok, NEG))
    low, high = bias_ref[0:1, :half], bias_ref[0:1, half:]
    near_bias = jnp.where(block > 0, jnp.where(odd == 0, low, high), NEG)
    far_bias = jnp.where(block > 0, jnp.where(odd == 0, high, low), NEG)

    def anchor(ref, which, head):
        order = [jnp.bitwise_xor(level, z) for z in range(ref.shape[0])]
        return jnp.concatenate([ref[z, which, :, head] for z in order], axis=0)

    def score(task):
        first, t = task
        head = slice(first, first + HSZ)
        q = q_ref[t * half : (t + 1) * half, head]
        scores = [dot_t(q, anchor(near_ref, 0, head)) + near_bias, dot_t(q, anchor(far_ref, 0, head)) + far_bias]
        if t == 1:
            scores.append(dot_t(q, kv_ref[0, :half, head]) + own[:, :half])
        scores.append(dot_t(q, kv_ref[0, t * half : (t + 1) * half, head]) + diag_ref[t])
        return scores

    def finish(task, scores):
        first, t = task
        head = slice(first, first + HSZ)
        _, total, weights = softmax(scores)
        values = [anchor(near_ref, 1, head), anchor(far_ref, 1, head)]
        values += [kv_ref[1, u * half : (u + 1) * half, head] for u in range(t + 1)]
        mixed = functools.reduce(jnp.add, [dot(w, v) for w, v in zip(weights, values)])
        place = t * half + lax.broadcasted_iota(jnp.int32, mixed.shape, 0)
        out = jnp.where(place < len_ref[block], mixed / total, 0.0)
        out_ref[t * half : (t + 1) * half, head] = out.astype(out_ref.dtype)

    pipelined([(first, t) for first in range(0, width, HSZ) for t in range(2)], score, finish)


def context_attend(at, lengths, q, kv, bias, near, far, before):
    rows, width = q.shape
    half = rows // 2
    wide = near.shape[3]
    heads = wide // HSZ
    both = lambda i, at, n: (0, 0, at[1])
    more = [] if before is None else [before]
    return pl.pallas_call(
        context_kernel,
        grid_spec=pltpu.PrefetchScalarGridSpec(
            num_scalar_prefetch=2,
            grid=(1,),
            in_specs=[
                pl.BlockSpec((rows, wide), lambda i, at, n: (0, at[1])),
                pl.BlockSpec((2, rows, wide), both),
                pl.BlockSpec(bias.shape, lambda i, *_: (0, 0)),
                pl.BlockSpec(near.shape, lambda i, *_: (0, 0, 0, 0)),
                pl.BlockSpec(far.shape, lambda i, *_: (0, 0, 0, 0)),
            ]
            + [pl.BlockSpec(memory_space=pl.ANY) for _ in more],
            out_specs=pl.BlockSpec((rows, wide), lambda i, at, n: (0, at[1])),
            scratch_shapes=[pltpu.VMEM((2, half, half), jnp.float32)],
        ),
        out_shape=jax.ShapeDtypeStruct((rows, width), q.dtype),
        input_output_aliases={7: 0} if more else {},
        compiler_params=pltpu.CompilerParams(vmem_limit_bytes=24 * 1024 * 1024),
        cost_estimate=pl.CostEstimate(
            flops=8 * rows * rows * wide,
            bytes_accessed=12 * rows * wide,
            transcendentals=2 * rows * rows * heads,
        ),
        name="context_attend",
    )(at, lengths, q, kv, bias, near, far, *more)


def swap(x, axis, k):
    return lax.ppermute(x, axis, [(i, i ^ k) for i in range(lax.axis_size(axis))])


def gather_hosts(x, hosts):
    near = jnp.stack([x] + [swap(x, "hst", k) for k in range(2, hosts, 2)], axis=0)
    far = swap(near, "hst", 1)
    return jnp.concatenate([near, far], axis=0)


def after(x, done):
    return lax.optimization_barrier((x, done))[0]


def scatter_rows(kv, hosts, groups):
    part = kv.shape[1] // hosts
    levels = hosts // 2
    rows = lambda p, count=1: kv[:, p * part : (p + count) * part]
    send = lambda x, a, b: lax.ppermute(x, BOTH, [(a * groups, b * groups)])
    first = (lax.axis_index("hst") == 0) & (lax.axis_index("grp") == 0)
    passing = send(rows(levels + 1, levels - 2), 0, 1)
    pieces = [jnp.where(first, rows(0), 0.0)]
    pieces += [send(rows(hosts - 1), 0, hosts - 1)]
    pieces += [send(rows(z), 0, 2 * z) for z in range(levels - 1, 0, -1)]
    pieces += [send(rows(levels), 0, 1)]
    pieces += [send(passing[:, (z - 1) * part : z * part], 1, 2 * z + 1) for z in range(levels - 2, 0, -1)]
    return functools.reduce(jnp.add, pieces), passing


def share_heads(slab, groups):
    wide = slab.shape[2] // groups
    piece = slab[:, :, :wide]
    for g in range(1, groups):
        piece = piece + lax.ppermute(slab[:, :, g * wide : (g + 1) * wide], "grp", [(0, g)])
    return piece


def per_device(queries, keys_values, token_ids, lengths, suffix_queries, suffix_kv):
    hosts, groups = lax.axis_size("hst"), lax.axis_size("grp")
    host, group = lax.axis_index("hst"), lax.axis_index("grp")
    cores = groups // 2
    rows = queries.shape[0]
    heads = suffix_queries.shape[1] // HSZ
    packed, keys_values = lax.optimization_barrier((pack(keys_values, groups), keys_values))
    swapped = lax.all_to_all(packed, "grp", split_axis=0, concat_axis=0, tiled=True)
    slab, passing = scatter_rows(keys_values, hosts, groups)
    gathered = gather_hosts(after(suffix_queries, passing), hosts)
    piece = share_heads(slab, groups)
    chunks = [piece] + [swap(piece, "hst", k) for k in range(2, hosts, 2)]
    seen = (token_ids.reshape(-1, rows) >= NAMB) & (jnp.arange(rows)[None, :] < lengths[:, None])
    bias = jnp.where(seen, 0.0, NEG).astype(jnp.float32)
    parts = suffix_attend(jnp.stack([host]), gathered, swapped, suffix_kv, bias, 0, heads, None)
    parts = parts.astype(jnp.float16)
    coded = lax.all_to_all(parts, "hst", split_axis=0, concat_axis=0, tiled=True)

    def context(k, anchor, before):
        at = jnp.stack([host * groups + group, group ^ k, host % 2, host // 2])
        return context_attend(at, lengths, queries, keys_values, bias, *anchor, before)

    near = jnp.stack(after(chunks, parts))
    far = swap(near, "hst", 1)
    held = {0: [near, far], cores: [swap(near, "grp", cores), swap(far, "grp", cores)]}
    for k in range(1, cores):
        held[k] = [swap(x, "grp", k) for x in held[0]]
    context_out = context(0, held[0], None)
    other = after(held[cores], context_out)
    for k in range(1, cores):
        held[cores ^ k] = [swap(x, "grp", k) for x in other]
    for k in range(1, groups):
        context_out = context(k, held[k], context_out)
    return (context_out, combine(coded.astype(jnp.float32)))


def solution(mesh):
    return jax.shard_map(
        per_device,
        mesh=mesh,
        in_specs=(
            P(("hst", "grp"), None),
            P(None, ("hst", "grp"), None),
            P(),
            P(),
            P("hst", "grp"),
            P(None, "hst", "grp"),
        ),
        out_specs=(P(("hst", "grp"), None), P("hst", "grp")),
        check_vma=False,
    )
```

```python
import functools
import math

import jax
import jax.numpy as jnp
from jax import lax
from jax.experimental import pallas as pl
from jax.experimental.pallas import tpu as pltpu
from jax.sharding import PartitionSpec as P

HSZ = 128
NAMB = 512
NEG = -1e30
FLOOR = -2000.0
EXTRA = 8
TILE = 256
C2 = math.log2(math.e) / math.sqrt(HSZ)
BOTH = ("hst", "grp")


def dot_t(a, b):
    return lax.dot_general(a, b, (((1,), (1,)), ((), ())), preferred_element_type=jnp.float32)


def dot(a, b):
    return lax.dot_general(a, b, (((1,), (0,)), ((), ())), preferred_element_type=jnp.float32)


def softmax(scores):
    top = functools.reduce(jnp.maximum, [jnp.max(s, axis=-1, keepdims=True) for s in scores])
    base = top * C2
    weights = [jnp.exp2(s * C2 - base) for s in scores]
    total = functools.reduce(jnp.add, [jnp.sum(w, axis=-1, keepdims=True) for w in weights])
    return base, total, [w.astype(jnp.bfloat16) for w in weights]


def pack_kernel(kv_ref, out_ref, below_ref, *refs):
    across_refs, diagonal_refs, (held, came, left) = refs[0:2], refs[2:4], refs[4:]
    groups, _, rows, part = out_ref.shape
    few, wide, pieces = rows // 4, groups * part // 2, [(s, i) for s in range(2) for i in range(4)]
    arrive = {}
    for s, i in pieces:
        band = pl.ds(i * few, few)
        arrive[s, i] = pltpu.make_async_copy(kv_ref.at[s, band], held.at[s, band], came.at[s, i])
        arrive[s, i].start()
    leave = []
    for s, i in pieces:
        arrive[s, i].wait()
        band, place = pl.ds(i * few, few), pl.ds(i % 2 * few, few)
        right = held.at[s, band, pl.ds(wide, wide)]
        moves = [(right, (across_refs if i < 2 else diagonal_refs)[s].at[place])]
        if i >= 2:
            moves.append((held.at[s, band, pl.ds(0, wide)], below_ref.at[s, place]))
        moves += [(held.at[s, band, pl.ds(g * part, part)], out_ref.at[g, s, band]) for g in range(groups)]
        for n, (source, target) in enumerate(moves):
            leave.append(pltpu.make_async_copy(source, target, left.at[s, i, n]))
            leave[-1].start()
    for copy in leave:
        copy.wait()


def pack(kv, groups):
    _, rows, width = kv.shape
    anywhere = pl.BlockSpec(memory_space=pl.ANY)
    half = jax.ShapeDtypeStruct((rows // 2, width // 2), kv.dtype)
    out, below, *others = pl.pallas_call(
        pack_kernel,
        in_specs=[anywhere],
        out_specs=[anywhere] * 6,
        out_shape=[
            jax.ShapeDtypeStruct((groups, 2, rows, width // groups), kv.dtype),
            jax.ShapeDtypeStruct((2, rows // 2, width // 2), kv.dtype),
        ]
        + [half] * 4,
        scratch_shapes=[
            pltpu.VMEM(kv.shape, kv.dtype),
            pltpu.SemaphoreType.DMA((2, 4)),
            pltpu.SemaphoreType.DMA((2, 4, groups + 2)),
        ],
        cost_estimate=pl.CostEstimate(flops=0, bytes_accessed=6 * kv.size, transcendentals=0),
        name="pack_heads",
    )(kv)
    return out, below, others[:2], others[2:]


def pipelined(tasks, score, finish):
    ahead = score(tasks[0])
    for n, task in enumerate(tasks):
        scores = ahead
        if n + 1 < len(tasks):
            ahead = score(tasks[n + 1])
        finish(task, scores)


def suffix_kernel(at_ref, q_ref, kv_ref, sk_ref, bias_ref, *rest):
    out_ref = rest[-1]
    host = at_ref[0]
    groups = kv_ref.shape[0]
    hosts, share, _ = q_ref.shape
    apart = list(range(0, hosts, 2)) + list(range(1, hosts, 2))
    chunks = min(hosts, max(1, TILE // share))
    bias = [bias_ref[pl.ds(host * groups + g, 1), :] for g in range(groups)]
    values = [kv_ref[g, 1] for g in range(groups)] + [sk_ref[1]]

    def score(first):
        q = jnp.concatenate([q_ref[first + c] for c in range(chunks)], axis=0)
        s = dot_t(q, sk_ref[0])
        row = lax.broadcasted_iota(jnp.int32, (share, share), 0)
        spos = host * share + lax.broadcasted_iota(jnp.int32, (share, share), 1)
        late = []
        for c in range(chunks):
            qpos = jnp.bitwise_xor(host, apart[first + c]) * share + row
            late.append(jnp.where(spos <= qpos, s[c * share : (c + 1) * share], NEG))
        return [dot_t(q, kv_ref[g, 0]) + bias[g] for g in range(groups)] + [jnp.concatenate(late, axis=0)]

    def finish(first, scores):
        base, total, weights = softmax(scores)
        mixed = functools.reduce(jnp.add, [dot(w, v) for w, v in zip(weights, values)])
        n = mixed / total
        size = jnp.max(jnp.abs(n), axis=-1, keepdims=True)
        shift = jnp.clip(jnp.floor(jnp.log2(size)), -100.0, 100.0)
        level = jnp.maximum(base + jnp.log2(total), FLOOR)
        whole = jnp.floor(level)
        rest = jnp.exp2(level - whole)
        coarse = jnp.round(rest * 512.0) * (1.0 / 512.0)
        fine = (rest - coarse) * 1024.0
        lane = lax.broadcasted_iota(jnp.int32, (chunks * share, HSZ), 1)
        stats = jnp.where(lane == 0, whole, jnp.where(lane == 1, coarse, jnp.where(lane == 2, fine, shift)))
        turned = stats.T
        n = n * jnp.exp2(-shift)
        for c in range(chunks):
            to = jnp.bitwise_xor(host, apart[first + c])
            out_ref[to, :share, :] = n[c * share : (c + 1) * share]
            out_ref[to, share : share + EXTRA, :share] = turned[:EXTRA, c * share : (c + 1) * share]

    pipelined(list(range(0, hosts, chunks)), score, finish)


def suffix_attend(host, q, kv, sk, bias, first, count, before):
    hosts, share, width = q.shape
    groups, _, rows, _ = kv.shape
    seen = groups * rows + share
    more = [] if before is None else [before]
    return pl.pallas_call(
        suffix_kernel,
        grid_spec=pltpu.PrefetchScalarGridSpec(
            num_scalar_prefetch=1,
            grid=(count,),
            in_specs=[
                pl.BlockSpec((hosts, share, HSZ), lambda i, at: (0, 0, first + i)),
                pl.BlockSpec((groups, 2, rows, HSZ), lambda i, at: (0, 0, 0, first + i)),
                pl.BlockSpec((2, share, HSZ), lambda i, at: (0, 0, first + i)),
                pl.BlockSpec(bias.shape, lambda i, at: (0, 0)),
            ]
            + [pl.BlockSpec(memory_space=pl.ANY) for _ in more],
            out_specs=pl.BlockSpec((hosts, share + EXTRA, HSZ), lambda i, at: (0, 0, first + i)),
        ),
        out_shape=jax.ShapeDtypeStruct((hosts, share + EXTRA, width), jnp.float32),
        input_output_aliases={5: 0} if more else {},
        compiler_params=pltpu.CompilerParams(vmem_limit_bytes=60 * 1024 * 1024),
        cost_estimate=pl.CostEstimate(
            flops=8 * count * hosts * share * seen * HSZ,
            bytes_accessed=4 * count * (groups * rows + 3 * hosts * share) * HSZ,
            transcendentals=count * hosts * share * seen,
        ),
        name="suffix_attend",
    )(host, q, kv, sk, bias, *more)


def combine_kernel(in_ref, out_ref):
    hosts, tall, _ = in_ref.shape
    share = tall - EXTRA
    whole, coarse, fine, shift = [in_ref[:, share + k, :] for k in range(4)]
    weight = jnp.exp2(whole - jnp.max(whole, axis=0, keepdims=True)) * (coarse + fine * (1.0 / 1024.0))
    factor = weight * jnp.exp2(shift) / jnp.sum(weight, axis=0, keepdims=True)
    factor = jnp.concatenate([factor, jnp.zeros((HSZ - hosts, HSZ), jnp.float32)], axis=0).T[:share, :]
    mixed = 0.0
    for g in range(hosts):
        mixed = mixed + factor[:, g : g + 1] * in_ref[g, :share, :]
    out_ref[...] = mixed.astype(out_ref.dtype)


def combine(parts):
    hosts, tall, width = parts.shape
    return pl.pallas_call(
        combine_kernel,
        grid=(width // HSZ,),
        in_specs=[pl.BlockSpec((hosts, tall, HSZ), lambda h: (0, 0, h))],
        out_specs=pl.BlockSpec((tall - EXTRA, HSZ), lambda h: (0, h)),
        out_shape=jax.ShapeDtypeStruct((tall - EXTRA, width), jnp.bfloat16),
        cost_estimate=pl.CostEstimate(flops=2 * parts.size, bytes_accessed=4 * parts.size, transcendentals=0),
        name="combine_groups",
    )(parts)


def context_kernel(at_ref, len_ref, q_ref, kv_ref, bias_ref, near_ref, far_ref, *rest):
    out_ref, diag_ref = rest[-2:]
    block, odd = at_ref[0], at_ref[2]
    rows, width = q_ref.shape
    half = rows // 2
    own = bias_ref[pl.ds(block, 1), :]
    row = lax.broadcasted_iota(jnp.int32, (half, half), 0)
    col = lax.broadcasted_iota(jnp.int32, (half, half), 1)
    for t in range(2):
        ok = own[:, t * half : (t + 1) * half]
        diag_ref[t] = jnp.where(col == row, 0.0, jnp.where(col < row, ok, NEG))
    low, high = bias_ref[0:1, :half], bias_ref[0:1, half:]
    near_bias = jnp.where(block > 0, jnp.where(odd == 0, low, high), NEG)
    far_bias = jnp.where(block > 0, jnp.where(odd == 0, high, low), NEG)

    def score(task):
        first, t = task
        head = slice(first, first + HSZ)
        q = q_ref[t * half : (t + 1) * half, head]
        scores = [dot_t(q, near_ref[0, :, head]) + near_bias, dot_t(q, far_ref[0, :, head]) + far_bias]
        if t == 1:
            scores.append(dot_t(q, kv_ref[0, :half, head]) + own[:, :half])
        scores.append(dot_t(q, kv_ref[0, t * half : (t + 1) * half, head]) + diag_ref[t])
        return scores

    def finish(task, scores):
        first, t = task
        head = slice(first, first + HSZ)
        _, total, weights = softmax(scores)
        values = [near_ref[1, :, head], far_ref[1, :, head]]
        values += [kv_ref[1, u * half : (u + 1) * half, head] for u in range(t + 1)]
        mixed = functools.reduce(jnp.add, [dot(w, v) for w, v in zip(weights, values)])
        place = t * half + lax.broadcasted_iota(jnp.int32, mixed.shape, 0)
        out = jnp.where(place < len_ref[block], mixed / total, 0.0)
        out_ref[t * half : (t + 1) * half, head] = out.astype(out_ref.dtype)

    pipelined([(first, t) for first in range(0, width, HSZ) for t in range(2)], score, finish)


def context_attend(at, lengths, q, kv, bias, near, far, before):
    rows, width = q.shape
    _, half, wide = near.shape
    heads = wide // HSZ
    both = lambda i, at, n: (0, 0, at[1])
    more = [] if before is None else [before]
    return pl.pallas_call(
        context_kernel,
        grid_spec=pltpu.PrefetchScalarGridSpec(
            num_scalar_prefetch=2,
            grid=(1,),
            in_specs=[
                pl.BlockSpec((rows, wide), lambda i, at, n: (0, at[1])),
                pl.BlockSpec((2, rows, wide), both),
                pl.BlockSpec(bias.shape, lambda i, *_: (0, 0)),
                pl.BlockSpec((2, half, wide), lambda i, *_: (0, 0, 0)),
                pl.BlockSpec((2, half, wide), lambda i, *_: (0, 0, 0)),
            ]
            + [pl.BlockSpec(memory_space=pl.ANY) for _ in more],
            out_specs=pl.BlockSpec((rows, wide), lambda i, at, n: (0, at[1])),
            scratch_shapes=[pltpu.VMEM((2, half, half), jnp.float32)],
        ),
        out_shape=jax.ShapeDtypeStruct((rows, width), q.dtype),
        input_output_aliases={7: 0} if more else {},
        compiler_params=pltpu.CompilerParams(vmem_limit_bytes=60 * 1024 * 1024),
        cost_estimate=pl.CostEstimate(
            flops=8 * rows * rows * wide,
            bytes_accessed=12 * rows * wide,
            transcendentals=2 * rows * rows * heads,
        ),
        name="context_attend",
    )(at, lengths, q, kv, bias, near, far, *more)


def swap(x, axis, k):
    return lax.ppermute(x, axis, [(i, i ^ k) for i in range(lax.axis_size(axis))])


def gather_hosts(x, hosts):
    near = jnp.stack([x] + [swap(x, "hst", k) for k in range(2, hosts, 2)], axis=0)
    far = swap(near, "hst", 1)
    return jnp.concatenate([near, far], axis=0)


def after(x, done):
    return lax.optimization_barrier((x, done))[0]


def scatter_anchor(kv, across, diagonal, below, groups):
    cores = groups // 2
    first = (lax.axis_index("hst") == 0) & (lax.axis_index("grp") == 0)
    send = lambda x, to: lax.ppermute(x, BOTH, [(0, to)])
    down = send(below, groups)
    _, rows, width = kv.shape
    slabs = []
    for s in range(2):
        slab = jnp.where(first, kv[s, : rows // 2, : width // 2], 0.0) + send(diagonal[s], groups + cores) + send(across[s], cores)
        slabs.append(slab + (after(down[s], slabs[0]) if s else down[s]))
    return slabs


def spread_anchor(slab, hosts, groups):
    cores = groups // 2
    wide = slab.shape[1] // cores
    piece = slab[:, :wide]
    for c in range(1, cores):
        pairs = [(x, x + c) for x in (0, cores)]
        piece = piece + lax.ppermute(slab[:, c * wide : (c + 1) * wide], "grp", pairs)
    far = hosts // 2
    while far >= 2:
        pairs = [(h, h + far) for h in range(hosts) if h % (2 * far) < 2]
        piece = piece + lax.ppermute(piece, "hst", pairs)
        far //= 2
    return piece


def per_device(queries, keys_values, token_ids, lengths, suffix_queries, suffix_kv):
    hosts, groups = lax.axis_size("hst"), lax.axis_size("grp")
    host, group = lax.axis_index("hst"), lax.axis_index("grp")
    rows = queries.shape[0]
    heads = suffix_queries.shape[1] // HSZ
    packed, below, across, diagonal = pack(keys_values, groups)
    swapped = lax.all_to_all(packed, "grp", split_axis=0, concat_axis=0, tiled=True)
    slabs = scatter_anchor(keys_values, across, diagonal, below, groups)
    near = jnp.stack([spread_anchor(x, hosts, groups) for x in slabs])
    suffix_queries = after(suffix_queries, slabs[0])
    gathered = gather_hosts(suffix_queries, hosts)
    seen = (token_ids.reshape(-1, rows) >= NAMB) & (jnp.arange(rows)[None, :] < lengths[:, None])
    bias = jnp.where(seen, 0.0, NEG).astype(jnp.float32)
    cores = groups // 2
    suffix = functools.partial(suffix_attend, jnp.stack([host]), gathered, swapped, suffix_kv, bias)
    early = max(1, heads - 1)
    parts = suffix(0, early, None)
    far, other_near, parts = lax.optimization_barrier((swap(near, "hst", 1), swap(near, "grp", cores), parts))
    other_far = swap(far, "grp", cores)
    held = {0: [near, far], cores: [other_near, other_far]}
    by_core = [[swap(x, "grp", k) for x in (near, far, other_near)] for k in range(1, cores)]
    if heads > early:
        parts = suffix(early, heads - early, parts)
    by_core, parts = lax.optimization_barrier((by_core, parts))
    parts = parts.astype(jnp.float16)
    held[0], other_far = after((held[0], other_far), parts)
    coded = lax.all_to_all(parts, "hst", split_axis=0, concat_axis=0, tiled=True)

    def context(k, before):
        at = jnp.stack([host * groups + group, group ^ k, host % 2])
        return context_attend(at, lengths, queries, keys_values, bias, *held[k], before)

    context_out = context(0, None)
    other_far = after(other_far, context_out)
    for k in range(1, cores):
        held[k] = by_core[k - 1][:2]
        held[cores ^ k] = [by_core[k - 1][2], swap(other_far, "grp", k)]
    for k in range(1, groups):
        context_out = context(k, context_out)
    return (context_out, combine(coded.astype(jnp.float32)))


def solution(mesh):
    return jax.shard_map(
        per_device,
        mesh=mesh,
        in_specs=(
            P(("hst", "grp"), None),
            P(None, ("hst", "grp"), None),
            P(),
            P(),
            P("hst", "grp"),
            P(None, "hst", "grp"),
        ),
        out_specs=(P(("hst", "grp"), None), P("hst", "grp")),
        check_vma=False,
    )
```

```python
import functools
import math

import jax
import jax.numpy as jnp
from jax import lax
from jax.experimental import pallas as pl
from jax.experimental.pallas import tpu as pltpu
from jax.sharding import PartitionSpec as P

HSZ = 128
NAMB = 512
NEG = -1e30
FLOOR = -2000.0
EXTRA = 8
TILE = 256
C2 = math.log2(math.e) / math.sqrt(HSZ)
BOTH = ("hst", "grp")


def dot_t(a, b):
    return lax.dot_general(a, b, (((1,), (1,)), ((), ())), preferred_element_type=jnp.float32)


def dot(a, b):
    return lax.dot_general(a, b, (((1,), (0,)), ((), ())), preferred_element_type=jnp.float32)


def softmax(scores):
    top = functools.reduce(jnp.maximum, [jnp.max(s, axis=-1, keepdims=True) for s in scores])
    base = top * C2
    weights = [jnp.exp2(s * C2 - base) for s in scores]
    total = functools.reduce(jnp.add, [jnp.sum(w, axis=-1, keepdims=True) for w in weights])
    return base, total, [w.astype(jnp.bfloat16) for w in weights]


def pack_kernel(kv_ref, out_ref, below_ref, *refs):
    across_refs, diagonal_refs, (held, came, left) = refs[0:2], refs[2:4], refs[4:]
    groups, _, rows, part = out_ref.shape
    few, wide, pieces = rows // 4, groups * part // 2, [(s, i) for s in range(2) for i in range(4)]
    arrive = {}
    for s, i in pieces:
        band = pl.ds(i * few, few)
        arrive[s, i] = pltpu.make_async_copy(kv_ref.at[s, band], held.at[s, band], came.at[s, i])
        arrive[s, i].start()
    leave = []
    for s, i in pieces:
        arrive[s, i].wait()
        band, place = pl.ds(i * few, few), pl.ds(i % 2 * few, few)
        right = held.at[s, band, pl.ds(wide, wide)]
        moves = [(right, (across_refs if i < 2 else diagonal_refs)[s].at[place])]
        if i >= 2:
            moves.append((held.at[s, band, pl.ds(0, wide)], below_ref.at[s, place]))
        moves += [(held.at[s, band, pl.ds(g * part, part)], out_ref.at[g, s, band]) for g in range(groups)]
        for n, (source, target) in enumerate(moves):
            leave.append(pltpu.make_async_copy(source, target, left.at[s, i, n]))
            leave[-1].start()
    for copy in leave:
        copy.wait()


def pack(kv, groups):
    _, rows, width = kv.shape
    anywhere = pl.BlockSpec(memory_space=pl.ANY)
    half = jax.ShapeDtypeStruct((rows // 2, width // 2), kv.dtype)
    out, below, *others = pl.pallas_call(
        pack_kernel,
        in_specs=[anywhere],
        out_specs=[anywhere] * 6,
        out_shape=[
            jax.ShapeDtypeStruct((groups, 2, rows, width // groups), kv.dtype),
            jax.ShapeDtypeStruct((2, rows // 2, width // 2), kv.dtype),
        ]
        + [half] * 4,
        scratch_shapes=[
            pltpu.VMEM(kv.shape, kv.dtype),
            pltpu.SemaphoreType.DMA((2, 4)),
            pltpu.SemaphoreType.DMA((2, 4, groups + 2)),
        ],
        cost_estimate=pl.CostEstimate(flops=0, bytes_accessed=6 * kv.size, transcendentals=0),
        name="pack_heads",
    )(kv)
    return out, below, others[:2], others[2:]


def pipelined(tasks, score, finish):
    ahead = score(tasks[0])
    for n, task in enumerate(tasks):
        scores = ahead
        if n + 1 < len(tasks):
            ahead = score(tasks[n + 1])
        finish(task, scores)


def suffix_kernel(at_ref, near_ref, far_ref, kv_ref, sk_ref, bias_ref, out_ref):
    host = at_ref[0]
    groups = kv_ref.shape[0]
    half, share, _ = near_ref.shape
    hosts = 2 * half
    chunk = lambda n: near_ref[n] if n < half else far_ref[n - half]
    apart = list(range(0, hosts, 2)) + list(range(1, hosts, 2))
    chunks = min(hosts, max(1, TILE // share))
    bias = [bias_ref[pl.ds(host * groups + g, 1), :] for g in range(groups)]
    values = [kv_ref[g, 1] for g in range(groups)] + [sk_ref[1]]

    def score(first):
        q = jnp.concatenate([chunk(first + c) for c in range(chunks)], axis=0)
        s = dot_t(q, sk_ref[0])
        row = lax.broadcasted_iota(jnp.int32, (share, share), 0)
        spos = host * share + lax.broadcasted_iota(jnp.int32, (share, share), 1)
        late = []
        for c in range(chunks):
            qpos = jnp.bitwise_xor(host, apart[first + c]) * share + row
            late.append(jnp.where(spos <= qpos, s[c * share : (c + 1) * share], NEG))
        return [dot_t(q, kv_ref[g, 0]) + bias[g] for g in range(groups)] + [jnp.concatenate(late, axis=0)]

    def finish(first, scores):
        base, total, weights = softmax(scores)
        mixed = functools.reduce(jnp.add, [dot(w, v) for w, v in zip(weights, values)])
        n = mixed / total
        size = jnp.max(jnp.abs(n), axis=-1, keepdims=True)
        shift = jnp.clip(jnp.floor(jnp.log2(size)), -100.0, 100.0)
        level = jnp.maximum(base + jnp.log2(total), FLOOR)
        whole = jnp.floor(level)
        rest = jnp.exp2(level - whole)
        coarse = jnp.round(rest * 512.0) * (1.0 / 512.0)
        fine = (rest - coarse) * 1024.0
        lane = lax.broadcasted_iota(jnp.int32, (chunks * share, HSZ), 1)
        stats = jnp.where(lane == 0, whole, jnp.where(lane == 1, coarse, jnp.where(lane == 2, fine, shift)))
        turned = stats.T
        n = n * jnp.exp2(-shift)
        for c in range(chunks):
            to = jnp.bitwise_xor(host, apart[first + c])
            out_ref[to, :share, :] = n[c * share : (c + 1) * share]
            out_ref[to, share : share + EXTRA, :share] = turned[:EXTRA, c * share : (c + 1) * share]

    pipelined(list(range(0, hosts, chunks)), score, finish)


def suffix_attend(host, near, far, kv, sk, bias):
    half, share, width = near.shape
    hosts, heads = 2 * half, width // HSZ
    groups, _, rows, _ = kv.shape
    seen = groups * rows + share
    column = lambda h, at: (0, 0, h)
    return pl.pallas_call(
        suffix_kernel,
        grid_spec=pltpu.PrefetchScalarGridSpec(
            num_scalar_prefetch=1,
            grid=(heads,),
            in_specs=[
                pl.BlockSpec((half, share, HSZ), column),
                pl.BlockSpec((half, share, HSZ), column),
                pl.BlockSpec((groups, 2, rows, HSZ), lambda h, at: (0, 0, 0, h)),
                pl.BlockSpec((2, share, HSZ), column),
                pl.BlockSpec(bias.shape, lambda h, at: (0, 0)),
            ],
            out_specs=pl.BlockSpec((hosts, share + EXTRA, HSZ), column),
        ),
        out_shape=jax.ShapeDtypeStruct((hosts, share + EXTRA, width), jnp.float32),
        compiler_params=pltpu.CompilerParams(vmem_limit_bytes=24 * 1024 * 1024),
        cost_estimate=pl.CostEstimate(
            flops=8 * hosts * share * seen * width,
            bytes_accessed=4 * (groups * rows + 3 * hosts * share) * width,
            transcendentals=heads * hosts * share * seen,
        ),
        name="suffix_attend",
    )(host, near, far, kv, sk, bias)


def combine_kernel(in_ref, out_ref):
    hosts, tall, _ = in_ref.shape
    share = tall - EXTRA
    whole, coarse, fine, shift = [in_ref[:, share + k, :] for k in range(4)]
    weight = jnp.exp2(whole - jnp.max(whole, axis=0, keepdims=True)) * (coarse + fine * (1.0 / 1024.0))
    factor = weight * jnp.exp2(shift) / jnp.sum(weight, axis=0, keepdims=True)
    factor = jnp.concatenate([factor, jnp.zeros((HSZ - hosts, HSZ), jnp.float32)], axis=0).T[:share, :]
    mixed = 0.0
    for g in range(hosts):
        mixed = mixed + factor[:, g : g + 1] * in_ref[g, :share, :]
    out_ref[...] = mixed.astype(out_ref.dtype)


def combine(parts):
    hosts, tall, width = parts.shape
    return pl.pallas_call(
        combine_kernel,
        grid=(width // HSZ,),
        in_specs=[pl.BlockSpec((hosts, tall, HSZ), lambda h: (0, 0, h))],
        out_specs=pl.BlockSpec((tall - EXTRA, HSZ), lambda h: (0, h)),
        out_shape=jax.ShapeDtypeStruct((tall - EXTRA, width), jnp.bfloat16),
        cost_estimate=pl.CostEstimate(flops=2 * parts.size, bytes_accessed=4 * parts.size, transcendentals=0),
        name="combine_groups",
    )(parts)


def context_kernel(at_ref, len_ref, q_ref, kv_ref, bias_ref, near_ref, far_ref, *rest):
    out_ref, diag_ref = rest[-2:]
    block, odd = at_ref[0], at_ref[2]
    rows, width = q_ref.shape
    half = rows // 2
    own = bias_ref[pl.ds(block, 1), :]
    row = lax.broadcasted_iota(jnp.int32, (half, half), 0)
    col = lax.broadcasted_iota(jnp.int32, (half, half), 1)
    for t in range(2):
        ok = own[:, t * half : (t + 1) * half]
        diag_ref[t] = jnp.where(col == row, 0.0, jnp.where(col < row, ok, NEG))
    low, high = bias_ref[0:1, :half], bias_ref[0:1, half:]
    near_bias = jnp.where(block > 0, jnp.where(odd == 0, low, high), NEG)
    far_bias = jnp.where(block > 0, jnp.where(odd == 0, high, low), NEG)

    def score(task):
        first, t = task
        head = slice(first, first + HSZ)
        q = q_ref[t * half : (t + 1) * half, head]
        scores = [dot_t(q, near_ref[0, :, head]) + near_bias, dot_t(q, far_ref[0, :, head]) + far_bias]
        if t == 1:
            scores.append(dot_t(q, kv_ref[0, :half, head]) + own[:, :half])
        scores.append(dot_t(q, kv_ref[0, t * half : (t + 1) * half, head]) + diag_ref[t])
        return scores

    def finish(task, scores):
        first, t = task
        head = slice(first, first + HSZ)
        _, total, weights = softmax(scores)
        values = [near_ref[1, :, head], far_ref[1, :, head]]
        values += [kv_ref[1, u * half : (u + 1) * half, head] for u in range(t + 1)]
        mixed = functools.reduce(jnp.add, [dot(w, v) for w, v in zip(weights, values)])
        place = t * half + lax.broadcasted_iota(jnp.int32, mixed.shape, 0)
        out = jnp.where(place < len_ref[block], mixed / total, 0.0)
        out_ref[t * half : (t + 1) * half, head] = out.astype(out_ref.dtype)

    pipelined([(first, t) for first in range(0, width, HSZ) for t in range(2)], score, finish)


def context_attend(at, lengths, q, kv, bias, near, far, before):
    rows, width = q.shape
    _, half, wide = near.shape
    heads = wide // HSZ
    both = lambda i, at, n: (0, 0, at[1])
    more = [] if before is None else [before]
    return pl.pallas_call(
        context_kernel,
        grid_spec=pltpu.PrefetchScalarGridSpec(
            num_scalar_prefetch=2,
            grid=(1,),
            in_specs=[
                pl.BlockSpec((rows, wide), lambda i, at, n: (0, at[1])),
                pl.BlockSpec((2, rows, wide), both),
                pl.BlockSpec(bias.shape, lambda i, *_: (0, 0)),
                pl.BlockSpec((2, half, wide), lambda i, *_: (0, 0, 0)),
                pl.BlockSpec((2, half, wide), lambda i, *_: (0, 0, 0)),
            ]
            + [pl.BlockSpec(memory_space=pl.ANY) for _ in more],
            out_specs=pl.BlockSpec((rows, wide), lambda i, at, n: (0, at[1])),
            scratch_shapes=[pltpu.VMEM((2, half, half), jnp.float32)],
        ),
        out_shape=jax.ShapeDtypeStruct((rows, width), q.dtype),
        input_output_aliases={7: 0} if more else {},
        compiler_params=pltpu.CompilerParams(vmem_limit_bytes=24 * 1024 * 1024),
        cost_estimate=pl.CostEstimate(
            flops=8 * rows * rows * wide,
            bytes_accessed=12 * rows * wide,
            transcendentals=2 * rows * rows * heads,
        ),
        name="context_attend",
    )(at, lengths, q, kv, bias, near, far, *more)


def swap(x, axis, k):
    return lax.ppermute(x, axis, [(i, i ^ k) for i in range(lax.axis_size(axis))])


def gather_hosts(x, hosts):
    near = jnp.stack([x] + [swap(x, "hst", k) for k in range(2, hosts, 2)], axis=0)
    return near, swap(near, "hst", 1)


def after(x, done):
    return lax.optimization_barrier((x, done))[0]


def scatter_anchor(kv, across, diagonal, below, groups):
    cores = groups // 2
    first = (lax.axis_index("hst") == 0) & (lax.axis_index("grp") == 0)
    send = lambda x, to: lax.ppermute(x, BOTH, [(0, to)])
    down = send(below, groups)
    _, rows, width = kv.shape
    slabs = []
    for s in range(2):
        slab = jnp.where(first, kv[s, : rows // 2, : width // 2], 0.0) + send(diagonal[s], groups + cores) + send(across[s], cores)
        slabs.append(slab + (after(down[s], slabs[0]) if s else down[s]))
    return slabs


def spread_anchor(slab, hosts, groups):
    cores = groups // 2
    wide = slab.shape[1] // cores
    piece = slab[:, :wide]
    for c in range(1, cores):
        pairs = [(x, x + c) for x in (0, cores)]
        piece = piece + lax.ppermute(slab[:, c * wide : (c + 1) * wide], "grp", pairs)
    far = hosts // 2
    while far >= 2:
        pairs = [(h, h + far) for h in range(hosts) if h % (2 * far) < 2]
        piece = piece + lax.ppermute(piece, "hst", pairs)
        far //= 2
    return piece


def per_device(queries, keys_values, token_ids, lengths, suffix_queries, suffix_kv):
    hosts, groups = lax.axis_size("hst"), lax.axis_size("grp")
    host, group = lax.axis_index("hst"), lax.axis_index("grp")
    rows = queries.shape[0]
    cores = groups // 2
    packed, below, across, diagonal = pack(keys_values, groups)
    slabs = scatter_anchor(keys_values, across, diagonal, below, groups)
    packed, suffix_queries = after((packed, suffix_queries), slabs[0])
    swapped = lax.all_to_all(packed, "grp", split_axis=0, concat_axis=0, tiled=True)
    near = jnp.stack([spread_anchor(x, hosts, groups) for x in slabs])
    gathered = gather_hosts(suffix_queries, hosts)
    seen = (token_ids.reshape(-1, rows) >= NAMB) & (jnp.arange(rows)[None, :] < lengths[:, None])
    bias = jnp.where(seen, 0.0, NEG).astype(jnp.float32)
    far, other_near, gathered = lax.optimization_barrier((swap(near, "hst", 1), swap(near, "grp", cores), gathered))
    other_far = swap(far, "grp", cores)
    by_core = [[swap(x, "grp", k) for x in (near, far, other_near)] for k in range(1, cores)]
    parts = suffix_attend(jnp.stack([host]), *gathered, swapped, suffix_kv, bias)
    other_far, by_core, parts = lax.optimization_barrier((other_far, by_core, parts))
    parts = parts.astype(jnp.float16)
    coded = lax.all_to_all(parts, "hst", split_axis=0, concat_axis=0, tiled=True)
    held = {0: after([near, far], parts), cores: [other_near, other_far]}

    def context(k, before):
        at = jnp.stack([host * groups + group, group ^ k, host % 2])
        return context_attend(at, lengths, queries, keys_values, bias, *held[k], before)

    context_out = context(0, None)
    for k in range(1, cores):
        held[k] = by_core[k - 1][:2]
        held[cores ^ k] = [by_core[k - 1][2], swap(other_far, "grp", k)]
    for k in range(1, groups):
        context_out = context(k, context_out)
    return (context_out, combine(coded.astype(jnp.float32)))


def solution(mesh):
    return jax.shard_map(
        per_device,
        mesh=mesh,
        in_specs=(
            P(("hst", "grp"), None),
            P(None, ("hst", "grp"), None),
            P(),
            P(),
            P("hst", "grp"),
            P(None, "hst", "grp"),
        ),
        out_specs=(P(("hst", "grp"), None), P("hst", "grp")),
        check_vma=False,
    )
```

```python
import functools
import math

import jax
import jax.numpy as jnp
from jax import lax
from jax.experimental import pallas as pl
from jax.experimental.pallas import tpu as pltpu
from jax.sharding import PartitionSpec as P

HSZ = 128
NAMB = 512
NEG = -1e30
FLOOR = -2000.0
EXTRA = 8
TILE = 256
C2 = math.log2(math.e) / math.sqrt(HSZ)
BOTH = ("hst", "grp")


def dot_t(a, b):
    return lax.dot_general(a, b, (((1,), (1,)), ((), ())), preferred_element_type=jnp.float32)


def dot(a, b):
    return lax.dot_general(a, b, (((1,), (0,)), ((), ())), preferred_element_type=jnp.float32)


def softmax(scores):
    top = functools.reduce(jnp.maximum, [jnp.max(s, axis=-1, keepdims=True) for s in scores])
    base = top * C2
    weights = [jnp.exp2(s * C2 - base) for s in scores]
    total = functools.reduce(jnp.add, [jnp.sum(w, axis=-1, keepdims=True) for w in weights])
    return base, total, [w.astype(jnp.bfloat16) for w in weights]


def pack_kernel(kv_ref, out_ref, below_ref, *refs):
    across_refs, diagonal_refs, (held, came, left) = refs[0:2], refs[2:4], refs[4:]
    groups, _, rows, part = out_ref.shape
    few, wide, pieces = rows // 4, groups * part // 2, [(s, i) for s in range(2) for i in range(4)]
    arrive = {}
    for s, i in pieces:
        band = pl.ds(i * few, few)
        arrive[s, i] = pltpu.make_async_copy(kv_ref.at[s, band], held.at[s, band], came.at[s, i])
        arrive[s, i].start()
    leave = []
    for s, i in pieces:
        arrive[s, i].wait()
        band, place = pl.ds(i * few, few), pl.ds(i % 2 * few, few)
        right = held.at[s, band, pl.ds(wide, wide)]
        moves = [(right, (across_refs if i < 2 else diagonal_refs)[s].at[place])]
        if i >= 2:
            moves.append((held.at[s, band, pl.ds(0, wide)], below_ref.at[s, place]))
        moves += [(held.at[s, band, pl.ds(g * part, part)], out_ref.at[g, s, band]) for g in range(groups)]
        for n, (source, target) in enumerate(moves):
            leave.append(pltpu.make_async_copy(source, target, left.at[s, i, n]))
            leave[-1].start()
    for copy in leave:
        copy.wait()


def pack(kv, groups):
    _, rows, width = kv.shape
    anywhere = pl.BlockSpec(memory_space=pl.ANY)
    half = jax.ShapeDtypeStruct((rows // 2, width // 2), kv.dtype)
    out, below, *others = pl.pallas_call(
        pack_kernel,
        in_specs=[anywhere],
        out_specs=[anywhere] * 6,
        out_shape=[
            jax.ShapeDtypeStruct((groups, 2, rows, width // groups), kv.dtype),
            jax.ShapeDtypeStruct((2, rows // 2, width // 2), kv.dtype),
        ]
        + [half] * 4,
        scratch_shapes=[
            pltpu.VMEM(kv.shape, kv.dtype),
            pltpu.SemaphoreType.DMA((2, 4)),
            pltpu.SemaphoreType.DMA((2, 4, groups + 2)),
        ],
        cost_estimate=pl.CostEstimate(flops=0, bytes_accessed=6 * kv.size, transcendentals=0),
        name="pack_heads",
    )(kv)
    return out, below, others[:2], others[2:]


def pipelined(tasks, score, finish):
    ahead = score(tasks[0])
    for n, task in enumerate(tasks):
        scores = ahead
        if n + 1 < len(tasks):
            ahead = score(tasks[n + 1])
        finish(task, scores)


def suffix_kernel(at_ref, near_ref, far_ref, kv_ref, sk_ref, bias_ref, *rest):
    out_ref = rest[-1]
    host = at_ref[0]
    groups = kv_ref.shape[0]
    half, share, _ = near_ref.shape
    hosts = 2 * half
    chunk = lambda n: near_ref[n] if n < half else far_ref[n - half]
    apart = list(range(0, hosts, 2)) + list(range(1, hosts, 2))
    chunks = min(hosts, max(1, TILE // share))
    bias = [bias_ref[pl.ds(host * groups + g, 1), :] for g in range(groups)]
    values = [kv_ref[g, 1] for g in range(groups)] + [sk_ref[1]]

    def score(first):
        q = jnp.concatenate([chunk(first + c) for c in range(chunks)], axis=0)
        s = dot_t(q, sk_ref[0])
        row = lax.broadcasted_iota(jnp.int32, (share, share), 0)
        spos = host * share + lax.broadcasted_iota(jnp.int32, (share, share), 1)
        late = []
        for c in range(chunks):
            qpos = jnp.bitwise_xor(host, apart[first + c]) * share + row
            late.append(jnp.where(spos <= qpos, s[c * share : (c + 1) * share], NEG))
        return [dot_t(q, kv_ref[g, 0]) + bias[g] for g in range(groups)] + [jnp.concatenate(late, axis=0)]

    def finish(first, scores):
        base, total, weights = softmax(scores)
        mixed = functools.reduce(jnp.add, [dot(w, v) for w, v in zip(weights, values)])
        n = mixed / total
        size = jnp.max(jnp.abs(n), axis=-1, keepdims=True)
        shift = jnp.clip(jnp.floor(jnp.log2(size)), -100.0, 100.0)
        level = jnp.maximum(base + jnp.log2(total), FLOOR)
        whole = jnp.floor(level)
        rest = jnp.exp2(level - whole)
        coarse = jnp.round(rest * 512.0) * (1.0 / 512.0)
        fine = (rest - coarse) * 1024.0
        lane = lax.broadcasted_iota(jnp.int32, (chunks * share, HSZ), 1)
        stats = jnp.where(lane == 0, whole, jnp.where(lane == 1, coarse, jnp.where(lane == 2, fine, shift)))
        turned = stats.T
        n = n * jnp.exp2(-shift)
        for c in range(chunks):
            to = jnp.bitwise_xor(host, apart[first + c])
            out_ref[to, :share, :] = n[c * share : (c + 1) * share]
            out_ref[to, share : share + EXTRA, :share] = turned[:EXTRA, c * share : (c + 1) * share]

    pipelined(list(range(0, hosts, chunks)), score, finish)


def suffix_attend(host, near, far, kv, sk, bias, first, count, before):
    half, share, width = near.shape
    hosts = 2 * half
    more = [] if before is None else [before]
    groups, _, rows, _ = kv.shape
    seen = groups * rows + share
    column = lambda h, at: (0, 0, first + h)
    return pl.pallas_call(
        suffix_kernel,
        grid_spec=pltpu.PrefetchScalarGridSpec(
            num_scalar_prefetch=1,
            grid=(count,),
            in_specs=[
                pl.BlockSpec((half, share, HSZ), column),
                pl.BlockSpec((half, share, HSZ), column),
                pl.BlockSpec((groups, 2, rows, HSZ), lambda h, at: (0, 0, 0, first + h)),
                pl.BlockSpec((2, share, HSZ), column),
                pl.BlockSpec(bias.shape, lambda h, at: (0, 0)),
            ]
            + [pl.BlockSpec(memory_space=pl.ANY) for _ in more],
            out_specs=pl.BlockSpec((hosts, share + EXTRA, HSZ), column),
        ),
        out_shape=jax.ShapeDtypeStruct((hosts, share + EXTRA, width), jnp.float32),
        input_output_aliases={6: 0} if more else {},
        compiler_params=pltpu.CompilerParams(vmem_limit_bytes=24 * 1024 * 1024),
        cost_estimate=pl.CostEstimate(
            flops=8 * count * hosts * share * seen * HSZ,
            bytes_accessed=4 * count * (groups * rows + 3 * hosts * share) * HSZ,
            transcendentals=count * hosts * share * seen,
        ),
        name="suffix_attend",
    )(host, near, far, kv, sk, bias, *more)


def combine_kernel(in_ref, out_ref):
    hosts, tall, width = in_ref.shape
    share = tall - EXTRA
    for first in range(0, width, HSZ):
        head = slice(first, first + HSZ)
        whole, coarse, fine, shift = [in_ref[:, share + k, head] for k in range(4)]
        weight = jnp.exp2(whole - jnp.max(whole, axis=0, keepdims=True)) * (coarse + fine * (1.0 / 1024.0))
        factor = weight * jnp.exp2(shift) / jnp.sum(weight, axis=0, keepdims=True)
        factor = jnp.concatenate([factor, jnp.zeros((HSZ - hosts, HSZ), jnp.float32)], axis=0).T[:share, :]
        mixed = 0.0
        for g in range(hosts):
            mixed = mixed + factor[:, g : g + 1] * in_ref[g, :share, head]
        out_ref[:, head] = mixed.astype(out_ref.dtype)


def combine(parts):
    _, tall, width = parts.shape
    return pl.pallas_call(
        combine_kernel,
        in_specs=[pl.BlockSpec(memory_space=pltpu.VMEM)],
        out_specs=pl.BlockSpec(memory_space=pltpu.VMEM),
        out_shape=jax.ShapeDtypeStruct((tall - EXTRA, width), jnp.bfloat16),
        cost_estimate=pl.CostEstimate(flops=2 * parts.size, bytes_accessed=4 * parts.size, transcendentals=0),
        name="combine_groups",
    )(parts)


def context_kernel(at_ref, len_ref, q_ref, kv_ref, bias_ref, near_ref, far_ref, *rest):
    out_ref, diag_ref = rest[-2:]
    block, odd = at_ref[0], at_ref[2]
    rows, width = q_ref.shape
    half = rows // 2
    own = bias_ref[pl.ds(block, 1), :]
    row = lax.broadcasted_iota(jnp.int32, (half, half), 0)
    col = lax.broadcasted_iota(jnp.int32, (half, half), 1)
    for t in range(2):
        ok = own[:, t * half : (t + 1) * half]
        diag_ref[t] = jnp.where(col == row, 0.0, jnp.where(col < row, ok, NEG))
    low, high = bias_ref[0:1, :half], bias_ref[0:1, half:]
    near_bias = jnp.where(block > 0, jnp.where(odd == 0, low, high), NEG)
    far_bias = jnp.where(block > 0, jnp.where(odd == 0, high, low), NEG)

    def score(task):
        first, t = task
        head = slice(first, first + HSZ)
        q = q_ref[t * half : (t + 1) * half, head]
        scores = [dot_t(q, near_ref[0, :, head]) + near_bias, dot_t(q, far_ref[0, :, head]) + far_bias]
        if t == 1:
            scores.append(dot_t(q, kv_ref[0, :half, head]) + own[:, :half])
        scores.append(dot_t(q, kv_ref[0, t * half : (t + 1) * half, head]) + diag_ref[t])
        return scores

    def finish(task, scores):
        first, t = task
        head = slice(first, first + HSZ)
        _, total, weights = softmax(scores)
        values = [near_ref[1, :, head], far_ref[1, :, head]]
        values += [kv_ref[1, u * half : (u + 1) * half, head] for u in range(t + 1)]
        mixed = functools.reduce(jnp.add, [dot(w, v) for w, v in zip(weights, values)])
        place = t * half + lax.broadcasted_iota(jnp.int32, mixed.shape, 0)
        out = jnp.where(place < len_ref[block], mixed / total, 0.0)
        out_ref[t * half : (t + 1) * half, head] = out.astype(out_ref.dtype)

    pipelined([(first, t) for first in range(0, width, HSZ) for t in range(2)], score, finish)


def context_attend(at, lengths, q, kv, bias, near, far, before):
    rows, width = q.shape
    _, half, wide = near.shape
    heads = wide // HSZ
    both = lambda i, at, n: (0, 0, at[1])
    more = [] if before is None else [before]
    return pl.pallas_call(
        context_kernel,
        grid_spec=pltpu.PrefetchScalarGridSpec(
            num_scalar_prefetch=2,
            grid=(1,),
            in_specs=[
                pl.BlockSpec((rows, wide), lambda i, at, n: (0, at[1])),
                pl.BlockSpec((2, rows, wide), both),
                pl.BlockSpec(bias.shape, lambda i, *_: (0, 0)),
                pl.BlockSpec((2, half, wide), lambda i, *_: (0, 0, 0)),
                pl.BlockSpec((2, half, wide), lambda i, *_: (0, 0, 0)),
            ]
            + [pl.BlockSpec(memory_space=pl.ANY) for _ in more],
            out_specs=pl.BlockSpec((rows, wide), lambda i, at, n: (0, at[1])),
            scratch_shapes=[pltpu.VMEM((2, half, half), jnp.float32)],
        ),
        out_shape=jax.ShapeDtypeStruct((rows, width), q.dtype),
        input_output_aliases={7: 0} if more else {},
        compiler_params=pltpu.CompilerParams(vmem_limit_bytes=24 * 1024 * 1024),
        cost_estimate=pl.CostEstimate(
            flops=8 * rows * rows * wide,
            bytes_accessed=12 * rows * wide,
            transcendentals=2 * rows * rows * heads,
        ),
        name="context_attend",
    )(at, lengths, q, kv, bias, near, far, *more)


def swap(x, axis, k):
    return lax.ppermute(x, axis, [(i, i ^ k) for i in range(lax.axis_size(axis))])


def gather_hosts(x, hosts):
    near = jnp.stack([x] + [swap(x, "hst", k) for k in range(2, hosts, 2)], axis=0)
    return near, swap(near, "hst", 1)


def after(x, done):
    return lax.optimization_barrier((x, done))[0]


def scatter_anchor(kv, across, diagonal, below, groups):
    cores = groups // 2
    first = (lax.axis_index("hst") == 0) & (lax.axis_index("grp") == 0)
    send = lambda x, to: lax.ppermute(x, BOTH, [(0, to)])
    down = send(below, groups)
    _, rows, width = kv.shape
    slabs = []
    for s in range(2):
        slab = jnp.where(first, kv[s, : rows // 2, : width // 2], 0.0) + send(diagonal[s], groups + cores) + send(across[s], cores)
        slabs.append(slab + (after(down[s], slabs[0]) if s else down[s]))
    return slabs, down


def spread_anchor(slab, hosts, groups):
    cores = groups // 2
    wide = slab.shape[1] // cores
    piece = slab[:, :wide]
    for c in range(1, cores):
        pairs = [(x, x + c) for x in (0, cores)]
        piece = piece + lax.ppermute(slab[:, c * wide : (c + 1) * wide], "grp", pairs)
    far = hosts // 2
    while far >= 2:
        pairs = [(h, h + far) for h in range(hosts) if h % (2 * far) < 2]
        piece = piece + lax.ppermute(piece, "hst", pairs)
        far //= 2
    return piece


def per_device(queries, keys_values, token_ids, lengths, suffix_queries, suffix_kv):
    hosts, groups = lax.axis_size("hst"), lax.axis_size("grp")
    host, group = lax.axis_index("hst"), lax.axis_index("grp")
    rows = queries.shape[0]
    cores = groups // 2
    packed, below, across, diagonal = pack(keys_values, groups)
    slabs, down = scatter_anchor(keys_values, across, diagonal, below, groups)
    swapped = lax.all_to_all(after(packed, down), "grp", split_axis=0, concat_axis=0, tiled=True)
    near = jnp.stack([spread_anchor(x, hosts, groups) for x in slabs])
    gathered = gather_hosts(after(suffix_queries, slabs[1]), hosts)
    seen = (token_ids.reshape(-1, rows) >= NAMB) & (jnp.arange(rows)[None, :] < lengths[:, None])
    bias = jnp.where(seen, 0.0, NEG).astype(jnp.float32)
    suffix = functools.partial(suffix_attend, jnp.stack([host]), *gathered, swapped, suffix_kv, bias)
    heads = suffix_queries.shape[1] // HSZ
    early = max(1, heads - 1)
    far, other_near = swap(near, "hst", 1), swap(after(near, swapped), "grp", cores)
    far, other_near, parts = lax.optimization_barrier((far, other_near, suffix(0, early, None)))
    other_far = swap(far, "grp", cores)
    by_core = [[swap(x, "grp", k) for x in (near, far)] for k in range(1, cores)]
    if heads > early:
        parts = suffix(early, heads - early, parts)
    by_core, parts = lax.optimization_barrier((by_core, parts))
    parts = parts.astype(jnp.float16)
    coded = lax.all_to_all(parts, "hst", split_axis=0, concat_axis=0, tiled=True)
    held = {0: after([near, far], parts), cores: [other_near, other_far]}

    def context(k, before):
        at = jnp.stack([host * groups + group, group ^ k, host % 2])
        return context_attend(at, lengths, queries, keys_values, bias, *held[k], before)

    context_out = context(0, None)
    for k in range(1, cores):
        held[k] = by_core[k - 1]
        context_out = context(k, context_out)
    other = after(held[cores], context_out)
    for k in range(1, cores):
        held[cores ^ k] = [swap(x, "grp", k) for x in other]
    for k in range(cores, groups):
        context_out = context(k, context_out)
    return (context_out, combine(coded.astype(jnp.float32)))


def solution(mesh):
    return jax.shard_map(
        per_device,
        mesh=mesh,
        in_specs=(
            P(("hst", "grp"), None),
            P(None, ("hst", "grp"), None),
            P(),
            P(),
            P("hst", "grp"),
            P(None, "hst", "grp"),
        ),
        out_specs=(P(("hst", "grp"), None), P("hst", "grp")),
        check_vma=False,
    )
```

```python
import functools
import math

import jax
import jax.numpy as jnp
from jax import lax
from jax.experimental import pallas as pl
from jax.experimental.pallas import tpu as pltpu
from jax.sharding import PartitionSpec as P

HSZ = 128
NAMB = 512
NEG = -1e30
FLOOR = -2000.0
EXTRA = 8
TILE = 256
C2 = math.log2(math.e) / math.sqrt(HSZ)
BOTH = ("hst", "grp")


def dot_t(a, b):
    return lax.dot_general(a, b, (((1,), (1,)), ((), ())), preferred_element_type=jnp.float32)


def dot(a, b):
    return lax.dot_general(a, b, (((1,), (0,)), ((), ())), preferred_element_type=jnp.float32)


def softmax(scores):
    top = functools.reduce(jnp.maximum, [jnp.max(s, axis=-1, keepdims=True) for s in scores])
    base = top * C2
    weights = [jnp.exp2(s * C2 - base) for s in scores]
    total = functools.reduce(jnp.add, [jnp.sum(w, axis=-1, keepdims=True) for w in weights])
    return base, total, [w.astype(jnp.bfloat16) for w in weights]


def pack_kernel(kv_ref, out_ref, below_ref, *refs):
    across_refs, diagonal_refs, (held, came, left) = refs[0:2], refs[2:4], refs[4:]
    groups, _, rows, part = out_ref.shape
    few, wide, pieces = rows // 4, groups * part // 2, [(s, i) for s in range(2) for i in range(4)]
    arrive = {}
    for s, i in pieces:
        band = pl.ds(i * few, few)
        arrive[s, i] = pltpu.make_async_copy(kv_ref.at[s, band], held.at[s, band], came.at[s, i])
        arrive[s, i].start()
    leave = []
    for s, i in pieces:
        arrive[s, i].wait()
        band, place = pl.ds(i * few, few), pl.ds(i % 2 * few, few)
        right = held.at[s, band, pl.ds(wide, wide)]
        moves = [(right, (across_refs if i < 2 else diagonal_refs)[s].at[place])]
        if i >= 2:
            moves.append((held.at[s, band, pl.ds(0, wide)], below_ref.at[s, place]))
        moves += [(held.at[s, band, pl.ds(g * part, part)], out_ref.at[g, s, band]) for g in range(groups)]
        for n, (source, target) in enumerate(moves):
            leave.append(pltpu.make_async_copy(source, target, left.at[s, i, n]))
            leave[-1].start()
    for copy in leave:
        copy.wait()


def pack(kv, groups):
    _, rows, width = kv.shape
    anywhere = pl.BlockSpec(memory_space=pl.ANY)
    half = jax.ShapeDtypeStruct((rows // 2, width // 2), kv.dtype)
    out, below, *others = pl.pallas_call(
        pack_kernel,
        in_specs=[anywhere],
        out_specs=[anywhere] * 6,
        out_shape=[
            jax.ShapeDtypeStruct((groups, 2, rows, width // groups), kv.dtype),
            jax.ShapeDtypeStruct((2, rows // 2, width // 2), kv.dtype),
        ]
        + [half] * 4,
        scratch_shapes=[
            pltpu.VMEM(kv.shape, kv.dtype),
            pltpu.SemaphoreType.DMA((2, 4)),
            pltpu.SemaphoreType.DMA((2, 4, groups + 2)),
        ],
        cost_estimate=pl.CostEstimate(flops=0, bytes_accessed=6 * kv.size, transcendentals=0),
        name="pack_heads",
    )(kv)
    return out, below, others[:2], others[2:]


def pipelined(tasks, score, finish):
    ahead = score(tasks[0])
    for n, task in enumerate(tasks):
        scores = ahead
        if n + 1 < len(tasks):
            ahead = score(tasks[n + 1])
        finish(task, scores)


def suffix_kernel(at_ref, near_ref, far_ref, kv_ref, sk_ref, bias_ref, *rest):
    out_ref = rest[-1]
    host = at_ref[0]
    groups = kv_ref.shape[0]
    half, share, _ = near_ref.shape
    hosts = 2 * half
    chunk = lambda n: near_ref[n] if n < half else far_ref[n - half]
    apart = list(range(0, hosts, 2)) + list(range(1, hosts, 2))
    chunks = min(hosts, max(1, TILE // share))
    bias = [bias_ref[pl.ds(host * groups + g, 1), :] for g in range(groups)]
    values = [kv_ref[g, 1] for g in range(groups)] + [sk_ref[1]]

    def score(first):
        q = jnp.concatenate([chunk(first + c) for c in range(chunks)], axis=0)
        s = dot_t(q, sk_ref[0])
        row = lax.broadcasted_iota(jnp.int32, (share, share), 0)
        spos = host * share + lax.broadcasted_iota(jnp.int32, (share, share), 1)
        late = []
        for c in range(chunks):
            qpos = jnp.bitwise_xor(host, apart[first + c]) * share + row
            late.append(jnp.where(spos <= qpos, s[c * share : (c + 1) * share], NEG))
        return [dot_t(q, kv_ref[g, 0]) + bias[g] for g in range(groups)] + [jnp.concatenate(late, axis=0)]

    def finish(first, scores):
        base, total, weights = softmax(scores)
        mixed = functools.reduce(jnp.add, [dot(w, v) for w, v in zip(weights, values)])
        n = mixed / total
        size = jnp.max(jnp.abs(n), axis=-1, keepdims=True)
        shift = jnp.clip(jnp.floor(jnp.log2(size)), -100.0, 100.0)
        level = jnp.maximum(base + jnp.log2(total), FLOOR)
        whole = jnp.floor(level)
        rest = jnp.exp2(level - whole)
        coarse = jnp.round(rest * 512.0) * (1.0 / 512.0)
        fine = (rest - coarse) * 1024.0
        lane = lax.broadcasted_iota(jnp.int32, (chunks * share, HSZ), 1)
        stats = jnp.where(lane == 0, whole, jnp.where(lane == 1, coarse, jnp.where(lane == 2, fine, shift)))
        turned = stats.T
        n = n * jnp.exp2(-shift)
        for c in range(chunks):
            to = jnp.bitwise_xor(host, apart[first + c])
            out_ref[to, :share, :] = n[c * share : (c + 1) * share]
            out_ref[to, share : share + EXTRA, :share] = turned[:EXTRA, c * share : (c + 1) * share]

    pipelined(list(range(0, hosts, chunks)), score, finish)


def suffix_attend(host, near, far, kv, sk, bias, first, count, before):
    half, share, width = near.shape
    hosts = 2 * half
    more = [] if before is None else [before]
    groups, _, rows, _ = kv.shape
    seen = groups * rows + share
    column = lambda h, at: (0, 0, first + h)
    return pl.pallas_call(
        suffix_kernel,
        grid_spec=pltpu.PrefetchScalarGridSpec(
            num_scalar_prefetch=1,
            grid=(count,),
            in_specs=[
                pl.BlockSpec((half, share, HSZ), column),
                pl.BlockSpec((half, share, HSZ), column),
                pl.BlockSpec((groups, 2, rows, HSZ), lambda h, at: (0, 0, 0, first + h)),
                pl.BlockSpec((2, share, HSZ), column),
                pl.BlockSpec(bias.shape, lambda h, at: (0, 0)),
            ]
            + [pl.BlockSpec(memory_space=pl.ANY) for _ in more],
            out_specs=pl.BlockSpec((hosts, share + EXTRA, HSZ), column),
        ),
        out_shape=jax.ShapeDtypeStruct((hosts, share + EXTRA, width), jnp.float32),
        input_output_aliases={6: 0} if more else {},
        compiler_params=pltpu.CompilerParams(vmem_limit_bytes=24 * 1024 * 1024),
        cost_estimate=pl.CostEstimate(
            flops=8 * count * hosts * share * seen * HSZ,
            bytes_accessed=4 * count * (groups * rows + 3 * hosts * share) * HSZ,
            transcendentals=count * hosts * share * seen,
        ),
        name="suffix_attend",
    )(host, near, far, kv, sk, bias, *more)


def combine_kernel(in_ref, out_ref):
    hosts, tall, width = in_ref.shape
    share = tall - EXTRA
    for first in range(0, width, HSZ):
        head = slice(first, first + HSZ)
        whole, coarse, fine, shift = [in_ref[:, share + k, head] for k in range(4)]
        weight = jnp.exp2(whole - jnp.max(whole, axis=0, keepdims=True)) * (coarse + fine * (1.0 / 1024.0))
        factor = weight * jnp.exp2(shift) / jnp.sum(weight, axis=0, keepdims=True)
        factor = jnp.concatenate([factor, jnp.zeros((HSZ - hosts, HSZ), jnp.float32)], axis=0).T[:share, :]
        mixed = 0.0
        for g in range(hosts):
            mixed = mixed + factor[:, g : g + 1] * in_ref[g, :share, head]
        out_ref[:, head] = mixed.astype(out_ref.dtype)


def combine(parts):
    _, tall, width = parts.shape
    return pl.pallas_call(
        combine_kernel,
        in_specs=[pl.BlockSpec(memory_space=pltpu.VMEM)],
        out_specs=pl.BlockSpec(memory_space=pltpu.VMEM),
        out_shape=jax.ShapeDtypeStruct((tall - EXTRA, width), jnp.bfloat16),
        cost_estimate=pl.CostEstimate(flops=2 * parts.size, bytes_accessed=4 * parts.size, transcendentals=0),
        name="combine_groups",
    )(parts)


def context_kernel(at_ref, len_ref, bias_ref, *refs):
    sources, (out_ref, diag_ref, *held, came) = refs[:4], refs[-7:]
    q_ref, kv_ref, near_ref, far_ref = held
    block, odd = at_ref[0], at_ref[2]
    rows, width = q_ref.shape
    half = rows // 2
    loads = {}
    for first in range(0, width, HSZ):
        there = pl.ds(pl.multiple_of(at_ref[1] * width, HSZ) + first, HSZ)
        here = pl.ds(first, HSZ)
        places = [(slice(None), there), (slice(None), slice(None), there)] + [(slice(None), slice(None), here)] * 2
        loads[first] = [
            pltpu.make_async_copy(source.at[place], to.at[(*place[:-1], here)], came.at[first // HSZ, n])
            for n, (source, place, to) in enumerate(zip(sources, places, held))
        ]
        for load in loads[first]:
            load.start()
    own = bias_ref[pl.ds(block, 1), :]
    row = lax.broadcasted_iota(jnp.int32, (half, half), 0)
    col = lax.broadcasted_iota(jnp.int32, (half, half), 1)
    for t in range(2):
        ok = own[:, t * half : (t + 1) * half]
        diag_ref[t] = jnp.where(col == row, 0.0, jnp.where(col < row, ok, NEG))
    low, high = bias_ref[0:1, :half], bias_ref[0:1, half:]
    near_bias = jnp.where(block > 0, jnp.where(odd == 0, low, high), NEG)
    far_bias = jnp.where(block > 0, jnp.where(odd == 0, high, low), NEG)

    def score(task):
        first, t = task
        head = slice(first, first + HSZ)
        if t == 0:
            for load in loads[first]:
                load.wait()
        q = q_ref[t * half : (t + 1) * half, head]
        scores = [dot_t(q, near_ref[0, :, head]) + near_bias, dot_t(q, far_ref[0, :, head]) + far_bias]
        if t == 1:
            scores.append(dot_t(q, kv_ref[0, :half, head]) + own[:, :half])
        scores.append(dot_t(q, kv_ref[0, t * half : (t + 1) * half, head]) + diag_ref[t])
        return scores

    def finish(task, scores):
        first, t = task
        head = slice(first, first + HSZ)
        _, total, weights = softmax(scores)
        values = [near_ref[1, :, head], far_ref[1, :, head]]
        values += [kv_ref[1, u * half : (u + 1) * half, head] for u in range(t + 1)]
        mixed = functools.reduce(jnp.add, [dot(w, v) for w, v in zip(weights, values)])
        place = t * half + lax.broadcasted_iota(jnp.int32, mixed.shape, 0)
        out = jnp.where(place < len_ref[block], mixed / total, 0.0)
        out_ref[t * half : (t + 1) * half, head] = out.astype(out_ref.dtype)

    pipelined([(first, t) for first in range(0, width, HSZ) for t in range(2)], score, finish)


def context_attend(at, lengths, q, kv, bias, near, far, before):
    rows, width = q.shape
    _, half, wide = near.shape
    heads = wide // HSZ
    more = [] if before is None else [before]
    anywhere = pl.BlockSpec(memory_space=pl.ANY)
    return pl.pallas_call(
        context_kernel,
        grid_spec=pltpu.PrefetchScalarGridSpec(
            num_scalar_prefetch=2,
            grid=(1,),
            in_specs=[pl.BlockSpec(bias.shape, lambda i, *_: (0, 0))] + [anywhere] * (4 + len(more)),
            out_specs=pl.BlockSpec((rows, wide), lambda i, at, n: (0, at[1])),
            scratch_shapes=[
                pltpu.VMEM((2, half, half), jnp.float32),
                pltpu.VMEM((rows, wide), q.dtype),
                pltpu.VMEM((2, rows, wide), kv.dtype),
                pltpu.VMEM((2, half, wide), near.dtype),
                pltpu.VMEM((2, half, wide), far.dtype),
                pltpu.SemaphoreType.DMA((heads, 4)),
            ],
        ),
        out_shape=jax.ShapeDtypeStruct((rows, width), q.dtype),
        input_output_aliases={7: 0} if more else {},
        compiler_params=pltpu.CompilerParams(vmem_limit_bytes=24 * 1024 * 1024),
        cost_estimate=pl.CostEstimate(
            flops=8 * rows * rows * wide,
            bytes_accessed=12 * rows * wide,
            transcendentals=2 * rows * rows * heads,
        ),
        name="context_attend",
    )(at, lengths, bias, q, kv, near, far, *more)


def swap(x, axis, k):
    return lax.ppermute(x, axis, [(i, i ^ k) for i in range(lax.axis_size(axis))])


def gather_hosts(x, hosts):
    near = jnp.stack([x] + [swap(x, "hst", k) for k in range(2, hosts, 2)], axis=0)
    return near, swap(near, "hst", 1)


def after(x, done):
    return lax.optimization_barrier((x, done))[0]


def scatter_anchor(kv, across, diagonal, below, groups):
    cores = groups // 2
    first = (lax.axis_index("hst") == 0) & (lax.axis_index("grp") == 0)
    send = lambda x, to: lax.ppermute(x, BOTH, [(0, to)])
    down = send(below, groups)
    _, rows, width = kv.shape
    slabs = []
    for s in range(2):
        slab = jnp.where(first, kv[s, : rows // 2, : width // 2], 0.0) + send(diagonal[s], groups + cores) + send(across[s], cores)
        slabs.append(slab + (after(down[s], slabs[0]) if s else down[s]))
    return slabs, down


def spread_anchor(slab, hosts, groups):
    cores = groups // 2
    wide = slab.shape[1] // cores
    piece = slab[:, :wide]
    for c in range(1, cores):
        pairs = [(x, x + c) for x in (0, cores)]
        piece = piece + lax.ppermute(slab[:, c * wide : (c + 1) * wide], "grp", pairs)
    far = hosts // 2
    while far >= 2:
        pairs = [(h, h + far) for h in range(hosts) if h % (2 * far) < 2]
        piece = piece + lax.ppermute(piece, "hst", pairs)
        far //= 2
    return piece


def per_device(queries, keys_values, token_ids, lengths, suffix_queries, suffix_kv):
    hosts, groups = lax.axis_size("hst"), lax.axis_size("grp")
    host, group = lax.axis_index("hst"), lax.axis_index("grp")
    rows = queries.shape[0]
    cores = groups // 2
    packed, below, across, diagonal = pack(keys_values, groups)
    slabs, down = scatter_anchor(keys_values, across, diagonal, below, groups)
    swapped = lax.all_to_all(after(packed, down), "grp", split_axis=0, concat_axis=0, tiled=True)
    near = jnp.stack([spread_anchor(x, hosts, groups) for x in slabs])
    gathered = gather_hosts(after(suffix_queries, slabs[1]), hosts)
    seen = (token_ids.reshape(-1, rows) >= NAMB) & (jnp.arange(rows)[None, :] < lengths[:, None])
    bias = jnp.where(seen, 0.0, NEG).astype(jnp.float32)
    suffix = functools.partial(suffix_attend, jnp.stack([host]), *gathered, swapped, suffix_kv, bias)
    far, other_near = swap(near, "hst", 1), swap(after(near, swapped), "grp", cores)
    parts = suffix(0, suffix_queries.shape[1] // HSZ, None)
    far, other_near, parts = lax.optimization_barrier((far, other_near, parts))
    other_far = swap(far, "grp", cores)
    by_core = [[swap(x, "grp", k) for x in (near, far)] for k in range(1, cores)]
    parts = parts.astype(jnp.float16)
    coded = lax.all_to_all(parts, "hst", split_axis=0, concat_axis=0, tiled=True)
    held = {0: after([near, far], parts), cores: [other_near, other_far]}

    def context(k, before):
        at = jnp.stack([host * groups + group, group ^ k, host % 2])
        return context_attend(at, lengths, queries, keys_values, bias, *held[k], before)

    context_out = context(0, None)
    for k in range(1, cores):
        held[k] = by_core[k - 1]
        context_out = context(k, context_out)
    other = after(held[cores], context_out)
    for k in range(1, cores):
        held[cores ^ k] = [swap(x, "grp", k) for x in other]
    for k in range(cores, groups):
        context_out = context(k, context_out)
    return (context_out, combine(coded.astype(jnp.float32)))


def solution(mesh):
    return jax.shard_map(
        per_device,
        mesh=mesh,
        in_specs=(
            P(("hst", "grp"), None),
            P(None, ("hst", "grp"), None),
            P(),
            P(),
            P("hst", "grp"),
            P(None, "hst", "grp"),
        ),
        out_specs=(P(("hst", "grp"), None), P("hst", "grp")),
        check_vma=False,
    )
```

```python
import functools
import math

import jax
import jax.numpy as jnp
from jax import lax
from jax.experimental import pallas as pl
from jax.experimental.pallas import tpu as pltpu
from jax.sharding import PartitionSpec as P

HSZ = 128
NAMB = 512
NEG = -1e30
FLOOR = -2000.0
EXTRA = 8
TILE = 256
C2 = math.log2(math.e) / math.sqrt(HSZ)
BOTH = ("hst", "grp")


def dot_t(a, b):
    return lax.dot_general(a, b, (((1,), (1,)), ((), ())), preferred_element_type=jnp.float32)


def dot(a, b):
    return lax.dot_general(a, b, (((1,), (0,)), ((), ())), preferred_element_type=jnp.float32)


def row_sums(x):
    coarse = x.astype(jnp.bfloat16)
    fine = (x - coarse.astype(jnp.float32)).astype(jnp.bfloat16)
    ones = jnp.ones((HSZ, HSZ), jnp.bfloat16)
    return dot(coarse, ones) + dot(fine, ones)


def softmax(scores):
    top = functools.reduce(jnp.maximum, [jnp.max(s, axis=-1, keepdims=True) for s in scores])
    base = top * C2
    weights = [jnp.exp2(s * C2 - base) for s in scores]
    whole = [w[:, c : c + HSZ] for w in weights for c in range(0, w.shape[1] - HSZ + 1, HSZ)]
    total = row_sums(functools.reduce(jnp.add, whole))
    for w in weights:
        if w.shape[1] % HSZ:
            total = total + jnp.sum(w[:, w.shape[1] // HSZ * HSZ :], axis=-1, keepdims=True)
    return base, total, [w.astype(jnp.bfloat16) for w in weights]


def pack_kernel(kv_ref, out_ref, below_ref, *refs):
    across_refs, diagonal_refs, (held, came, left) = refs[0:2], refs[2:4], refs[4:]
    groups, _, rows, part = out_ref.shape
    few, wide, pieces = rows // 4, groups * part // 2, [(s, i) for s in range(2) for i in range(4)]
    arrive = {}
    for s, i in pieces:
        band = pl.ds(i * few, few)
        arrive[s, i] = pltpu.make_async_copy(kv_ref.at[s, band], held.at[s, band], came.at[s, i])
        arrive[s, i].start()
    leave = []
    for s, i in pieces:
        arrive[s, i].wait()
        band, place = pl.ds(i * few, few), pl.ds(i % 2 * few, few)
        right = held.at[s, band, pl.ds(wide, wide)]
        moves = [(right, (across_refs if i < 2 else diagonal_refs)[s].at[place])]
        if i >= 2:
            moves.append((held.at[s, band, pl.ds(0, wide)], below_ref.at[s, place]))
        moves += [(held.at[s, band, pl.ds(g * part, part)], out_ref.at[g, s, band]) for g in range(groups)]
        for n, (source, target) in enumerate(moves):
            leave.append(pltpu.make_async_copy(source, target, left.at[s, i, n]))
            leave[-1].start()
    for copy in leave:
        copy.wait()


def pack(kv, groups):
    _, rows, width = kv.shape
    anywhere = pl.BlockSpec(memory_space=pl.ANY)
    half = jax.ShapeDtypeStruct((rows // 2, width // 2), kv.dtype)
    out, below, *others = pl.pallas_call(
        pack_kernel,
        in_specs=[anywhere],
        out_specs=[anywhere] * 6,
        out_shape=[
            jax.ShapeDtypeStruct((groups, 2, rows, width // groups), kv.dtype),
            jax.ShapeDtypeStruct((2, rows // 2, width // 2), kv.dtype),
        ]
        + [half] * 4,
        scratch_shapes=[
            pltpu.VMEM(kv.shape, kv.dtype),
            pltpu.SemaphoreType.DMA((2, 4)),
            pltpu.SemaphoreType.DMA((2, 4, groups + 2)),
        ],
        cost_estimate=pl.CostEstimate(flops=0, bytes_accessed=6 * kv.size, transcendentals=0),
        name="pack_heads",
    )(kv)
    return out, below, others[:2], others[2:]


def pipelined(tasks, score, finish):
    ahead = score(tasks[0])
    for n, task in enumerate(tasks):
        scores = ahead
        if n + 1 < len(tasks):
            ahead = score(tasks[n + 1])
        finish(task, scores)


def suffix_kernel(at_ref, near_ref, far_ref, kv_ref, sk_ref, bias_ref, *rest):
    out_ref = rest[-1]
    host = at_ref[0]
    groups = kv_ref.shape[0]
    half, share, _ = near_ref.shape
    hosts = 2 * half
    chunk = lambda n: near_ref[n] if n < half else far_ref[n - half]
    apart = list(range(0, hosts, 2)) + list(range(1, hosts, 2))
    chunks = min(hosts, max(1, TILE // share))
    bias = [bias_ref[pl.ds(host * groups + g, 1), :] for g in range(groups)]
    values = [kv_ref[g, 1] for g in range(groups)] + [sk_ref[1]]

    def score(first):
        q = jnp.concatenate([chunk(first + c) for c in range(chunks)], axis=0)
        s = dot_t(q, sk_ref[0])
        row = lax.broadcasted_iota(jnp.int32, (share, share), 0)
        spos = host * share + lax.broadcasted_iota(jnp.int32, (share, share), 1)
        late = []
        for c in range(chunks):
            qpos = jnp.bitwise_xor(host, apart[first + c]) * share + row
            late.append(jnp.where(spos <= qpos, s[c * share : (c + 1) * share], NEG))
        return [dot_t(q, kv_ref[g, 0]) + bias[g] for g in range(groups)] + [jnp.concatenate(late, axis=0)]

    def finish(first, scores):
        base, total, weights = softmax(scores)
        mixed = functools.reduce(jnp.add, [dot(w, v) for w, v in zip(weights, values)])
        n = mixed / total
        size = jnp.max(jnp.abs(n), axis=-1, keepdims=True)
        shift = jnp.clip(jnp.floor(jnp.log2(size)), -100.0, 100.0)
        level = jnp.maximum(base + jnp.log2(total), FLOOR)
        whole = jnp.floor(level)
        rest = jnp.exp2(level - whole)
        coarse = jnp.round(rest * 512.0) * (1.0 / 512.0)
        fine = (rest - coarse) * 1024.0
        lane = lax.broadcasted_iota(jnp.int32, (chunks * share, HSZ), 1)
        stats = jnp.where(lane == 0, whole, jnp.where(lane == 1, coarse, jnp.where(lane == 2, fine, shift)))
        turned = stats.T
        n = n * jnp.exp2(-shift)
        for c in range(chunks):
            to = jnp.bitwise_xor(host, apart[first + c])
            out_ref[to, :share, :] = n[c * share : (c + 1) * share]
            out_ref[to, share : share + EXTRA, :share] = turned[:EXTRA, c * share : (c + 1) * share]

    pipelined(list(range(0, hosts, chunks)), score, finish)


def suffix_attend(host, near, far, kv, sk, bias, first, count, before):
    half, share, width = near.shape
    hosts = 2 * half
    more = [] if before is None else [before]
    groups, _, rows, _ = kv.shape
    seen = groups * rows + share
    column = lambda h, at: (0, 0, first + h)
    return pl.pallas_call(
        suffix_kernel,
        grid_spec=pltpu.PrefetchScalarGridSpec(
            num_scalar_prefetch=1,
            grid=(count,),
            in_specs=[
                pl.BlockSpec((half, share, HSZ), column),
                pl.BlockSpec((half, share, HSZ), column),
                pl.BlockSpec((groups, 2, rows, HSZ), lambda h, at: (0, 0, 0, first + h)),
                pl.BlockSpec((2, share, HSZ), column),
                pl.BlockSpec(bias.shape, lambda h, at: (0, 0)),
            ]
            + [pl.BlockSpec(memory_space=pl.ANY) for _ in more],
            out_specs=pl.BlockSpec((hosts, share + EXTRA, HSZ), column),
        ),
        out_shape=jax.ShapeDtypeStruct((hosts, share + EXTRA, width), jnp.float32),
        input_output_aliases={6: 0} if more else {},
        compiler_params=pltpu.CompilerParams(vmem_limit_bytes=24 * 1024 * 1024),
        cost_estimate=pl.CostEstimate(
            flops=8 * count * hosts * share * seen * HSZ,
            bytes_accessed=4 * count * (groups * rows + 3 * hosts * share) * HSZ,
            transcendentals=count * hosts * share * seen,
        ),
        name="suffix_attend",
    )(host, near, far, kv, sk, bias, *more)


def combine_kernel(in_ref, out_ref):
    hosts, tall, width = in_ref.shape
    share = tall - EXTRA
    for first in range(0, width, HSZ):
        head = slice(first, first + HSZ)
        whole, coarse, fine, shift = [in_ref[:, share + k, head] for k in range(4)]
        weight = jnp.exp2(whole - jnp.max(whole, axis=0, keepdims=True)) * (coarse + fine * (1.0 / 1024.0))
        factor = weight * jnp.exp2(shift) / jnp.sum(weight, axis=0, keepdims=True)
        factor = jnp.concatenate([factor, jnp.zeros((HSZ - hosts, HSZ), jnp.float32)], axis=0).T[:share, :]
        mixed = 0.0
        for g in range(hosts):
            mixed = mixed + factor[:, g : g + 1] * in_ref[g, :share, head]
        out_ref[:, head] = mixed.astype(out_ref.dtype)


def combine(parts):
    _, tall, width = parts.shape
    return pl.pallas_call(
        combine_kernel,
        in_specs=[pl.BlockSpec(memory_space=pltpu.VMEM)],
        out_specs=pl.BlockSpec(memory_space=pltpu.VMEM),
        out_shape=jax.ShapeDtypeStruct((tall - EXTRA, width), jnp.bfloat16),
        cost_estimate=pl.CostEstimate(flops=2 * parts.size, bytes_accessed=4 * parts.size, transcendentals=0),
        name="combine_groups",
    )(parts)


def context_kernel(at_ref, len_ref, q_ref, kv_ref, bias_ref, near_ref, far_ref, *rest):
    out_ref, diag_ref = rest[-2:]
    block, odd = at_ref[0], at_ref[2]
    rows, width = q_ref.shape
    half = rows // 2
    own = bias_ref[pl.ds(block, 1), :]
    row = lax.broadcasted_iota(jnp.int32, (half, half), 0)
    col = lax.broadcasted_iota(jnp.int32, (half, half), 1)
    for t in range(2):
        ok = own[:, t * half : (t + 1) * half]
        diag_ref[t] = jnp.where(col == row, 0.0, jnp.where(col < row, ok, NEG))
    low, high = bias_ref[0:1, :half], bias_ref[0:1, half:]
    near_bias = jnp.where(block > 0, jnp.where(odd == 0, low, high), NEG)
    far_bias = jnp.where(block > 0, jnp.where(odd == 0, high, low), NEG)

    def score(task):
        first, t = task
        head = slice(first, first + HSZ)
        q = q_ref[t * half : (t + 1) * half, head]
        scores = [dot_t(q, near_ref[0, :, head]) + near_bias, dot_t(q, far_ref[0, :, head]) + far_bias]
        if t == 1:
            scores.append(dot_t(q, kv_ref[0, :half, head]) + own[:, :half])
        scores.append(dot_t(q, kv_ref[0, t * half : (t + 1) * half, head]) + diag_ref[t])
        return scores

    def finish(task, scores):
        first, t = task
        head = slice(first, first + HSZ)
        _, total, weights = softmax(scores)
        values = [near_ref[1, :, head], far_ref[1, :, head]]
        values += [kv_ref[1, u * half : (u + 1) * half, head] for u in range(t + 1)]
        mixed = functools.reduce(jnp.add, [dot(w, v) for w, v in zip(weights, values)])
        place = t * half + lax.broadcasted_iota(jnp.int32, mixed.shape, 0)
        out = jnp.where(place < len_ref[block], mixed / total, 0.0)
        out_ref[t * half : (t + 1) * half, head] = out.astype(out_ref.dtype)

    pipelined([(first, t) for first in range(0, width, HSZ) for t in range(2)], score, finish)


def context_attend(at, lengths, q, kv, bias, near, far, before):
    rows, width = q.shape
    _, half, wide = near.shape
    heads = wide // HSZ
    both = lambda i, at, n: (0, 0, at[1])
    more = [] if before is None else [before]
    return pl.pallas_call(
        context_kernel,
        grid_spec=pltpu.PrefetchScalarGridSpec(
            num_scalar_prefetch=2,
            grid=(1,),
            in_specs=[
                pl.BlockSpec((rows, wide), lambda i, at, n: (0, at[1])),
                pl.BlockSpec((2, rows, wide), both),
                pl.BlockSpec(bias.shape, lambda i, *_: (0, 0)),
                pl.BlockSpec((2, half, wide), lambda i, *_: (0, 0, 0)),
                pl.BlockSpec((2, half, wide), lambda i, *_: (0, 0, 0)),
            ]
            + [pl.BlockSpec(memory_space=pl.ANY) for _ in more],
            out_specs=pl.BlockSpec((rows, wide), lambda i, at, n: (0, at[1])),
            scratch_shapes=[pltpu.VMEM((2, half, half), jnp.float32)],
        ),
        out_shape=jax.ShapeDtypeStruct((rows, width), q.dtype),
        input_output_aliases={7: 0} if more else {},
        compiler_params=pltpu.CompilerParams(vmem_limit_bytes=24 * 1024 * 1024),
        cost_estimate=pl.CostEstimate(
            flops=8 * rows * rows * wide,
            bytes_accessed=12 * rows * wide,
            transcendentals=2 * rows * rows * heads,
        ),
        name="context_attend",
    )(at, lengths, q, kv, bias, near, far, *more)


def swap(x, axis, k):
    return lax.ppermute(x, axis, [(i, i ^ k) for i in range(lax.axis_size(axis))])


def gather_hosts(x, hosts):
    near = jnp.stack([x] + [swap(x, "hst", k) for k in range(2, hosts, 2)], axis=0)
    return near, swap(near, "hst", 1)


def after(x, done):
    return lax.optimization_barrier((x, done))[0]


def scatter_anchor(kv, across, diagonal, below, groups):
    cores = groups // 2
    first = (lax.axis_index("hst") == 0) & (lax.axis_index("grp") == 0)
    send = lambda x, to: lax.ppermute(x, BOTH, [(0, to)])
    down = send(below, groups)
    _, rows, width = kv.shape
    slabs = []
    for s in range(2):
        slab = jnp.where(first, kv[s, : rows // 2, : width // 2], 0.0) + send(diagonal[s], groups + cores) + send(across[s], cores)
        slabs.append(slab + (after(down[s], slabs[0]) if s else down[s]))
    return slabs, down


def spread_anchor(slab, hosts, groups):
    cores = groups // 2
    wide = slab.shape[1] // cores
    piece = slab[:, :wide]
    for c in range(1, cores):
        pairs = [(x, x + c) for x in (0, cores)]
        piece = piece + lax.ppermute(slab[:, c * wide : (c + 1) * wide], "grp", pairs)
    far = hosts // 2
    while far >= 2:
        pairs = [(h, h + far) for h in range(hosts) if h % (2 * far) < 2]
        piece = piece + lax.ppermute(piece, "hst", pairs)
        far //= 2
    return piece


def per_device(queries, keys_values, token_ids, lengths, suffix_queries, suffix_kv):
    hosts, groups = lax.axis_size("hst"), lax.axis_size("grp")
    host, group = lax.axis_index("hst"), lax.axis_index("grp")
    rows = queries.shape[0]
    cores = groups // 2
    packed, below, across, diagonal = pack(keys_values, groups)
    slabs, down = scatter_anchor(keys_values, across, diagonal, below, groups)
    swapped = lax.all_to_all(after(packed, down), "grp", split_axis=0, concat_axis=0, tiled=True)
    near = jnp.stack([spread_anchor(x, hosts, groups) for x in slabs])
    gathered = gather_hosts(after(suffix_queries, slabs[1]), hosts)
    seen = (token_ids.reshape(-1, rows) >= NAMB) & (jnp.arange(rows)[None, :] < lengths[:, None])
    bias = jnp.where(seen, 0.0, NEG).astype(jnp.float32)
    suffix = functools.partial(suffix_attend, jnp.stack([host]), *gathered, swapped, suffix_kv, bias)
    far, other_near = swap(near, "hst", 1), swap(after(near, swapped), "grp", cores)
    parts = suffix(0, suffix_queries.shape[1] // HSZ, None)
    far, other_near, parts = lax.optimization_barrier((far, other_near, parts))
    other_far = swap(far, "grp", cores)
    by_core = [[swap(x, "grp", k) for x in (near, far)] for k in range(1, cores)]
    parts = parts.astype(jnp.float16)
    coded = lax.all_to_all(parts, "hst", split_axis=0, concat_axis=0, tiled=True)
    held = {0: after([near, far], parts), cores: [other_near, other_far]}

    def context(k, before):
        at = jnp.stack([host * groups + group, group ^ k, host % 2])
        return context_attend(at, lengths, queries, keys_values, bias, *held[k], before)

    context_out = context(0, None)
    for k in range(1, cores):
        held[k] = by_core[k - 1]
        context_out = context(k, context_out)
    other = after(held[cores], context_out)
    for k in range(1, cores):
        held[cores ^ k] = [swap(x, "grp", k) for x in other]
    for k in range(cores, groups):
        context_out = context(k, context_out)
    return (context_out, combine(coded.astype(jnp.float32)))


def solution(mesh):
    return jax.shard_map(
        per_device,
        mesh=mesh,
        in_specs=(
            P(("hst", "grp"), None),
            P(None, ("hst", "grp"), None),
            P(),
            P(),
            P("hst", "grp"),
            P(None, "hst", "grp"),
        ),
        out_specs=(P(("hst", "grp"), None), P("hst", "grp")),
        check_vma=False,
    )
```

```python
import functools
import math

import jax
import jax.numpy as jnp
from jax import lax
from jax.experimental import pallas as pl
from jax.experimental.pallas import tpu as pltpu
from jax.sharding import PartitionSpec as P

HSZ = 128
NAMB = 512
NEG = -1e30
FLOOR = -2000.0
EXTRA = 8
TILE = 256
C2 = math.log2(math.e) / math.sqrt(HSZ)
BOTH = ("hst", "grp")


def dot_t(a, b):
    return lax.dot_general(a, b, (((1,), (1,)), ((), ())), preferred_element_type=jnp.float32)


def dot(a, b):
    return lax.dot_general(a, b, (((1,), (0,)), ((), ())), preferred_element_type=jnp.float32)


def softmax(scores):
    top = functools.reduce(jnp.maximum, [jnp.max(s, axis=-1, keepdims=True) for s in scores])
    base = top * C2
    weights = [jnp.exp2(s * C2 - base) for s in scores]
    total = functools.reduce(jnp.add, [jnp.sum(w, axis=-1, keepdims=True) for w in weights])
    return base, total, [w.astype(jnp.bfloat16) for w in weights]


def pack_kernel(kv_ref, out_ref, *refs):
    below_refs, across_refs, diagonal_refs, (held, came, left) = refs[0:2], refs[2:4], refs[4:6], refs[6:]
    groups, _, rows, part = out_ref.shape
    few, wide, pieces = rows // 4, groups * part // 2, [(s, i) for s in range(2) for i in range(4)]
    arrive = {}
    for s, i in pieces:
        band = pl.ds(i * few, few)
        arrive[s, i] = pltpu.make_async_copy(kv_ref.at[s, band], held.at[s, band], came.at[s, i])
        arrive[s, i].start()
    leave = []
    for s, i in pieces:
        arrive[s, i].wait()
        band, place = pl.ds(i * few, few), pl.ds(i % 2 * few, few)
        right = held.at[s, band, pl.ds(wide, wide)]
        moves = [(right, (across_refs if i < 2 else diagonal_refs)[s].at[place])]
        if i >= 2:
            moves.append((held.at[s, band, pl.ds(0, wide)], below_refs[s].at[place]))
        moves += [(held.at[s, band, pl.ds(g * part, part)], out_ref.at[g, s, band]) for g in range(groups)]
        for n, (source, target) in enumerate(moves):
            leave.append(pltpu.make_async_copy(source, target, left.at[s, i, n]))
            leave[-1].start()
    for copy in leave:
        copy.wait()


def pack(kv, groups):
    _, rows, width = kv.shape
    anywhere = pl.BlockSpec(memory_space=pl.ANY)
    half = jax.ShapeDtypeStruct((rows // 2, width // 2), kv.dtype)
    out, *quarters = pl.pallas_call(
        pack_kernel,
        in_specs=[anywhere],
        out_specs=[anywhere] * 7,
        out_shape=[jax.ShapeDtypeStruct((groups, 2, rows, width // groups), kv.dtype)] + [half] * 6,
        scratch_shapes=[
            pltpu.VMEM(kv.shape, kv.dtype),
            pltpu.SemaphoreType.DMA((2, 4)),
            pltpu.SemaphoreType.DMA((2, 4, groups + 2)),
        ],
        cost_estimate=pl.CostEstimate(flops=0, bytes_accessed=6 * kv.size, transcendentals=0),
        name="pack_heads",
    )(kv)
    return out, quarters[:2], quarters[2:4], quarters[4:]


def pipelined(tasks, score, finish):
    ahead = score(tasks[0])
    for n, task in enumerate(tasks):
        scores = ahead
        if n + 1 < len(tasks):
            ahead = score(tasks[n + 1])
        finish(task, scores)


def suffix_kernel(at_ref, near_ref, far_ref, kv_ref, sk_ref, bias_ref, *rest):
    out_ref = rest[-1]
    host = at_ref[0]
    groups = kv_ref.shape[0]
    half, share, _ = near_ref.shape
    hosts = 2 * half
    chunk = lambda n: near_ref[n] if n < half else far_ref[n - half]
    apart = list(range(0, hosts, 2)) + list(range(1, hosts, 2))
    chunks = min(hosts, max(1, TILE // share))
    bias = [bias_ref[pl.ds(host * groups + g, 1), :] for g in range(groups)]
    values = [kv_ref[g, 1] for g in range(groups)] + [sk_ref[1]]

    def score(first):
        q = jnp.concatenate([chunk(first + c) for c in range(chunks)], axis=0)
        s = dot_t(q, sk_ref[0])
        row = lax.broadcasted_iota(jnp.int32, (share, share), 0)
        spos = host * share + lax.broadcasted_iota(jnp.int32, (share, share), 1)
        late = []
        for c in range(chunks):
            qpos = jnp.bitwise_xor(host, apart[first + c]) * share + row
            late.append(jnp.where(spos <= qpos, s[c * share : (c + 1) * share], NEG))
        return [dot_t(q, kv_ref[g, 0]) + bias[g] for g in range(groups)] + [jnp.concatenate(late, axis=0)]

    def finish(first, scores):
        base, total, weights = softmax(scores)
        mixed = functools.reduce(jnp.add, [dot(w, v) for w, v in zip(weights, values)])
        n = mixed / total
        size = jnp.max(jnp.abs(n), axis=-1, keepdims=True)
        shift = jnp.clip(jnp.floor(jnp.log2(size)), -100.0, 100.0)
        level = jnp.maximum(base + jnp.log2(total), FLOOR)
        whole = jnp.floor(level)
        rest = jnp.exp2(level - whole)
        coarse = jnp.round(rest * 512.0) * (1.0 / 512.0)
        fine = (rest - coarse) * 1024.0
        lane = lax.broadcasted_iota(jnp.int32, (chunks * share, HSZ), 1)
        stats = jnp.where(lane == 0, whole, jnp.where(lane == 1, coarse, jnp.where(lane == 2, fine, shift)))
        turned = stats.T
        n = n * jnp.exp2(-shift)
        for c in range(chunks):
            to = jnp.bitwise_xor(host, apart[first + c])
            out_ref[to, :share, :] = n[c * share : (c + 1) * share]
            out_ref[to, share : share + EXTRA, :share] = turned[:EXTRA, c * share : (c + 1) * share]

    pipelined(list(range(0, hosts, chunks)), score, finish)


def suffix_attend(host, near, far, kv, sk, bias, first, count, before):
    half, share, width = near.shape
    hosts = 2 * half
    more = [] if before is None else [before]
    groups, _, rows, _ = kv.shape
    seen = groups * rows + share
    column = lambda h, at: (0, 0, first + h)
    return pl.pallas_call(
        suffix_kernel,
        grid_spec=pltpu.PrefetchScalarGridSpec(
            num_scalar_prefetch=1,
            grid=(count,),
            in_specs=[
                pl.BlockSpec((half, share, HSZ), column),
                pl.BlockSpec((half, share, HSZ), column),
                pl.BlockSpec((groups, 2, rows, HSZ), lambda h, at: (0, 0, 0, first + h)),
                pl.BlockSpec((2, share, HSZ), column),
                pl.BlockSpec(bias.shape, lambda h, at: (0, 0)),
            ]
            + [pl.BlockSpec(memory_space=pl.ANY) for _ in more],
            out_specs=pl.BlockSpec((hosts, share + EXTRA, HSZ), column),
        ),
        out_shape=jax.ShapeDtypeStruct((hosts, share + EXTRA, width), jnp.float32),
        input_output_aliases={6: 0} if more else {},
        compiler_params=pltpu.CompilerParams(vmem_limit_bytes=24 * 1024 * 1024),
        cost_estimate=pl.CostEstimate(
            flops=8 * count * hosts * share * seen * HSZ,
            bytes_accessed=4 * count * (groups * rows + 3 * hosts * share) * HSZ,
            transcendentals=count * hosts * share * seen,
        ),
        name="suffix_attend",
    )(host, near, far, kv, sk, bias, *more)


def combine_kernel(in_ref, out_ref):
    hosts, tall, width = in_ref.shape
    share = tall - EXTRA
    for first in range(0, width, HSZ):
        head = slice(first, first + HSZ)
        whole, coarse, fine, shift = [in_ref[:, share + k, head] for k in range(4)]
        weight = jnp.exp2(whole - jnp.max(whole, axis=0, keepdims=True)) * (coarse + fine * (1.0 / 1024.0))
        factor = weight * jnp.exp2(shift) / jnp.sum(weight, axis=0, keepdims=True)
        factor = jnp.concatenate([factor, jnp.zeros((HSZ - hosts, HSZ), jnp.float32)], axis=0).T[:share, :]
        mixed = 0.0
        for g in range(hosts):
            mixed = mixed + factor[:, g : g + 1] * in_ref[g, :share, head]
        out_ref[:, head] = mixed.astype(out_ref.dtype)


def combine(parts):
    _, tall, width = parts.shape
    return pl.pallas_call(
        combine_kernel,
        in_specs=[pl.BlockSpec(memory_space=pltpu.VMEM)],
        out_specs=pl.BlockSpec(memory_space=pltpu.VMEM),
        out_shape=jax.ShapeDtypeStruct((tall - EXTRA, width), jnp.bfloat16),
        cost_estimate=pl.CostEstimate(flops=2 * parts.size, bytes_accessed=4 * parts.size, transcendentals=0),
        name="combine_groups",
    )(parts)


def context_kernel(at_ref, len_ref, q_ref, kv_ref, bias_ref, near_ref, far_ref, *rest):
    out_ref, diag_ref = rest[-2:]
    block, odd = at_ref[0], at_ref[2]
    rows, width = q_ref.shape
    half = rows // 2
    own = bias_ref[pl.ds(block, 1), :]
    row = lax.broadcasted_iota(jnp.int32, (half, half), 0)
    col = lax.broadcasted_iota(jnp.int32, (half, half), 1)
    for t in range(2):
        ok = own[:, t * half : (t + 1) * half]
        diag_ref[t] = jnp.where(col == row, 0.0, jnp.where(col < row, ok, NEG))
    low, high = bias_ref[0:1, :half], bias_ref[0:1, half:]
    near_bias = jnp.where(block > 0, jnp.where(odd == 0, low, high), NEG)
    far_bias = jnp.where(block > 0, jnp.where(odd == 0, high, low), NEG)

    def score(task):
        first, t = task
        head = slice(first, first + HSZ)
        q = q_ref[t * half : (t + 1) * half, head]
        scores = [dot_t(q, near_ref[0, :, head]) + near_bias, dot_t(q, far_ref[0, :, head]) + far_bias]
        if t == 1:
            scores.append(dot_t(q, kv_ref[0, :half, head]) + own[:, :half])
        scores.append(dot_t(q, kv_ref[0, t * half : (t + 1) * half, head]) + diag_ref[t])
        return scores

    def finish(task, scores):
        first, t = task
        head = slice(first, first + HSZ)
        _, total, weights = softmax(scores)
        values = [near_ref[1, :, head], far_ref[1, :, head]]
        values += [kv_ref[1, u * half : (u + 1) * half, head] for u in range(t + 1)]
        mixed = functools.reduce(jnp.add, [dot(w, v) for w, v in zip(weights, values)])
        place = t * half + lax.broadcasted_iota(jnp.int32, mixed.shape, 0)
        out = jnp.where(place < len_ref[block], mixed / total, 0.0)
        out_ref[t * half : (t + 1) * half, head] = out.astype(out_ref.dtype)

    pipelined([(first, t) for first in range(0, width, HSZ) for t in range(2)], score, finish)


def context_attend(at, lengths, q, kv, bias, near, far, before):
    rows, width = q.shape
    _, half, wide = near.shape
    heads = wide // HSZ
    both = lambda i, at, n: (0, 0, at[1])
    more = [] if before is None else [before]
    return pl.pallas_call(
        context_kernel,
        grid_spec=pltpu.PrefetchScalarGridSpec(
            num_scalar_prefetch=2,
            grid=(1,),
            in_specs=[
                pl.BlockSpec((rows, wide), lambda i, at, n: (0, at[1])),
                pl.BlockSpec((2, rows, wide), both),
                pl.BlockSpec(bias.shape, lambda i, *_: (0, 0)),
                pl.BlockSpec((2, half, wide), lambda i, *_: (0, 0, 0)),
                pl.BlockSpec((2, half, wide), lambda i, *_: (0, 0, 0)),
            ]
            + [pl.BlockSpec(memory_space=pl.ANY) for _ in more],
            out_specs=pl.BlockSpec((rows, wide), lambda i, at, n: (0, at[1])),
            scratch_shapes=[pltpu.VMEM((2, half, half), jnp.float32)],
        ),
        out_shape=jax.ShapeDtypeStruct((rows, width), q.dtype),
        input_output_aliases={7: 0} if more else {},
        compiler_params=pltpu.CompilerParams(vmem_limit_bytes=24 * 1024 * 1024),
        cost_estimate=pl.CostEstimate(
            flops=8 * rows * rows * wide,
            bytes_accessed=12 * rows * wide,
            transcendentals=2 * rows * rows * heads,
        ),
        name="context_attend",
    )(at, lengths, q, kv, bias, near, far, *more)


def swap(x, axis, k):
    return lax.ppermute(x, axis, [(i, i ^ k) for i in range(lax.axis_size(axis))])


def gather_hosts(x, hosts):
    near = jnp.stack([x] + [swap(x, "hst", k) for k in range(2, hosts, 2)], axis=0)
    return near, swap(near, "hst", 1)


def after(x, done):
    return lax.optimization_barrier((x, done))[0]


def scatter_anchor(kv, across, diagonal, below, groups):
    cores = groups // 2
    first = (lax.axis_index("hst") == 0) & (lax.axis_index("grp") == 0)
    send = lambda x, to: lax.ppermute(x, BOTH, [(0, to)])
    _, rows, width = kv.shape
    slabs = []
    for s in range(2):
        down = send(below[s], groups)
        if s:
            down = after(down, slabs[0])
        else:
            come = down
        slab = jnp.where(first, kv[s, : rows // 2, : width // 2], 0.0)
        slabs.append(slab + send(diagonal[s], groups + cores) + send(across[s], cores) + down)
    return slabs, come


def spread_anchor(slab, hosts, groups):
    cores = groups // 2
    wide = slab.shape[1] // cores
    piece = slab[:, :wide]
    for c in range(1, cores):
        pairs = [(x, x + c) for x in (0, cores)]
        piece = piece + lax.ppermute(slab[:, c * wide : (c + 1) * wide], "grp", pairs)
    far = hosts // 2
    while far >= 2:
        pairs = [(h, h + far) for h in range(hosts) if h % (2 * far) < 2]
        piece = piece + lax.ppermute(piece, "hst", pairs)
        far //= 2
    return piece


def per_device(queries, keys_values, token_ids, lengths, suffix_queries, suffix_kv):
    hosts, groups = lax.axis_size("hst"), lax.axis_size("grp")
    host, group = lax.axis_index("hst"), lax.axis_index("grp")
    rows = queries.shape[0]
    cores = groups // 2
    packed, below, across, diagonal = pack(keys_values, groups)
    slabs, down = scatter_anchor(keys_values, across, diagonal, below, groups)
    swapped = lax.all_to_all(after(packed, down), "grp", split_axis=0, concat_axis=0, tiled=True)
    near = jnp.stack([spread_anchor(x, hosts, groups) for x in slabs])
    gathered = gather_hosts(after(suffix_queries, slabs[1]), hosts)
    token_ids = after(token_ids, slabs[1])
    seen = (token_ids.reshape(-1, rows) >= NAMB) & (jnp.arange(rows)[None, :] < lengths[:, None])
    bias = jnp.where(seen, 0.0, NEG).astype(jnp.float32)
    suffix = functools.partial(suffix_attend, jnp.stack([host]), *gathered, swapped, suffix_kv, bias)
    heads = suffix_queries.shape[1] // HSZ
    early = max(1, heads - 1)
    far, other_near = swap(near, "hst", 1), swap(after(near, swapped), "grp", cores)
    far, other_near, parts = lax.optimization_barrier((far, other_near, suffix(0, early, None)))
    other_far = swap(far, "grp", cores)
    by_core = [[swap(x, "grp", k) for x in (near, far)] for k in range(1, cores)]
    if heads > early:
        parts = suffix(early, heads - early, parts)
    by_core, parts = lax.optimization_barrier((by_core, parts))
    parts = parts.astype(jnp.float16)
    coded = lax.all_to_all(parts, "hst", split_axis=0, concat_axis=0, tiled=True)
    held = {0: after([near, far], parts), cores: [other_near, other_far]}

    def context(k, before):
        at = jnp.stack([host * groups + group, group ^ k, host % 2])
        return context_attend(at, lengths, queries, keys_values, bias, *held[k], before)

    context_out = context(0, None)
    for k in range(1, cores):
        held[k] = by_core[k - 1]
        context_out = context(k, context_out)
    other = after(held[cores], context_out)
    for k in range(1, cores):
        held[cores ^ k] = [swap(x, "grp", k) for x in other]
    for k in range(cores, groups):
        context_out = context(k, context_out)
    return (context_out, combine(coded.astype(jnp.float32)))


def solution(mesh):
    return jax.shard_map(
        per_device,
        mesh=mesh,
        in_specs=(
            P(("hst", "grp"), None),
            P(None, ("hst", "grp"), None),
            P(),
            P(),
            P("hst", "grp"),
            P(None, "hst", "grp"),
        ),
        out_specs=(P(("hst", "grp"), None), P("hst", "grp")),
        check_vma=False,
    )
```

```python
import functools
import math

import jax
import jax.numpy as jnp
from jax import lax
from jax.experimental import pallas as pl
from jax.experimental.pallas import tpu as pltpu
from jax.sharding import PartitionSpec as P

HSZ = 128
NAMB = 512
NEG = -1e30
FLOOR = -2000.0
EXTRA = 8
TILE = 256
C2 = math.log2(math.e) / math.sqrt(HSZ)
BOTH = ("hst", "grp")


def dot_t(a, b):
    return lax.dot_general(a, b, (((1,), (1,)), ((), ())), preferred_element_type=jnp.float32)


def dot(a, b):
    return lax.dot_general(a, b, (((1,), (0,)), ((), ())), preferred_element_type=jnp.float32)


def softmax(scores):
    top = functools.reduce(jnp.maximum, [jnp.max(s, axis=-1, keepdims=True) for s in scores])
    base = top * C2
    weights = [jnp.exp2(s * C2 - base) for s in scores]
    total = functools.reduce(jnp.add, [jnp.sum(w, axis=-1, keepdims=True) for w in weights])
    return base, total, [w.astype(jnp.bfloat16) for w in weights]


def pack_kernel(kv_ref, out_ref, *refs):
    below_refs, across_refs, diagonal_refs, (held, came, left) = refs[0:2], refs[2:4], refs[4:6], refs[6:]
    groups, _, rows, part = out_ref.shape
    few, wide, pieces = rows // 4, groups * part // 2, [(s, i) for s in range(2) for i in range(4)]
    arrive = {}
    for s, i in pieces:
        band = pl.ds(i * few, few)
        arrive[s, i] = pltpu.make_async_copy(kv_ref.at[s, band], held.at[s, band], came.at[s, i])
        arrive[s, i].start()
    leave = []
    for s, i in pieces:
        arrive[s, i].wait()
        band, place = pl.ds(i * few, few), pl.ds(i % 2 * few, few)
        right = held.at[s, band, pl.ds(wide, wide)]
        moves = [(right, (across_refs if i < 2 else diagonal_refs)[s].at[place])]
        if i >= 2:
            moves.append((held.at[s, band, pl.ds(0, wide)], below_refs[s].at[place]))
        moves += [(held.at[s, band, pl.ds(g * part, part)], out_ref.at[g, s, band]) for g in range(groups)]
        for n, (source, target) in enumerate(moves):
            leave.append(pltpu.make_async_copy(source, target, left.at[s, i, n]))
            leave[-1].start()
    for copy in leave:
        copy.wait()


def pack(kv, groups):
    _, rows, width = kv.shape
    anywhere = pl.BlockSpec(memory_space=pl.ANY)
    half = jax.ShapeDtypeStruct((rows // 2, width // 2), kv.dtype)
    out, *quarters = pl.pallas_call(
        pack_kernel,
        in_specs=[anywhere],
        out_specs=[anywhere] * 7,
        out_shape=[jax.ShapeDtypeStruct((groups, 2, rows, width // groups), kv.dtype)] + [half] * 6,
        scratch_shapes=[
            pltpu.VMEM(kv.shape, kv.dtype),
            pltpu.SemaphoreType.DMA((2, 4)),
            pltpu.SemaphoreType.DMA((2, 4, groups + 2)),
        ],
        cost_estimate=pl.CostEstimate(flops=0, bytes_accessed=6 * kv.size, transcendentals=0),
        name="pack_heads",
    )(kv)
    return out, quarters[:2], quarters[2:4], quarters[4:]


def pipelined(tasks, score, finish):
    ahead = score(tasks[0])
    for n, task in enumerate(tasks):
        scores = ahead
        if n + 1 < len(tasks):
            ahead = score(tasks[n + 1])
        finish(task, scores)


def suffix_kernel(at_ref, near_ref, far_ref, kv_ref, sk_ref, bias_ref, *rest):
    out_ref = rest[-1]
    host = at_ref[0]
    groups = kv_ref.shape[0]
    half, share, _ = near_ref.shape
    hosts = 2 * half
    chunk = lambda n: near_ref[n] if n < half else far_ref[n - half]
    apart = list(range(0, hosts, 2)) + list(range(1, hosts, 2))
    chunks = min(hosts, max(1, TILE // share))
    bias = [bias_ref[pl.ds(host * groups + g, 1), :] for g in range(groups)]
    values = [kv_ref[g, 1] for g in range(groups)] + [sk_ref[1]]

    def score(first):
        q = jnp.concatenate([chunk(first + c) for c in range(chunks)], axis=0)
        s = dot_t(q, sk_ref[0])
        row = lax.broadcasted_iota(jnp.int32, (share, share), 0)
        spos = host * share + lax.broadcasted_iota(jnp.int32, (share, share), 1)
        late = []
        for c in range(chunks):
            qpos = jnp.bitwise_xor(host, apart[first + c]) * share + row
            late.append(jnp.where(spos <= qpos, s[c * share : (c + 1) * share], NEG))
        return [dot_t(q, kv_ref[g, 0]) + bias[g] for g in range(groups)] + [jnp.concatenate(late, axis=0)]

    def finish(first, scores):
        base, total, weights = softmax(scores)
        mixed = functools.reduce(jnp.add, [dot(w, v) for w, v in zip(weights, values)])
        n = mixed / total
        size = jnp.max(jnp.abs(n), axis=-1, keepdims=True)
        shift = jnp.clip(jnp.floor(jnp.log2(size)), -100.0, 100.0)
        level = jnp.maximum(base + jnp.log2(total), FLOOR)
        whole = jnp.floor(level)
        rest = jnp.exp2(level - whole)
        coarse = jnp.round(rest * 512.0) * (1.0 / 512.0)
        fine = (rest - coarse) * 1024.0
        lane = lax.broadcasted_iota(jnp.int32, (chunks * share, HSZ), 1)
        stats = jnp.where(lane == 0, whole, jnp.where(lane == 1, coarse, jnp.where(lane == 2, fine, shift)))
        turned = stats.T
        n = n * jnp.exp2(-shift)
        for c in range(chunks):
            to = jnp.bitwise_xor(host, apart[first + c])
            out_ref[to, :share, :] = n[c * share : (c + 1) * share]
            out_ref[to, share : share + EXTRA, :share] = turned[:EXTRA, c * share : (c + 1) * share]

    pipelined(list(range(0, hosts, chunks)), score, finish)


def suffix_attend(host, near, far, kv, sk, bias, first, count, before):
    half, share, width = near.shape
    hosts = 2 * half
    more = [] if before is None else [before]
    groups, _, rows, _ = kv.shape
    seen = groups * rows + share
    column = lambda h, at: (0, 0, first + h)
    return pl.pallas_call(
        suffix_kernel,
        grid_spec=pltpu.PrefetchScalarGridSpec(
            num_scalar_prefetch=1,
            grid=(count,),
            in_specs=[
                pl.BlockSpec((half, share, HSZ), column),
                pl.BlockSpec((half, share, HSZ), column),
                pl.BlockSpec((groups, 2, rows, HSZ), lambda h, at: (0, 0, 0, first + h)),
                pl.BlockSpec((2, share, HSZ), column),
                pl.BlockSpec(bias.shape, lambda h, at: (0, 0)),
            ]
            + [pl.BlockSpec(memory_space=pl.ANY) for _ in more],
            out_specs=pl.BlockSpec((hosts, share + EXTRA, HSZ), column),
        ),
        out_shape=jax.ShapeDtypeStruct((hosts, share + EXTRA, width), jnp.float32),
        input_output_aliases={6: 0} if more else {},
        compiler_params=pltpu.CompilerParams(vmem_limit_bytes=24 * 1024 * 1024),
        cost_estimate=pl.CostEstimate(
            flops=8 * count * hosts * share * seen * HSZ,
            bytes_accessed=4 * count * (groups * rows + 3 * hosts * share) * HSZ,
            transcendentals=count * hosts * share * seen,
        ),
        name="suffix_attend",
    )(host, near, far, kv, sk, bias, *more)


def combine_kernel(in_ref, out_ref):
    hosts, tall, width = in_ref.shape
    share = tall - EXTRA
    for first in range(0, width, HSZ):
        head = slice(first, first + HSZ)
        whole, coarse, fine, shift = [in_ref[:, share + k, head] for k in range(4)]
        weight = jnp.exp2(whole - jnp.max(whole, axis=0, keepdims=True)) * (coarse + fine * (1.0 / 1024.0))
        factor = weight * jnp.exp2(shift) / jnp.sum(weight, axis=0, keepdims=True)
        factor = jnp.concatenate([factor, jnp.zeros((HSZ - hosts, HSZ), jnp.float32)], axis=0).T[:share, :]
        mixed = 0.0
        for g in range(hosts):
            mixed = mixed + factor[:, g : g + 1] * in_ref[g, :share, head]
        out_ref[:, head] = mixed.astype(out_ref.dtype)


def combine(parts):
    _, tall, width = parts.shape
    return pl.pallas_call(
        combine_kernel,
        in_specs=[pl.BlockSpec(memory_space=pltpu.VMEM)],
        out_specs=pl.BlockSpec(memory_space=pltpu.VMEM),
        out_shape=jax.ShapeDtypeStruct((tall - EXTRA, width), jnp.bfloat16),
        cost_estimate=pl.CostEstimate(flops=2 * parts.size, bytes_accessed=4 * parts.size, transcendentals=0),
        name="combine_groups",
    )(parts)


def context_kernel(at_ref, len_ref, q_ref, kv_ref, bias_ref, near_ref, far_ref, *rest):
    out_ref, diag_ref = rest[-2:]
    block, odd = at_ref[0], at_ref[2]
    rows, width = q_ref.shape
    half = rows // 2
    own = bias_ref[pl.ds(block, 1), :]
    row = lax.broadcasted_iota(jnp.int32, (half, half), 0)
    col = lax.broadcasted_iota(jnp.int32, (half, half), 1)
    for t in range(2):
        ok = own[:, t * half : (t + 1) * half]
        diag_ref[t] = jnp.where(col == row, 0.0, jnp.where(col < row, ok, NEG))
    low, high = bias_ref[0:1, :half], bias_ref[0:1, half:]
    near_bias = jnp.where(block > 0, jnp.where(odd == 0, low, high), NEG)
    far_bias = jnp.where(block > 0, jnp.where(odd == 0, high, low), NEG)

    def score(task):
        first, t = task
        head = slice(first, first + HSZ)
        q = q_ref[t * half : (t + 1) * half, head]
        scores = [dot_t(q, near_ref[0, :, head]) + near_bias, dot_t(q, far_ref[0, :, head]) + far_bias]
        if t == 1:
            scores.append(dot_t(q, kv_ref[0, :half, head]) + own[:, :half])
        scores.append(dot_t(q, kv_ref[0, t * half : (t + 1) * half, head]) + diag_ref[t])
        return scores

    def finish(task, scores):
        first, t = task
        head = slice(first, first + HSZ)
        _, total, weights = softmax(scores)
        values = [near_ref[1, :, head], far_ref[1, :, head]]
        values += [kv_ref[1, u * half : (u + 1) * half, head] for u in range(t + 1)]
        mixed = functools.reduce(jnp.add, [dot(w, v) for w, v in zip(weights, values)])
        place = t * half + lax.broadcasted_iota(jnp.int32, mixed.shape, 0)
        out = jnp.where(place < len_ref[block], mixed / total, 0.0)
        out_ref[t * half : (t + 1) * half, head] = out.astype(out_ref.dtype)

    pipelined([(first, t) for first in range(0, width, HSZ) for t in range(2)], score, finish)


def context_attend(at, lengths, q, kv, bias, near, far, before):
    rows, width = q.shape
    _, half, wide = near.shape
    heads = wide // HSZ
    both = lambda i, at, n: (0, 0, at[1])
    more = [] if before is None else [before]
    return pl.pallas_call(
        context_kernel,
        grid_spec=pltpu.PrefetchScalarGridSpec(
            num_scalar_prefetch=2,
            grid=(1,),
            in_specs=[
                pl.BlockSpec((rows, wide), lambda i, at, n: (0, at[1])),
                pl.BlockSpec((2, rows, wide), both),
                pl.BlockSpec(bias.shape, lambda i, *_: (0, 0)),
                pl.BlockSpec((2, half, wide), lambda i, *_: (0, 0, 0)),
                pl.BlockSpec((2, half, wide), lambda i, *_: (0, 0, 0)),
            ]
            + [pl.BlockSpec(memory_space=pl.ANY) for _ in more],
            out_specs=pl.BlockSpec((rows, wide), lambda i, at, n: (0, at[1])),
            scratch_shapes=[pltpu.VMEM((2, half, half), jnp.float32)],
        ),
        out_shape=jax.ShapeDtypeStruct((rows, width), q.dtype),
        input_output_aliases={7: 0} if more else {},
        compiler_params=pltpu.CompilerParams(vmem_limit_bytes=24 * 1024 * 1024),
        cost_estimate=pl.CostEstimate(
            flops=8 * rows * rows * wide,
            bytes_accessed=12 * rows * wide,
            transcendentals=2 * rows * rows * heads,
        ),
        name="context_attend",
    )(at, lengths, q, kv, bias, near, far, *more)


def swap(x, axis, k):
    return lax.ppermute(x, axis, [(i, i ^ k) for i in range(lax.axis_size(axis))])


def gather_hosts(x, hosts):
    near = jnp.stack([x] + [swap(x, "hst", k) for k in range(2, hosts, 2)], axis=0)
    return near, swap(near, "hst", 1)


def after(x, done):
    return lax.optimization_barrier((x, done))[0]


def scatter_anchor(kv, across, diagonal, below, groups):
    cores = groups // 2
    first = (lax.axis_index("hst") == 0) & (lax.axis_index("grp") == 0)
    send = lambda x, to: lax.ppermute(x, BOTH, [(0, to), (to, 0)])
    _, rows, width = kv.shape
    slabs, come = [], None
    for s in range(2):
        down = send(below[s], groups)
        if s:
            down = after(down, slabs[0])
        else:
            come = down
        got = send(diagonal[s], groups + cores) + send(across[s], cores) + down
        slabs.append(jnp.where(first, kv[s, : rows // 2, : width // 2], got))
    return slabs, come


def spread_anchor(slab, hosts, groups):
    cores = groups // 2
    wide = slab.shape[1] // cores
    piece = slab[:, :wide]
    for c in range(1, cores):
        pairs = [(x, x + c) for x in (0, cores)]
        piece = piece + lax.ppermute(slab[:, c * wide : (c + 1) * wide], "grp", pairs)
    shared = piece
    far = hosts // 2
    while far >= 2:
        pairs = [(h, h + far) for h in range(hosts) if h % (2 * far) < 2]
        piece = piece + lax.ppermute(piece, "hst", pairs)
        far //= 2
    return piece, shared


def per_device(queries, keys_values, token_ids, lengths, suffix_queries, suffix_kv):
    hosts, groups = lax.axis_size("hst"), lax.axis_size("grp")
    host, group = lax.axis_index("hst"), lax.axis_index("grp")
    rows = queries.shape[0]
    cores = groups // 2
    packed, below, across, diagonal = pack(keys_values, groups)
    slabs, down = scatter_anchor(keys_values, across, diagonal, below, groups)
    swapped = lax.all_to_all(after(packed, down), "grp", split_axis=0, concat_axis=0, tiled=True)
    spread = [spread_anchor(x, hosts, groups) for x in slabs]
    near = jnp.stack([x for x, _ in spread])
    gathered = gather_hosts(after(suffix_queries, spread[1][1]), hosts)
    seen = (token_ids.reshape(-1, rows) >= NAMB) & (jnp.arange(rows)[None, :] < lengths[:, None])
    bias = jnp.where(seen, 0.0, NEG).astype(jnp.float32)
    suffix = functools.partial(suffix_attend, jnp.stack([host]), *gathered, swapped, suffix_kv, bias)
    heads = suffix_queries.shape[1] // HSZ
    early = max(1, heads - 1)
    far, other_near = swap(near, "hst", 1), swap(after(near, swapped), "grp", cores)
    far, other_near, parts = lax.optimization_barrier((far, other_near, suffix(0, early, None)))
    other_far = swap(far, "grp", cores)
    by_core = [[swap(x, "grp", k) for x in (near, far)] for k in range(1, cores)]
    if heads > early:
        parts = suffix(early, heads - early, parts)
    by_core, parts = lax.optimization_barrier((by_core, parts))
    parts = parts.astype(jnp.float16)
    coded = lax.all_to_all(parts, "hst", split_axis=0, concat_axis=0, tiled=True)
    held = {0: after([near, far], parts), cores: [other_near, other_far]}

    def context(k, before):
        at = jnp.stack([host * groups + group, group ^ k, host % 2])
        return context_attend(at, lengths, queries, keys_values, bias, *held[k], before)

    context_out = context(0, None)
    for k in range(1, cores):
        held[k] = by_core[k - 1]
        context_out = context(k, context_out)
    other = after(held[cores], context_out)
    for k in range(1, cores):
        held[cores ^ k] = [swap(x, "grp", k) for x in other]
    for k in range(cores, groups):
        context_out = context(k, context_out)
    return (context_out, combine(coded.astype(jnp.float32)))


def solution(mesh):
    return jax.shard_map(
        per_device,
        mesh=mesh,
        in_specs=(
            P(("hst", "grp"), None),
            P(None, ("hst", "grp"), None),
            P(),
            P(),
            P("hst", "grp"),
            P(None, "hst", "grp"),
        ),
        out_specs=(P(("hst", "grp"), None), P("hst", "grp")),
        check_vma=False,
    )
```

```python
import functools
import math

import jax
import jax.numpy as jnp
from jax import lax
from jax.experimental import pallas as pl
from jax.experimental.pallas import tpu as pltpu
from jax.sharding import PartitionSpec as P

HSZ = 128
NAMB = 512
NEG = -1e30
FLOOR = -2000.0
EXTRA = 8
TILE = 256
C2 = math.log2(math.e) / math.sqrt(HSZ)
BOTH = ("hst", "grp")


def dot_t(a, b):
    return lax.dot_general(a, b, (((1,), (1,)), ((), ())), preferred_element_type=jnp.float32)


def dot(a, b):
    return lax.dot_general(a, b, (((1,), (0,)), ((), ())), preferred_element_type=jnp.float32)


def softmax(scores):
    top = functools.reduce(jnp.maximum, [jnp.max(s, axis=-1, keepdims=True) for s in scores])
    base = top * C2
    weights = [jnp.exp2(s * C2 - base) for s in scores]
    total = functools.reduce(jnp.add, [jnp.sum(w, axis=-1, keepdims=True) for w in weights])
    return base, total, [w.astype(jnp.bfloat16) for w in weights]


def pack_kernel(kv_ref, out_ref, *refs):
    below_refs, (across_ref, diagonal_ref, held, came, left) = refs[0:2], refs[2:]
    groups, _, rows, part = out_ref.shape
    few, wide, pieces = rows // 4, groups * part // 2, [(s, i) for s in range(2) for i in range(4)]
    arrive = {}
    for s, i in pieces:
        band = pl.ds(i * few, few)
        arrive[s, i] = pltpu.make_async_copy(kv_ref.at[s, band], held.at[s, band], came.at[s, i])
        arrive[s, i].start()
    leave = []
    for s, i in pieces:
        arrive[s, i].wait()
        band, place = pl.ds(i * few, few), pl.ds(i % 2 * few, few)
        right = held.at[s, band, pl.ds(wide, wide)]
        moves = [(right, (across_ref if i < 2 else diagonal_ref).at[s, place])]
        if i >= 2:
            moves.append((held.at[s, band, pl.ds(0, wide)], below_refs[s].at[place]))
        moves += [(held.at[s, band, pl.ds(g * part, part)], out_ref.at[g, s, band]) for g in range(groups)]
        for n, (source, target) in enumerate(moves):
            leave.append(pltpu.make_async_copy(source, target, left.at[s, i, n]))
            leave[-1].start()
    for copy in leave:
        copy.wait()


def pack(kv, groups):
    _, rows, width = kv.shape
    anywhere = pl.BlockSpec(memory_space=pl.ANY)
    array = lambda *shape: jax.ShapeDtypeStruct(shape, kv.dtype)
    tall, wide = rows // 2, width // 2
    out, *quarters = pl.pallas_call(
        pack_kernel,
        in_specs=[anywhere],
        out_specs=[anywhere] * 5,
        out_shape=[array(groups, 2, rows, width // groups)]
        + [array(tall, wide)] * 2
        + [array(2, tall, wide)] * 2,
        scratch_shapes=[
            pltpu.VMEM(kv.shape, kv.dtype),
            pltpu.SemaphoreType.DMA((2, 4)),
            pltpu.SemaphoreType.DMA((2, 4, groups + 2)),
        ],
        cost_estimate=pl.CostEstimate(flops=0, bytes_accessed=6 * kv.size, transcendentals=0),
        name="pack_heads",
    )(kv)
    return out, quarters[:2], *quarters[2:]


def pipelined(tasks, score, finish):
    ahead = score(tasks[0])
    for n, task in enumerate(tasks):
        scores = ahead
        if n + 1 < len(tasks):
            ahead = score(tasks[n + 1])
        finish(task, scores)


def suffix_kernel(at_ref, near_ref, far_ref, kv_ref, sk_ref, bias_ref, *rest):
    out_ref = rest[-1]
    host = at_ref[0]
    groups = kv_ref.shape[0]
    half, share, _ = near_ref.shape
    hosts = 2 * half
    chunk = lambda n: near_ref[n] if n < half else far_ref[n - half]
    apart = list(range(0, hosts, 2)) + list(range(1, hosts, 2))
    chunks = min(hosts, max(1, TILE // share))
    bias = [bias_ref[pl.ds(host * groups + g, 1), :] for g in range(groups)]
    values = [kv_ref[g, 1] for g in range(groups)] + [sk_ref[1]]

    def score(first):
        q = jnp.concatenate([chunk(first + c) for c in range(chunks)], axis=0)
        s = dot_t(q, sk_ref[0])
        row = lax.broadcasted_iota(jnp.int32, (share, share), 0)
        spos = host * share + lax.broadcasted_iota(jnp.int32, (share, share), 1)
        late = []
        for c in range(chunks):
            qpos = jnp.bitwise_xor(host, apart[first + c]) * share + row
            late.append(jnp.where(spos <= qpos, s[c * share : (c + 1) * share], NEG))
        return [dot_t(q, kv_ref[g, 0]) + bias[g] for g in range(groups)] + [jnp.concatenate(late, axis=0)]

    def finish(first, scores):
        base, total, weights = softmax(scores)
        mixed = functools.reduce(jnp.add, [dot(w, v) for w, v in zip(weights, values)])
        n = mixed / total
        size = jnp.max(jnp.abs(n), axis=-1, keepdims=True)
        shift = jnp.clip(jnp.floor(jnp.log2(size)), -100.0, 100.0)
        level = jnp.maximum(base + jnp.log2(total), FLOOR)
        whole = jnp.floor(level)
        rest = jnp.exp2(level - whole)
        coarse = jnp.round(rest * 512.0) * (1.0 / 512.0)
        fine = (rest - coarse) * 1024.0
        lane = lax.broadcasted_iota(jnp.int32, (chunks * share, HSZ), 1)
        stats = jnp.where(lane == 0, whole, jnp.where(lane == 1, coarse, jnp.where(lane == 2, fine, shift)))
        turned = stats.T
        n = n * jnp.exp2(-shift)
        for c in range(chunks):
            to = jnp.bitwise_xor(host, apart[first + c])
            out_ref[to, :share, :] = n[c * share : (c + 1) * share]
            out_ref[to, share : share + EXTRA, :share] = turned[:EXTRA, c * share : (c + 1) * share]

    pipelined(list(range(0, hosts, chunks)), score, finish)


def suffix_attend(host, near, far, kv, sk, bias, first, count, before):
    half, share, width = near.shape
    hosts = 2 * half
    more = [] if before is None else [before]
    groups, _, rows, _ = kv.shape
    seen = groups * rows + share
    column = lambda h, at: (0, 0, first + h)
    return pl.pallas_call(
        suffix_kernel,
        grid_spec=pltpu.PrefetchScalarGridSpec(
            num_scalar_prefetch=1,
            grid=(count,),
            in_specs=[
                pl.BlockSpec((half, share, HSZ), column),
                pl.BlockSpec((half, share, HSZ), column),
                pl.BlockSpec((groups, 2, rows, HSZ), lambda h, at: (0, 0, 0, first + h)),
                pl.BlockSpec((2, share, HSZ), column),
                pl.BlockSpec(bias.shape, lambda h, at: (0, 0)),
            ]
            + [pl.BlockSpec(memory_space=pl.ANY) for _ in more],
            out_specs=pl.BlockSpec((hosts, share + EXTRA, HSZ), column),
        ),
        out_shape=jax.ShapeDtypeStruct((hosts, share + EXTRA, width), jnp.float32),
        input_output_aliases={6: 0} if more else {},
        compiler_params=pltpu.CompilerParams(vmem_limit_bytes=24 * 1024 * 1024),
        cost_estimate=pl.CostEstimate(
            flops=8 * count * hosts * share * seen * HSZ,
            bytes_accessed=4 * count * (groups * rows + 3 * hosts * share) * HSZ,
            transcendentals=count * hosts * share * seen,
        ),
        name="suffix_attend",
    )(host, near, far, kv, sk, bias, *more)


def combine_kernel(in_ref, out_ref):
    hosts, tall, width = in_ref.shape
    share = tall - EXTRA
    for first in range(0, width, HSZ):
        head = slice(first, first + HSZ)
        whole, coarse, fine, shift = [in_ref[:, share + k, head] for k in range(4)]
        weight = jnp.exp2(whole - jnp.max(whole, axis=0, keepdims=True)) * (coarse + fine * (1.0 / 1024.0))
        factor = weight * jnp.exp2(shift) / jnp.sum(weight, axis=0, keepdims=True)
        factor = jnp.concatenate([factor, jnp.zeros((HSZ - hosts, HSZ), jnp.float32)], axis=0).T[:share, :]
        mixed = 0.0
        for g in range(hosts):
            mixed = mixed + factor[:, g : g + 1] * in_ref[g, :share, head]
        out_ref[:, head] = mixed.astype(out_ref.dtype)


def combine(parts):
    _, tall, width = parts.shape
    return pl.pallas_call(
        combine_kernel,
        in_specs=[pl.BlockSpec(memory_space=pltpu.VMEM)],
        out_specs=pl.BlockSpec(memory_space=pltpu.VMEM),
        out_shape=jax.ShapeDtypeStruct((tall - EXTRA, width), jnp.bfloat16),
        cost_estimate=pl.CostEstimate(flops=2 * parts.size, bytes_accessed=4 * parts.size, transcendentals=0),
        name="combine_groups",
    )(parts)


def context_kernel(at_ref, len_ref, q_ref, kv_ref, bias_ref, near_ref, far_ref, *rest):
    out_ref, diag_ref = rest[-2:]
    block, odd = at_ref[0], at_ref[2]
    rows, width = q_ref.shape
    half = rows // 2
    own = bias_ref[pl.ds(block, 1), :]
    row = lax.broadcasted_iota(jnp.int32, (half, half), 0)
    col = lax.broadcasted_iota(jnp.int32, (half, half), 1)
    for t in range(2):
        ok = own[:, t * half : (t + 1) * half]
        diag_ref[t] = jnp.where(col == row, 0.0, jnp.where(col < row, ok, NEG))
    low, high = bias_ref[0:1, :half], bias_ref[0:1, half:]
    near_bias = jnp.where(block > 0, jnp.where(odd == 0, low, high), NEG)
    far_bias = jnp.where(block > 0, jnp.where(odd == 0, high, low), NEG)

    def score(task):
        first, t = task
        head = slice(first, first + HSZ)
        q = q_ref[t * half : (t + 1) * half, head]
        scores = [dot_t(q, near_ref[0, :, head]) + near_bias, dot_t(q, far_ref[0, :, head]) + far_bias]
        if t == 1:
            scores.append(dot_t(q, kv_ref[0, :half, head]) + own[:, :half])
        scores.append(dot_t(q, kv_ref[0, t * half : (t + 1) * half, head]) + diag_ref[t])
        return scores

    def finish(task, scores):
        first, t = task
        head = slice(first, first + HSZ)
        _, total, weights = softmax(scores)
        values = [near_ref[1, :, head], far_ref[1, :, head]]
        values += [kv_ref[1, u * half : (u + 1) * half, head] for u in range(t + 1)]
        mixed = functools.reduce(jnp.add, [dot(w, v) for w, v in zip(weights, values)])
        place = t * half + lax.broadcasted_iota(jnp.int32, mixed.shape, 0)
        out = jnp.where(place < len_ref[block], mixed / total, 0.0)
        out_ref[t * half : (t + 1) * half, head] = out.astype(out_ref.dtype)

    pipelined([(first, t) for first in range(0, width, HSZ) for t in range(2)], score, finish)


def context_attend(at, lengths, q, kv, bias, near, far, before):
    rows, width = q.shape
    _, half, wide = near.shape
    heads = wide // HSZ
    both = lambda i, at, n: (0, 0, at[1])
    more = [] if before is None else [before]
    return pl.pallas_call(
        context_kernel,
        grid_spec=pltpu.PrefetchScalarGridSpec(
            num_scalar_prefetch=2,
            grid=(1,),
            in_specs=[
                pl.BlockSpec((rows, wide), lambda i, at, n: (0, at[1])),
                pl.BlockSpec((2, rows, wide), both),
                pl.BlockSpec(bias.shape, lambda i, *_: (0, 0)),
                pl.BlockSpec((2, half, wide), lambda i, *_: (0, 0, 0)),
                pl.BlockSpec((2, half, wide), lambda i, *_: (0, 0, 0)),
            ]
            + [pl.BlockSpec(memory_space=pl.ANY) for _ in more],
            out_specs=pl.BlockSpec((rows, wide), lambda i, at, n: (0, at[1])),
            scratch_shapes=[pltpu.VMEM((2, half, half), jnp.float32)],
        ),
        out_shape=jax.ShapeDtypeStruct((rows, width), q.dtype),
        input_output_aliases={7: 0} if more else {},
        compiler_params=pltpu.CompilerParams(vmem_limit_bytes=24 * 1024 * 1024),
        cost_estimate=pl.CostEstimate(
            flops=8 * rows * rows * wide,
            bytes_accessed=12 * rows * wide,
            transcendentals=2 * rows * rows * heads,
        ),
        name="context_attend",
    )(at, lengths, q, kv, bias, near, far, *more)


def swap(x, axis, k):
    return lax.ppermute(x, axis, [(i, i ^ k) for i in range(lax.axis_size(axis))])


def gather_hosts(x, hosts):
    near = jnp.stack([x] + [swap(x, "hst", k) for k in range(2, hosts, 2)], axis=0)
    return near, swap(near, "hst", 1)


def after(x, done):
    return lax.optimization_barrier((x, done))[0]


def scatter_anchor(kv, across, diagonal, below, groups):
    cores = groups // 2
    first = (lax.axis_index("hst") == 0) & (lax.axis_index("grp") == 0)
    send = lambda x, to: lax.ppermute(x, BOTH, [(0, to), (to, 0)])
    _, rows, width = kv.shape
    slabs, come = [], send(below[0], groups)
    right = send(diagonal, groups + cores) + send(across, cores)
    for s in range(2):
        down = after(send(below[s], groups), slabs[0]) if s else come
        slabs.append(jnp.where(first, kv[s, : rows // 2, : width // 2], right[s] + down))
    return slabs, come


def spread_anchor(slab, hosts, groups):
    cores = groups // 2
    wide = slab.shape[1] // cores
    piece = slab[:, :wide]
    for c in range(1, cores):
        pairs = [(x, x + c) for x in (0, cores)]
        piece = piece + lax.ppermute(slab[:, c * wide : (c + 1) * wide], "grp", pairs)
    shared = piece
    far = hosts // 2
    while far >= 2:
        pairs = [(h, h + far) for h in range(hosts) if h % (2 * far) < 2]
        piece = piece + lax.ppermute(piece, "hst", pairs)
        far //= 2
    return piece, shared


def per_device(queries, keys_values, token_ids, lengths, suffix_queries, suffix_kv):
    hosts, groups = lax.axis_size("hst"), lax.axis_size("grp")
    host, group = lax.axis_index("hst"), lax.axis_index("grp")
    rows = queries.shape[0]
    cores = groups // 2
    packed, below, across, diagonal = pack(keys_values, groups)
    slabs, down = scatter_anchor(keys_values, across, diagonal, below, groups)
    swapped = lax.all_to_all(after(packed, down), "grp", split_axis=0, concat_axis=0, tiled=True)
    spread = [spread_anchor(x, hosts, groups) for x in slabs]
    near = jnp.stack([x for x, _ in spread])
    gathered = gather_hosts(after(suffix_queries, spread[1][1]), hosts)
    seen = (token_ids.reshape(-1, rows) >= NAMB) & (jnp.arange(rows)[None, :] < lengths[:, None])
    bias = jnp.where(seen, 0.0, NEG).astype(jnp.float32)
    suffix = functools.partial(suffix_attend, jnp.stack([host]), *gathered, swapped, suffix_kv, bias)
    heads = suffix_queries.shape[1] // HSZ
    early = max(1, heads - 1)
    far, other_near = swap(near, "hst", 1), swap(after(near, swapped), "grp", cores)
    far, other_near, parts = lax.optimization_barrier((far, other_near, suffix(0, early, None)))
    other_far = swap(far, "grp", cores)
    by_core = [[swap(x, "grp", k) for x in (near, far)] for k in range(1, cores)]
    if heads > early:
        parts = suffix(early, heads - early, parts)
    by_core, parts = lax.optimization_barrier((by_core, parts))
    parts = parts.astype(jnp.float16)
    coded = lax.all_to_all(parts, "hst", split_axis=0, concat_axis=0, tiled=True)
    held = {0: after([near, far], parts), cores: [other_near, other_far]}

    def context(k, before):
        at = jnp.stack([host * groups + group, group ^ k, host % 2])
        return context_attend(at, lengths, queries, keys_values, bias, *held[k], before)

    context_out = context(0, None)
    for k in range(1, cores):
        held[k] = by_core[k - 1]
        context_out = context(k, context_out)
    other = after(held[cores], context_out)
    for k in range(1, cores):
        held[cores ^ k] = [swap(x, "grp", k) for x in other]
    for k in range(cores, groups):
        context_out = context(k, context_out)
    return (context_out, combine(coded.astype(jnp.float32)))


def solution(mesh):
    return jax.shard_map(
        per_device,
        mesh=mesh,
        in_specs=(
            P(("hst", "grp"), None),
            P(None, ("hst", "grp"), None),
            P(),
            P(),
            P("hst", "grp"),
            P(None, "hst", "grp"),
        ),
        out_specs=(P(("hst", "grp"), None), P("hst", "grp")),
        check_vma=False,
    )
```

```python
import functools
import math

import jax
import jax.numpy as jnp
from jax import lax
from jax.experimental import pallas as pl
from jax.experimental.pallas import tpu as pltpu
from jax.sharding import PartitionSpec as P

HSZ = 128
NAMB = 512
NEG = -1e30
FLOOR = -2000.0
EXTRA = 8
TILE = 256
C2 = math.log2(math.e) / math.sqrt(HSZ)
BOTH = ("hst", "grp")


def dot_t(a, b):
    return lax.dot_general(a, b, (((1,), (1,)), ((), ())), preferred_element_type=jnp.float32)


def dot(a, b):
    return lax.dot_general(a, b, (((1,), (0,)), ((), ())), preferred_element_type=jnp.float32)


def softmax(scores):
    top = functools.reduce(jnp.maximum, [jnp.max(s, axis=-1, keepdims=True) for s in scores])
    base = top * C2
    weights = [jnp.exp2(s * C2 - base) for s in scores]
    total = functools.reduce(jnp.add, [jnp.sum(w, axis=-1, keepdims=True) for w in weights])
    return base, total, [w.astype(jnp.bfloat16) for w in weights]


def pack_kernel(kv_ref, out_ref, *refs):
    below_refs, across_refs, diagonal_refs, (held, came, left) = refs[0:2], refs[2:4], refs[4:6], refs[6:]
    groups, _, rows, part = out_ref.shape
    few, wide, pieces = rows // 4, groups * part // 2, [(s, i) for s in range(2) for i in range(4)]
    arrive = {}
    for s, i in pieces:
        band = pl.ds(i * few, few)
        arrive[s, i] = pltpu.make_async_copy(kv_ref.at[s, band], held.at[s, band], came.at[s, i])
        arrive[s, i].start()
    leave = []
    for s, i in pieces:
        arrive[s, i].wait()
        band, place = pl.ds(i * few, few), pl.ds(i % 2 * few, few)
        right = held.at[s, band, pl.ds(wide, wide)]
        moves = [(right, (across_refs if i < 2 else diagonal_refs)[s].at[place])]
        if i >= 2:
            moves.append((held.at[s, band, pl.ds(0, wide)], below_refs[s].at[place]))
        moves += [(held.at[s, band, pl.ds(g * part, part)], out_ref.at[g, s, band]) for g in range(groups)]
        for n, (source, target) in enumerate(moves):
            leave.append(pltpu.make_async_copy(source, target, left.at[s, i, n]))
            leave[-1].start()
    for copy in leave:
        copy.wait()


def pack(kv, groups):
    _, rows, width = kv.shape
    anywhere = pl.BlockSpec(memory_space=pl.ANY)
    half = jax.ShapeDtypeStruct((rows // 2, width // 2), kv.dtype)
    out, *quarters = pl.pallas_call(
        pack_kernel,
        in_specs=[anywhere],
        out_specs=[anywhere] * 7,
        out_shape=[jax.ShapeDtypeStruct((groups, 2, rows, width // groups), kv.dtype)] + [half] * 6,
        scratch_shapes=[
            pltpu.VMEM(kv.shape, kv.dtype),
            pltpu.SemaphoreType.DMA((2, 4)),
            pltpu.SemaphoreType.DMA((2, 4, groups + 2)),
        ],
        cost_estimate=pl.CostEstimate(flops=0, bytes_accessed=6 * kv.size, transcendentals=0),
        name="pack_heads",
    )(kv)
    return out, quarters[:2], quarters[2:4], quarters[4:]


def pipelined(tasks, score, finish):
    ahead = score(tasks[0])
    for n, task in enumerate(tasks):
        scores = ahead
        if n + 1 < len(tasks):
            ahead = score(tasks[n + 1])
        finish(task, scores)


def suffix_kernel(at_ref, near_ref, far_ref, kv_ref, sk_ref, bias_ref, *rest):
    out_ref = rest[-1]
    host = at_ref[0]
    groups = kv_ref.shape[0]
    half, share, _ = near_ref.shape
    hosts = 2 * half
    chunk = lambda n: near_ref[n] if n < half else far_ref[n - half]
    apart = list(range(0, hosts, 2)) + list(range(1, hosts, 2))
    chunks = min(hosts, max(1, TILE // share))
    bias = [bias_ref[pl.ds(host * groups + g, 1), :] for g in range(groups)]
    values = [kv_ref[g, 1] for g in range(groups)] + [sk_ref[1]]

    def score(first):
        q = jnp.concatenate([chunk(first + c) for c in range(chunks)], axis=0)
        s = dot_t(q, sk_ref[0])
        row = lax.broadcasted_iota(jnp.int32, (share, share), 0)
        spos = host * share + lax.broadcasted_iota(jnp.int32, (share, share), 1)
        late = []
        for c in range(chunks):
            qpos = jnp.bitwise_xor(host, apart[first + c]) * share + row
            late.append(jnp.where(spos <= qpos, s[c * share : (c + 1) * share], NEG))
        return [dot_t(q, kv_ref[g, 0]) + bias[g] for g in range(groups)] + [jnp.concatenate(late, axis=0)]

    def finish(first, scores):
        base, total, weights = softmax(scores)
        mixed = functools.reduce(jnp.add, [dot(w, v) for w, v in zip(weights, values)])
        n = mixed / total
        size = jnp.max(jnp.abs(n), axis=-1, keepdims=True)
        shift = jnp.clip(jnp.floor(jnp.log2(size)), -100.0, 100.0)
        level = jnp.maximum(base + jnp.log2(total), FLOOR)
        whole = jnp.floor(level)
        rest = jnp.exp2(level - whole)
        coarse = jnp.round(rest * 512.0) * (1.0 / 512.0)
        fine = (rest - coarse) * 1024.0
        lane = lax.broadcasted_iota(jnp.int32, (chunks * share, HSZ), 1)
        stats = jnp.where(lane == 0, whole, jnp.where(lane == 1, coarse, jnp.where(lane == 2, fine, shift)))
        turned = stats.T
        n = n * jnp.exp2(-shift)
        for c in range(chunks):
            to = jnp.bitwise_xor(host, apart[first + c])
            out_ref[to, :share, :] = n[c * share : (c + 1) * share]
            out_ref[to, share : share + EXTRA, :share] = turned[:EXTRA, c * share : (c + 1) * share]

    pipelined(list(range(0, hosts, chunks)), score, finish)


def suffix_attend(host, near, far, kv, sk, bias, first, count, before):
    half, share, width = near.shape
    hosts = 2 * half
    more = [] if before is None else [before]
    groups, _, rows, _ = kv.shape
    seen = groups * rows + share
    column = lambda h, at: (0, 0, first + h)
    return pl.pallas_call(
        suffix_kernel,
        grid_spec=pltpu.PrefetchScalarGridSpec(
            num_scalar_prefetch=1,
            grid=(count,),
            in_specs=[
                pl.BlockSpec((half, share, HSZ), column),
                pl.BlockSpec((half, share, HSZ), column),
                pl.BlockSpec((groups, 2, rows, HSZ), lambda h, at: (0, 0, 0, first + h)),
                pl.BlockSpec((2, share, HSZ), column),
                pl.BlockSpec(bias.shape, lambda h, at: (0, 0)),
            ]
            + [pl.BlockSpec(memory_space=pl.ANY) for _ in more],
            out_specs=pl.BlockSpec((hosts, share + EXTRA, HSZ), column),
        ),
        out_shape=jax.ShapeDtypeStruct((hosts, share + EXTRA, width), jnp.float32),
        input_output_aliases={6: 0} if more else {},
        compiler_params=pltpu.CompilerParams(vmem_limit_bytes=16 * 1024 * 1024),
        cost_estimate=pl.CostEstimate(
            flops=8 * count * hosts * share * seen * HSZ,
            bytes_accessed=4 * count * (groups * rows + 3 * hosts * share) * HSZ,
            transcendentals=count * hosts * share * seen,
        ),
        name="suffix_attend",
    )(host, near, far, kv, sk, bias, *more)


def combine_kernel(in_ref, out_ref):
    hosts, tall, width = in_ref.shape
    share = tall - EXTRA
    for first in range(0, width, HSZ):
        head = slice(first, first + HSZ)
        whole, coarse, fine, shift = [in_ref[:, share + k, head] for k in range(4)]
        weight = jnp.exp2(whole - jnp.max(whole, axis=0, keepdims=True)) * (coarse + fine * (1.0 / 1024.0))
        factor = weight * jnp.exp2(shift) / jnp.sum(weight, axis=0, keepdims=True)
        factor = jnp.concatenate([factor, jnp.zeros((HSZ - hosts, HSZ), jnp.float32)], axis=0).T[:share, :]
        mixed = 0.0
        for g in range(hosts):
            mixed = mixed + factor[:, g : g + 1] * in_ref[g, :share, head]
        out_ref[:, head] = mixed.astype(out_ref.dtype)


def combine(parts):
    _, tall, width = parts.shape
    return pl.pallas_call(
        combine_kernel,
        in_specs=[pl.BlockSpec(memory_space=pltpu.VMEM)],
        out_specs=pl.BlockSpec(memory_space=pltpu.VMEM),
        out_shape=jax.ShapeDtypeStruct((tall - EXTRA, width), jnp.bfloat16),
        cost_estimate=pl.CostEstimate(flops=2 * parts.size, bytes_accessed=4 * parts.size, transcendentals=0),
        name="combine_groups",
    )(parts)


def context_kernel(at_ref, len_ref, q_ref, kv_ref, bias_ref, near_ref, far_ref, *rest):
    out_ref, diag_ref = rest[-2:]
    block, odd = at_ref[0], at_ref[2]
    rows, width = q_ref.shape
    half = rows // 2
    own = bias_ref[pl.ds(block, 1), :]
    row = lax.broadcasted_iota(jnp.int32, (half, half), 0)
    col = lax.broadcasted_iota(jnp.int32, (half, half), 1)
    for t in range(2):
        ok = own[:, t * half : (t + 1) * half]
        diag_ref[t] = jnp.where(col == row, 0.0, jnp.where(col < row, ok, NEG))
    low, high = bias_ref[0:1, :half], bias_ref[0:1, half:]
    near_bias = jnp.where(block > 0, jnp.where(odd == 0, low, high), NEG)
    far_bias = jnp.where(block > 0, jnp.where(odd == 0, high, low), NEG)

    def score(task):
        first, t = task
        head = slice(first, first + HSZ)
        q = q_ref[t * half : (t + 1) * half, head]
        scores = [dot_t(q, near_ref[0, :, head]) + near_bias, dot_t(q, far_ref[0, :, head]) + far_bias]
        if t == 1:
            scores.append(dot_t(q, kv_ref[0, :half, head]) + own[:, :half])
        scores.append(dot_t(q, kv_ref[0, t * half : (t + 1) * half, head]) + diag_ref[t])
        return scores

    def finish(task, scores):
        first, t = task
        head = slice(first, first + HSZ)
        _, total, weights = softmax(scores)
        values = [near_ref[1, :, head], far_ref[1, :, head]]
        values += [kv_ref[1, u * half : (u + 1) * half, head] for u in range(t + 1)]
        mixed = functools.reduce(jnp.add, [dot(w, v) for w, v in zip(weights, values)])
        place = t * half + lax.broadcasted_iota(jnp.int32, mixed.shape, 0)
        out = jnp.where(place < len_ref[block], mixed / total, 0.0)
        out_ref[t * half : (t + 1) * half, head] = out.astype(out_ref.dtype)

    pipelined([(first, t) for first in range(0, width, HSZ) for t in range(2)], score, finish)


def context_attend(at, lengths, q, kv, bias, near, far, before):
    rows, width = q.shape
    _, half, wide = near.shape
    heads = wide // HSZ
    both = lambda i, at, n: (0, 0, at[1])
    more = [] if before is None else [before]
    return pl.pallas_call(
        context_kernel,
        grid_spec=pltpu.PrefetchScalarGridSpec(
            num_scalar_prefetch=2,
            grid=(1,),
            in_specs=[
                pl.BlockSpec((rows, wide), lambda i, at, n: (0, at[1])),
                pl.BlockSpec((2, rows, wide), both),
                pl.BlockSpec(bias.shape, lambda i, *_: (0, 0)),
                pl.BlockSpec((2, half, wide), lambda i, *_: (0, 0, 0)),
                pl.BlockSpec((2, half, wide), lambda i, *_: (0, 0, 0)),
            ]
            + [pl.BlockSpec(memory_space=pl.ANY) for _ in more],
            out_specs=pl.BlockSpec((rows, wide), lambda i, at, n: (0, at[1])),
            scratch_shapes=[pltpu.VMEM((2, half, half), jnp.float32)],
        ),
        out_shape=jax.ShapeDtypeStruct((rows, width), q.dtype),
        input_output_aliases={7: 0} if more else {},
        compiler_params=pltpu.CompilerParams(vmem_limit_bytes=16 * 1024 * 1024),
        cost_estimate=pl.CostEstimate(
            flops=8 * rows * rows * wide,
            bytes_accessed=12 * rows * wide,
            transcendentals=2 * rows * rows * heads,
        ),
        name="context_attend",
    )(at, lengths, q, kv, bias, near, far, *more)


def swap(x, axis, k):
    return lax.ppermute(x, axis, [(i, i ^ k) for i in range(lax.axis_size(axis))])


def gather_hosts(x, hosts):
    near = jnp.stack([x] + [swap(x, "hst", k) for k in range(2, hosts, 2)], axis=0)
    return near, swap(near, "hst", 1)


def after(x, done):
    return lax.optimization_barrier((x, done))[0]


def scatter_anchor(kv, across, diagonal, below, groups):
    cores = groups // 2
    first = (lax.axis_index("hst") == 0) & (lax.axis_index("grp") == 0)
    send = lambda x, to: lax.ppermute(x, BOTH, [(0, to), (to, 0)])
    _, rows, width = kv.shape
    slabs, come = [], None
    for s in range(2):
        down = send(below[s], groups)
        if s:
            down = after(down, slabs[0])
        else:
            come = down
        got = send(diagonal[s], groups + cores) + send(across[s], cores) + down
        slabs.append(jnp.where(first, kv[s, : rows // 2, : width // 2], got))
    return slabs, come


def spread_anchor(slab, hosts, groups):
    cores = groups // 2
    wide = slab.shape[1] // cores
    piece = slab[:, :wide]
    for c in range(1, cores):
        pairs = [(x, x + c) for x in (0, cores)]
        piece = piece + lax.ppermute(slab[:, c * wide : (c + 1) * wide], "grp", pairs)
    shared = piece
    far = hosts // 2
    while far >= 2:
        pairs = [(h, h + far) for h in range(hosts) if h % (2 * far) < 2]
        piece = piece + lax.ppermute(piece, "hst", pairs)
        far //= 2
    return piece, shared


def per_device(queries, keys_values, token_ids, lengths, suffix_queries, suffix_kv):
    hosts, groups = lax.axis_size("hst"), lax.axis_size("grp")
    host, group = lax.axis_index("hst"), lax.axis_index("grp")
    rows = queries.shape[0]
    cores = groups // 2
    packed, below, across, diagonal = pack(keys_values, groups)
    slabs, down = scatter_anchor(keys_values, across, diagonal, below, groups)
    swapped = lax.all_to_all(after(packed, down), "grp", split_axis=0, concat_axis=0, tiled=True)
    spread = [spread_anchor(x, hosts, groups) for x in slabs]
    near = jnp.stack([x for x, _ in spread])
    gathered = gather_hosts(after(suffix_queries, spread[1][1]), hosts)
    seen = (token_ids.reshape(-1, rows) >= NAMB) & (jnp.arange(rows)[None, :] < lengths[:, None])
    bias = jnp.where(seen, 0.0, NEG).astype(jnp.float32)
    suffix = functools.partial(suffix_attend, jnp.stack([host]), *gathered, swapped, suffix_kv, bias)
    heads = suffix_queries.shape[1] // HSZ
    early = max(1, heads - 1)
    far, other_near = swap(near, "hst", 1), swap(after(near, swapped), "grp", cores)
    far, other_near, parts = lax.optimization_barrier((far, other_near, suffix(0, early, None)))
    other_far = swap(far, "grp", cores)
    by_core = [[swap(x, "grp", k) for x in (near, far)] for k in range(1, cores)]
    if heads > early:
        parts = suffix(early, heads - early, parts)
    by_core, parts = lax.optimization_barrier((by_core, parts))
    parts = parts.astype(jnp.float16)
    coded = lax.all_to_all(parts, "hst", split_axis=0, concat_axis=0, tiled=True)
    held = {0: after([near, far], parts), cores: [other_near, other_far]}

    def context(k, before):
        at = jnp.stack([host * groups + group, group ^ k, host % 2])
        return context_attend(at, lengths, queries, keys_values, bias, *held[k], before)

    context_out = context(0, None)
    for k in range(1, cores):
        held[k] = by_core[k - 1]
        context_out = context(k, context_out)
    other = after(held[cores], context_out)
    for k in range(1, cores):
        held[cores ^ k] = [swap(x, "grp", k) for x in other]
    for k in range(cores, groups):
        context_out = context(k, context_out)
    return (context_out, combine(coded.astype(jnp.float32)))


def solution(mesh):
    return jax.shard_map(
        per_device,
        mesh=mesh,
        in_specs=(
            P(("hst", "grp"), None),
            P(None, ("hst", "grp"), None),
            P(),
            P(),
            P("hst", "grp"),
            P(None, "hst", "grp"),
        ),
        out_specs=(P(("hst", "grp"), None), P("hst", "grp")),
        check_vma=False,
    )
```

```python
import functools
import math

import jax
import jax.numpy as jnp
from jax import lax
from jax.experimental import pallas as pl
from jax.experimental.pallas import tpu as pltpu
from jax.sharding import PartitionSpec as P

HSZ = 128
NAMB = 512
NEG = -1e30
FLOOR = -2000.0
EXTRA = 8
TILE = 256
C2 = math.log2(math.e) / math.sqrt(HSZ)
BOTH = ("hst", "grp")


def dot_t(a, b):
    return lax.dot_general(a, b, (((1,), (1,)), ((), ())), preferred_element_type=jnp.float32)


def dot(a, b):
    return lax.dot_general(a, b, (((1,), (0,)), ((), ())), preferred_element_type=jnp.float32)


def softmax(scores):
    top = functools.reduce(jnp.maximum, [jnp.max(s, axis=-1, keepdims=True) for s in scores])
    base = top * C2
    weights = [jnp.exp2(s * C2 - base) for s in scores]
    total = functools.reduce(jnp.add, [jnp.sum(w, axis=-1, keepdims=True) for w in weights])
    return base, total, [w.astype(jnp.bfloat16) for w in weights]


def pack_kernel(kv_ref, out_ref, *refs):
    below_refs, across_refs, diagonal_refs, (held, came, left) = refs[0:2], refs[2:4], refs[4:6], refs[6:]
    groups, _, rows, part = out_ref.shape
    few, wide, pieces = rows // 4, groups * part // 2, [(s, i) for s in range(2) for i in range(4)]
    arrive = {}
    for s, i in pieces:
        band = pl.ds(i * few, few)
        arrive[s, i] = pltpu.make_async_copy(kv_ref.at[s, band], held.at[s, band], came.at[s, i])
        arrive[s, i].start()
    leave = []
    for s, i in pieces:
        arrive[s, i].wait()
        band, place = pl.ds(i * few, few), pl.ds(i % 2 * few, few)
        right = held.at[s, band, pl.ds(wide, wide)]
        moves = [(right, (across_refs if i < 2 else diagonal_refs)[s].at[place])]
        if i >= 2:
            moves.append((held.at[s, band, pl.ds(0, wide)], below_refs[s].at[place]))
        moves += [(held.at[s, band, pl.ds(g * part, part)], out_ref.at[g, s, band]) for g in range(groups)]
        for n, (source, target) in enumerate(moves):
            leave.append(pltpu.make_async_copy(source, target, left.at[s, i, n]))
            leave[-1].start()
    for copy in leave:
        copy.wait()


def pack(kv, groups):
    _, rows, width = kv.shape
    anywhere = pl.BlockSpec(memory_space=pl.ANY)
    half = jax.ShapeDtypeStruct((rows // 2, width // 2), kv.dtype)
    out, *quarters = pl.pallas_call(
        pack_kernel,
        in_specs=[anywhere],
        out_specs=[anywhere] * 7,
        out_shape=[jax.ShapeDtypeStruct((groups, 2, rows, width // groups), kv.dtype)] + [half] * 6,
        scratch_shapes=[
            pltpu.VMEM(kv.shape, kv.dtype),
            pltpu.SemaphoreType.DMA((2, 4)),
            pltpu.SemaphoreType.DMA((2, 4, groups + 2)),
        ],
        cost_estimate=pl.CostEstimate(flops=0, bytes_accessed=6 * kv.size, transcendentals=0),
        name="pack_heads",
    )(kv)
    return out, quarters[:2], quarters[2:4], quarters[4:]


def pipelined(tasks, score, finish):
    ahead = score(tasks[0])
    for n, task in enumerate(tasks):
        scores = ahead
        if n + 1 < len(tasks):
            ahead = score(tasks[n + 1])
        finish(task, scores)


def suffix_kernel(at_ref, near_ref, far_ref, kv_ref, sk_ref, bias_ref, *rest):
    out_ref = rest[-1]
    host = at_ref[0]
    groups = kv_ref.shape[0]
    half, share, _ = near_ref.shape
    hosts = 2 * half
    chunk = lambda n: near_ref[n] if n < half else far_ref[n - half]
    apart = list(range(0, hosts, 2)) + list(range(1, hosts, 2))
    chunks = min(hosts, max(1, TILE // share))
    bias = [bias_ref[pl.ds(host * groups + g, 1), :] for g in range(groups)]
    values = [kv_ref[g, 1] for g in range(groups)] + [sk_ref[1]]

    def score(first):
        q = jnp.concatenate([chunk(first + c) for c in range(chunks)], axis=0)
        s = dot_t(q, sk_ref[0])
        row = lax.broadcasted_iota(jnp.int32, (share, share), 0)
        spos = host * share + lax.broadcasted_iota(jnp.int32, (share, share), 1)
        late = []
        for c in range(chunks):
            qpos = jnp.bitwise_xor(host, apart[first + c]) * share + row
            late.append(jnp.where(spos <= qpos, s[c * share : (c + 1) * share], NEG))
        return [dot_t(q, kv_ref[g, 0]) + bias[g] for g in range(groups)] + [jnp.concatenate(late, axis=0)]

    def finish(first, scores):
        base, total, weights = softmax(scores)
        mixed = functools.reduce(jnp.add, [dot(w, v) for w, v in zip(weights, values)])
        n = mixed / total
        size = jnp.max(jnp.abs(n), axis=-1, keepdims=True)
        shift = jnp.clip(jnp.floor(jnp.log2(size)), -100.0, 100.0)
        level = jnp.maximum(base + jnp.log2(total), FLOOR)
        whole = jnp.floor(level)
        rest = jnp.exp2(level - whole)
        coarse = jnp.round(rest * 512.0) * (1.0 / 512.0)
        fine = (rest - coarse) * 1024.0
        lane = lax.broadcasted_iota(jnp.int32, (chunks * share, HSZ), 1)
        stats = jnp.where(lane == 0, whole, jnp.where(lane == 1, coarse, jnp.where(lane == 2, fine, shift)))
        turned = stats.T
        n = n * jnp.exp2(-shift)
        for c in range(chunks):
            to = jnp.bitwise_xor(host, apart[first + c])
            out_ref[to, :share, :] = n[c * share : (c + 1) * share]
            out_ref[to, share : share + EXTRA, :share] = turned[:EXTRA, c * share : (c + 1) * share]

    pipelined(list(range(0, hosts, chunks)), score, finish)


def suffix_attend(host, near, far, kv, sk, bias, first, count, before):
    half, share, width = near.shape
    hosts = 2 * half
    more = [] if before is None else [before]
    groups, _, rows, _ = kv.shape
    seen = groups * rows + share
    column = lambda h, at: (0, 0, first + h)
    return pl.pallas_call(
        suffix_kernel,
        grid_spec=pltpu.PrefetchScalarGridSpec(
            num_scalar_prefetch=1,
            grid=(count,),
            in_specs=[
                pl.BlockSpec((half, share, HSZ), column),
                pl.BlockSpec((half, share, HSZ), column),
                pl.BlockSpec((groups, 2, rows, HSZ), lambda h, at: (0, 0, 0, first + h)),
                pl.BlockSpec((2, share, HSZ), column),
                pl.BlockSpec(bias.shape, lambda h, at: (0, 0)),
            ]
            + [pl.BlockSpec(memory_space=pl.ANY) for _ in more],
            out_specs=pl.BlockSpec((hosts, share + EXTRA, HSZ), column),
        ),
        out_shape=jax.ShapeDtypeStruct((hosts, share + EXTRA, width), jnp.float32),
        input_output_aliases={6: 0} if more else {},
        compiler_params=pltpu.CompilerParams(vmem_limit_bytes=16 * 1024 * 1024),
        cost_estimate=pl.CostEstimate(
            flops=8 * count * hosts * share * seen * HSZ,
            bytes_accessed=4 * count * (groups * rows + 3 * hosts * share) * HSZ,
            transcendentals=count * hosts * share * seen,
        ),
        name="suffix_attend",
    )(host, near, far, kv, sk, bias, *more)


def combine_kernel(in_ref, out_ref):
    hosts, tall, width = in_ref.shape
    share = tall - EXTRA
    for first in range(0, width, HSZ):
        head = slice(first, first + HSZ)
        whole, coarse, fine, shift = [in_ref[:, share + k, head] for k in range(4)]
        weight = jnp.exp2(whole - jnp.max(whole, axis=0, keepdims=True)) * (coarse + fine * (1.0 / 1024.0))
        factor = weight * jnp.exp2(shift) / jnp.sum(weight, axis=0, keepdims=True)
        factor = jnp.concatenate([factor, jnp.zeros((HSZ - hosts, HSZ), jnp.float32)], axis=0).T[:share, :]
        mixed = 0.0
        for g in range(hosts):
            mixed = mixed + factor[:, g : g + 1] * in_ref[g, :share, head]
        out_ref[:, head] = mixed.astype(out_ref.dtype)


def combine(parts):
    _, tall, width = parts.shape
    return pl.pallas_call(
        combine_kernel,
        in_specs=[pl.BlockSpec(memory_space=pltpu.VMEM)],
        out_specs=pl.BlockSpec(memory_space=pltpu.VMEM),
        out_shape=jax.ShapeDtypeStruct((tall - EXTRA, width), jnp.bfloat16),
        cost_estimate=pl.CostEstimate(flops=2 * parts.size, bytes_accessed=4 * parts.size, transcendentals=0),
        name="combine_groups",
    )(parts)


def context_kernel(at_ref, len_ref, q_ref, kv_ref, bias_ref, near_ref, far_ref, *rest):
    out_ref, diag_ref = rest[-2:]
    block, odd = at_ref[0], at_ref[2]
    rows, width = q_ref.shape
    half = rows // 2
    own = bias_ref[pl.ds(block, 1), :]
    row = lax.broadcasted_iota(jnp.int32, (half, half), 0)
    col = lax.broadcasted_iota(jnp.int32, (half, half), 1)
    for t in range(2):
        ok = own[:, t * half : (t + 1) * half]
        diag_ref[t] = jnp.where(col == row, 0.0, jnp.where(col < row, ok, NEG))
    low, high = bias_ref[0:1, :half], bias_ref[0:1, half:]
    near_bias = jnp.where(block > 0, jnp.where(odd == 0, low, high), NEG)
    far_bias = jnp.where(block > 0, jnp.where(odd == 0, high, low), NEG)

    def score(task):
        first, t = task
        head = slice(first, first + HSZ)
        q = q_ref[t * half : (t + 1) * half, head]
        scores = [dot_t(q, near_ref[0, :, head]) + near_bias, dot_t(q, far_ref[0, :, head]) + far_bias]
        if t == 1:
            scores.append(dot_t(q, kv_ref[0, :half, head]) + own[:, :half])
        scores.append(dot_t(q, kv_ref[0, t * half : (t + 1) * half, head]) + diag_ref[t])
        return scores

    def finish(task, scores):
        first, t = task
        head = slice(first, first + HSZ)
        _, total, weights = softmax(scores)
        values = [near_ref[1, :, head], far_ref[1, :, head]]
        values += [kv_ref[1, u * half : (u + 1) * half, head] for u in range(t + 1)]
        mixed = functools.reduce(jnp.add, [dot(w, v) for w, v in zip(weights, values)])
        place = t * half + lax.broadcasted_iota(jnp.int32, mixed.shape, 0)
        out = jnp.where(place < len_ref[block], mixed / total, 0.0)
        out_ref[t * half : (t + 1) * half, head] = out.astype(out_ref.dtype)

    pipelined([(first, t) for first in range(0, width, HSZ) for t in range(2)], score, finish)


def context_attend(at, lengths, q, kv, bias, near, far, before):
    rows, width = q.shape
    _, half, wide = near.shape
    heads = wide // HSZ
    both = lambda i, at, n: (0, 0, at[1])
    more = [] if before is None else [before]
    return pl.pallas_call(
        context_kernel,
        grid_spec=pltpu.PrefetchScalarGridSpec(
            num_scalar_prefetch=2,
            grid=(1,),
            in_specs=[
                pl.BlockSpec((rows, wide), lambda i, at, n: (0, at[1])),
                pl.BlockSpec((2, rows, wide), both),
                pl.BlockSpec(bias.shape, lambda i, *_: (0, 0)),
                pl.BlockSpec((2, half, wide), lambda i, *_: (0, 0, 0)),
                pl.BlockSpec((2, half, wide), lambda i, *_: (0, 0, 0)),
            ]
            + [pl.BlockSpec(memory_space=pl.ANY) for _ in more],
            out_specs=pl.BlockSpec((rows, wide), lambda i, at, n: (0, at[1])),
            scratch_shapes=[pltpu.VMEM((2, half, half), jnp.float32)],
        ),
        out_shape=jax.ShapeDtypeStruct((rows, width), q.dtype),
        input_output_aliases={7: 0} if more else {},
        compiler_params=pltpu.CompilerParams(vmem_limit_bytes=60 * 1024 * 1024),
        cost_estimate=pl.CostEstimate(
            flops=8 * rows * rows * wide,
            bytes_accessed=12 * rows * wide,
            transcendentals=2 * rows * rows * heads,
        ),
        name="context_attend",
    )(at, lengths, q, kv, bias, near, far, *more)


def swap(x, axis, k):
    return lax.ppermute(x, axis, [(i, i ^ k) for i in range(lax.axis_size(axis))])


def gather_hosts(x, hosts):
    near = jnp.stack([x] + [swap(x, "hst", k) for k in range(2, hosts, 2)], axis=0)
    return near, swap(near, "hst", 1)


def after(x, done):
    return lax.optimization_barrier((x, done))[0]


def scatter_anchor(kv, across, diagonal, below, groups):
    cores = groups // 2
    first = (lax.axis_index("hst") == 0) & (lax.axis_index("grp") == 0)
    send = lambda x, to: lax.ppermute(x, BOTH, [(0, to), (to, 0)])
    _, rows, width = kv.shape
    slabs, come = [], None
    for s in range(2):
        down = send(below[s], groups)
        if s:
            down = after(down, slabs[0])
        else:
            come = down
        got = send(diagonal[s], groups + cores) + send(across[s], cores) + down
        slabs.append(jnp.where(first, kv[s, : rows // 2, : width // 2], got))
    return slabs, come


def spread_anchor(slab, hosts, groups):
    cores = groups // 2
    wide = slab.shape[1] // cores
    piece = slab[:, :wide]
    for c in range(1, cores):
        pairs = [(x, x + c) for x in (0, cores)]
        piece = piece + lax.ppermute(slab[:, c * wide : (c + 1) * wide], "grp", pairs)
    shared = piece
    far = hosts // 2
    while far >= 2:
        pairs = [(h, h + far) for h in range(hosts) if h % (2 * far) < 2]
        piece = piece + lax.ppermute(piece, "hst", pairs)
        far //= 2
    return piece, shared


def per_device(queries, keys_values, token_ids, lengths, suffix_queries, suffix_kv):
    hosts, groups = lax.axis_size("hst"), lax.axis_size("grp")
    host, group = lax.axis_index("hst"), lax.axis_index("grp")
    rows = queries.shape[0]
    cores = groups // 2
    packed, below, across, diagonal = pack(keys_values, groups)
    slabs, down = scatter_anchor(keys_values, across, diagonal, below, groups)
    swapped = lax.all_to_all(after(packed, down), "grp", split_axis=0, concat_axis=0, tiled=True)
    spread = [spread_anchor(x, hosts, groups) for x in slabs]
    near = jnp.stack([x for x, _ in spread])
    gathered = gather_hosts(after(suffix_queries, spread[1][1]), hosts)
    seen = (token_ids.reshape(-1, rows) >= NAMB) & (jnp.arange(rows)[None, :] < lengths[:, None])
    bias = jnp.where(seen, 0.0, NEG).astype(jnp.float32)
    suffix = functools.partial(suffix_attend, jnp.stack([host]), *gathered, swapped, suffix_kv, bias)
    heads = suffix_queries.shape[1] // HSZ
    early = max(1, heads - 1)
    far, other_near = swap(near, "hst", 1), swap(after(near, swapped), "grp", cores)
    far, other_near, parts = lax.optimization_barrier((far, other_near, suffix(0, early, None)))
    other_far = swap(far, "grp", cores)
    by_core = [[swap(x, "grp", k) for x in (near, far)] for k in range(1, cores)]
    if heads > early:
        parts = suffix(early, heads - early, parts)
    by_core, parts = lax.optimization_barrier((by_core, parts))
    parts = parts.astype(jnp.float16)
    coded = lax.all_to_all(parts, "hst", split_axis=0, concat_axis=0, tiled=True)
    held = {0: after([near, far], parts), cores: [other_near, other_far]}

    def context(k, before):
        at = jnp.stack([host * groups + group, group ^ k, host % 2])
        return context_attend(at, lengths, queries, keys_values, bias, *held[k], before)

    context_out = context(0, None)
    for k in range(1, cores):
        held[k] = by_core[k - 1]
        context_out = context(k, context_out)
    other = after(held[cores], context_out)
    for k in range(1, cores):
        held[cores ^ k] = [swap(x, "grp", k) for x in other]
    for k in range(cores, groups):
        context_out = context(k, context_out)
    return (context_out, combine(coded.astype(jnp.float32)))


def solution(mesh):
    return jax.shard_map(
        per_device,
        mesh=mesh,
        in_specs=(
            P(("hst", "grp"), None),
            P(None, ("hst", "grp"), None),
            P(),
            P(),
            P("hst", "grp"),
            P(None, "hst", "grp"),
        ),
        out_specs=(P(("hst", "grp"), None), P("hst", "grp")),
        check_vma=False,
    )
```

```python
import functools
import math

import jax
import jax.numpy as jnp
from jax import lax
from jax.experimental import pallas as pl
from jax.experimental.pallas import tpu as pltpu
from jax.sharding import PartitionSpec as P

HSZ = 128
NAMB = 512
NEG = -1e30
FLOOR = -2000.0
EXTRA = 8
TILE = 256
C2 = math.log2(math.e) / math.sqrt(HSZ)
BOTH = ("hst", "grp")


def dot_t(a, b):
    return lax.dot_general(a, b, (((1,), (1,)), ((), ())), preferred_element_type=jnp.float32)


def dot(a, b):
    return lax.dot_general(a, b, (((1,), (0,)), ((), ())), preferred_element_type=jnp.float32)


def softmax(scores):
    top = functools.reduce(jnp.maximum, [jnp.max(s, axis=-1, keepdims=True) for s in scores])
    base = top * C2
    weights = [jnp.exp2(s * C2 - base) for s in scores]
    total = functools.reduce(jnp.add, [jnp.sum(w, axis=-1, keepdims=True) for w in weights])
    return base, total, [w.astype(jnp.bfloat16) for w in weights]


def pack_kernel(kv_ref, out_ref, *refs):
    below_refs, across_refs, diagonal_refs, (held, came, left) = refs[0:2], refs[2:4], refs[4:6], refs[6:]
    groups, _, rows, part = out_ref.shape
    few, wide, pieces = rows // 4, groups * part // 2, [(s, i) for s in range(2) for i in range(4)]
    arrive = {}
    for s, i in pieces:
        band = pl.ds(i * few, few)
        arrive[s, i] = pltpu.make_async_copy(kv_ref.at[s, band], held.at[s, band], came.at[s, i])
        arrive[s, i].start()
    leave = []
    for s, i in pieces:
        arrive[s, i].wait()
        band, place = pl.ds(i * few, few), pl.ds(i % 2 * few, few)
        right = held.at[s, band, pl.ds(wide, wide)]
        moves = [(right, (across_refs if i < 2 else diagonal_refs)[s].at[place])]
        if i >= 2:
            moves.append((held.at[s, band, pl.ds(0, wide)], below_refs[s].at[place]))
        moves += [(held.at[s, band, pl.ds(g * part, part)], out_ref.at[g, s, band]) for g in range(groups)]
        for n, (source, target) in enumerate(moves):
            leave.append(pltpu.make_async_copy(source, target, left.at[s, i, n]))
            leave[-1].start()
    for copy in leave:
        copy.wait()


def pack(kv, groups):
    _, rows, width = kv.shape
    anywhere = pl.BlockSpec(memory_space=pl.ANY)
    half = jax.ShapeDtypeStruct((rows // 2, width // 2), kv.dtype)
    out, *quarters = pl.pallas_call(
        pack_kernel,
        in_specs=[anywhere],
        out_specs=[anywhere] * 7,
        out_shape=[jax.ShapeDtypeStruct((groups, 2, rows, width // groups), kv.dtype)] + [half] * 6,
        scratch_shapes=[
            pltpu.VMEM(kv.shape, kv.dtype),
            pltpu.SemaphoreType.DMA((2, 4)),
            pltpu.SemaphoreType.DMA((2, 4, groups + 2)),
        ],
        cost_estimate=pl.CostEstimate(flops=0, bytes_accessed=6 * kv.size, transcendentals=0),
        name="pack_heads",
    )(kv)
    return out, quarters[:2], quarters[2:4], quarters[4:]


def pipelined(tasks, score, finish):
    ahead = score(tasks[0])
    for n, task in enumerate(tasks):
        scores = ahead
        if n + 1 < len(tasks):
            ahead = score(tasks[n + 1])
        finish(task, scores)


def suffix_kernel(at_ref, near_ref, far_ref, kv_ref, sk_ref, bias_ref, *rest):
    out_ref = rest[-1]
    host = at_ref[0]
    groups = kv_ref.shape[0]
    half, share, _ = near_ref.shape
    hosts = 2 * half
    chunk = lambda n: near_ref[n] if n < half else far_ref[n - half]
    apart = list(range(0, hosts, 2)) + list(range(1, hosts, 2))
    chunks = min(hosts, max(1, TILE // share))
    bias = [bias_ref[pl.ds(host * groups + g, 1), :] for g in range(groups)]
    values = [kv_ref[g, 1] for g in range(groups)] + [sk_ref[1]]

    def score(first):
        q = jnp.concatenate([chunk(first + c) for c in range(chunks)], axis=0)
        s = dot_t(q, sk_ref[0])
        row = lax.broadcasted_iota(jnp.int32, (share, share), 0)
        spos = host * share + lax.broadcasted_iota(jnp.int32, (share, share), 1)
        late = []
        for c in range(chunks):
            qpos = jnp.bitwise_xor(host, apart[first + c]) * share + row
            late.append(jnp.where(spos <= qpos, s[c * share : (c + 1) * share], NEG))
        return [dot_t(q, kv_ref[g, 0]) + bias[g] for g in range(groups)] + [jnp.concatenate(late, axis=0)]

    def finish(first, scores):
        base, total, weights = softmax(scores)
        mixed = functools.reduce(jnp.add, [dot(w, v) for w, v in zip(weights, values)])
        n = mixed / total
        size = jnp.max(jnp.abs(n), axis=-1, keepdims=True)
        shift = jnp.clip(jnp.floor(jnp.log2(size)), -100.0, 100.0)
        level = jnp.maximum(base + jnp.log2(total), FLOOR)
        whole = jnp.floor(level)
        rest = jnp.exp2(level - whole)
        coarse = jnp.round(rest * 512.0) * (1.0 / 512.0)
        fine = (rest - coarse) * 1024.0
        lane = lax.broadcasted_iota(jnp.int32, (chunks * share, HSZ), 1)
        stats = jnp.where(lane == 0, whole, jnp.where(lane == 1, coarse, jnp.where(lane == 2, fine, shift)))
        turned = stats.T
        n = n * jnp.exp2(-shift)
        for c in range(chunks):
            to = jnp.bitwise_xor(host, apart[first + c])
            out_ref[to, :share, :] = n[c * share : (c + 1) * share]
            out_ref[to, share : share + EXTRA, :share] = turned[:EXTRA, c * share : (c + 1) * share]

    pipelined(list(range(0, hosts, chunks)), score, finish)


def suffix_attend(host, near, far, kv, sk, bias, first, count, before):
    half, share, width = near.shape
    hosts = 2 * half
    more = [] if before is None else [before]
    groups, _, rows, _ = kv.shape
    seen = groups * rows + share
    column = lambda h, at: (0, 0, first + h)
    return pl.pallas_call(
        suffix_kernel,
        grid_spec=pltpu.PrefetchScalarGridSpec(
            num_scalar_prefetch=1,
            grid=(count,),
            in_specs=[
                pl.BlockSpec((half, share, HSZ), column),
                pl.BlockSpec((half, share, HSZ), column),
                pl.BlockSpec((groups, 2, rows, HSZ), lambda h, at: (0, 0, 0, first + h)),
                pl.BlockSpec((2, share, HSZ), column),
                pl.BlockSpec(bias.shape, lambda h, at: (0, 0)),
            ]
            + [pl.BlockSpec(memory_space=pl.ANY) for _ in more],
            out_specs=pl.BlockSpec((hosts, share + EXTRA, HSZ), column),
        ),
        out_shape=jax.ShapeDtypeStruct((hosts, share + EXTRA, width), jnp.float32),
        input_output_aliases={6: 0} if more else {},
        compiler_params=pltpu.CompilerParams(vmem_limit_bytes=16 * 1024 * 1024),
        cost_estimate=pl.CostEstimate(
            flops=8 * count * hosts * share * seen * HSZ,
            bytes_accessed=4 * count * (groups * rows + 3 * hosts * share) * HSZ,
            transcendentals=count * hosts * share * seen,
        ),
        name="suffix_attend",
    )(host, near, far, kv, sk, bias, *more)


def combine_kernel(in_ref, out_ref):
    hosts, tall, width = in_ref.shape
    share = tall - EXTRA
    for first in range(0, width, HSZ):
        head = slice(first, first + HSZ)
        whole, coarse, fine, shift = [in_ref[:, share + k, head] for k in range(4)]
        weight = jnp.exp2(whole - jnp.max(whole, axis=0, keepdims=True)) * (coarse + fine * (1.0 / 1024.0))
        factor = weight * jnp.exp2(shift) / jnp.sum(weight, axis=0, keepdims=True)
        factor = jnp.concatenate([factor, jnp.zeros((HSZ - hosts, HSZ), jnp.float32)], axis=0).T[:share, :]
        mixed = 0.0
        for g in range(hosts):
            mixed = mixed + factor[:, g : g + 1] * in_ref[g, :share, head]
        out_ref[:, head] = mixed.astype(out_ref.dtype)


def combine(parts):
    _, tall, width = parts.shape
    return pl.pallas_call(
        combine_kernel,
        in_specs=[pl.BlockSpec(memory_space=pltpu.VMEM)],
        out_specs=pl.BlockSpec(memory_space=pltpu.VMEM),
        out_shape=jax.ShapeDtypeStruct((tall - EXTRA, width), jnp.bfloat16),
        cost_estimate=pl.CostEstimate(flops=2 * parts.size, bytes_accessed=4 * parts.size, transcendentals=0),
        name="combine_groups",
    )(parts)


def context_kernel(at_ref, len_ref, q_ref, kv_ref, bias_ref, near_ref, far_ref, *rest):
    out_ref, diag_ref = rest[-2:]
    block, odd = at_ref[0], at_ref[2]
    rows, width = q_ref.shape
    half = rows // 2
    own = bias_ref[pl.ds(block, 1), :]
    row = lax.broadcasted_iota(jnp.int32, (half, half), 0)
    col = lax.broadcasted_iota(jnp.int32, (half, half), 1)
    for t in range(2):
        ok = own[:, t * half : (t + 1) * half]
        diag_ref[t] = jnp.where(col == row, 0.0, jnp.where(col < row, ok, NEG))
    low, high = bias_ref[0:1, :half], bias_ref[0:1, half:]
    near_bias = jnp.where(block > 0, jnp.where(odd == 0, low, high), NEG)
    far_bias = jnp.where(block > 0, jnp.where(odd == 0, high, low), NEG)

    def score(task):
        first, t = task
        head = slice(first, first + HSZ)
        q = q_ref[t * half : (t + 1) * half, head]
        scores = [dot_t(q, near_ref[0, :, head]) + near_bias, dot_t(q, far_ref[0, :, head]) + far_bias]
        if t == 1:
            scores.append(dot_t(q, kv_ref[0, :half, head]) + own[:, :half])
        scores.append(dot_t(q, kv_ref[0, t * half : (t + 1) * half, head]) + diag_ref[t])
        return scores

    def finish(task, scores):
        first, t = task
        head = slice(first, first + HSZ)
        _, total, weights = softmax(scores)
        values = [near_ref[1, :, head], far_ref[1, :, head]]
        values += [kv_ref[1, u * half : (u + 1) * half, head] for u in range(t + 1)]
        mixed = functools.reduce(jnp.add, [dot(w, v) for w, v in zip(weights, values)])
        place = t * half + lax.broadcasted_iota(jnp.int32, mixed.shape, 0)
        out = jnp.where(place < len_ref[block], mixed / total, 0.0)
        out_ref[t * half : (t + 1) * half, head] = out.astype(out_ref.dtype)

    pipelined([(first, t) for first in range(0, width, HSZ) for t in range(2)], score, finish)


def context_attend(at, lengths, q, kv, bias, near, far, before):
    rows, width = q.shape
    _, half, wide = near.shape
    heads = wide // HSZ
    both = lambda i, at, n: (0, 0, at[1])
    more = [] if before is None else [before]
    return pl.pallas_call(
        context_kernel,
        grid_spec=pltpu.PrefetchScalarGridSpec(
            num_scalar_prefetch=2,
            grid=(1,),
            in_specs=[
                pl.BlockSpec((rows, wide), lambda i, at, n: (0, at[1])),
                pl.BlockSpec((2, rows, wide), both),
                pl.BlockSpec(bias.shape, lambda i, *_: (0, 0)),
                pl.BlockSpec((2, half, wide), lambda i, *_: (0, 0, 0)),
                pl.BlockSpec((2, half, wide), lambda i, *_: (0, 0, 0)),
            ]
            + [pl.BlockSpec(memory_space=pl.ANY) for _ in more],
            out_specs=pl.BlockSpec((rows, wide), lambda i, at, n: (0, at[1])),
            scratch_shapes=[pltpu.VMEM((2, half, half), jnp.float32)],
        ),
        out_shape=jax.ShapeDtypeStruct((rows, width), q.dtype),
        input_output_aliases={7: 0} if more else {},
        compiler_params=pltpu.CompilerParams(vmem_limit_bytes=16 * 1024 * 1024),
        cost_estimate=pl.CostEstimate(
            flops=8 * rows * rows * wide,
            bytes_accessed=12 * rows * wide,
            transcendentals=2 * rows * rows * heads,
        ),
        name="context_attend",
    )(at, lengths, q, kv, bias, near, far, *more)


def swap(x, axis, k):
    return lax.ppermute(x, axis, [(i, i ^ k) for i in range(lax.axis_size(axis))])


def gather_hosts(x, hosts):
    near = jnp.stack([x] + [swap(x, "hst", k) for k in range(2, hosts, 2)], axis=0)
    return near, swap(near, "hst", 1)


def after(x, done):
    return lax.optimization_barrier((x, done))[0]


def scatter_anchor(kv, across, diagonal, below, groups):
    cores = groups // 2
    first = (lax.axis_index("hst") == 0) & (lax.axis_index("grp") == 0)
    send = lambda x, to: lax.ppermute(x, BOTH, [(0, to), (to, 0)])
    _, rows, width = kv.shape
    slabs, come = [], None
    for s in range(2):
        down = send(below[s], groups)
        if s:
            down = after(down, slabs[0])
        else:
            come = down
        got = send(diagonal[s], groups + cores) + send(across[s], cores) + down
        slabs.append(jnp.where(first, kv[s, : rows // 2, : width // 2], got))
    return slabs, come


def spread_anchor(slab, hosts, groups):
    cores = groups // 2
    wide = slab.shape[1] // cores
    piece = slab[:, :wide]
    for c in range(1, cores):
        pairs = [(x, x + c) for x in (0, cores)]
        piece = piece + lax.ppermute(slab[:, c * wide : (c + 1) * wide], "grp", pairs)
    shared = piece
    far = hosts // 2
    while far >= 2:
        pairs = [(h, h + far) for h in range(hosts) if h % (2 * far) < 2]
        piece = piece + lax.ppermute(piece, "hst", pairs)
        far //= 2
    return piece, shared


def per_device(queries, keys_values, token_ids, lengths, suffix_queries, suffix_kv):
    hosts, groups = lax.axis_size("hst"), lax.axis_size("grp")
    host, group = lax.axis_index("hst"), lax.axis_index("grp")
    rows = queries.shape[0]
    cores = groups // 2
    packed, below, across, diagonal = pack(keys_values, groups)
    slabs, down = scatter_anchor(keys_values, across, diagonal, below, groups)
    swapped = lax.all_to_all(after(packed, down), "grp", split_axis=0, concat_axis=0, tiled=True)
    spread = [spread_anchor(x, hosts, groups) for x in slabs]
    near = jnp.stack([x for x, _ in spread])
    gathered = gather_hosts(after(suffix_queries, spread[1][1]), hosts)
    seen = (token_ids.reshape(-1, rows) >= NAMB) & (jnp.arange(rows)[None, :] < lengths[:, None])
    bias = jnp.where(seen, 0.0, NEG).astype(jnp.float32)
    suffix = functools.partial(suffix_attend, jnp.stack([host]), *gathered, swapped, suffix_kv, bias)
    heads = suffix_queries.shape[1] // HSZ
    early = max(1, heads - 1)
    far, other_near = swap(near, "hst", 1), swap(after(near, swapped), "grp", cores)
    far, other_near, parts = lax.optimization_barrier((far, other_near, suffix(0, early, None)))
    other_far = swap(far, "grp", cores)
    by_core = [[swap(x, "grp", k) for x in (near, far)] for k in range(1, cores)]
    if heads > early:
        parts = suffix(early, heads - early, parts)
    parts = parts.astype(jnp.float16)
    by_core = after(by_core, parts)
    coded = lax.all_to_all(parts, "hst", split_axis=0, concat_axis=0, tiled=True)
    held = {0: after([near, far], parts), cores: [other_near, other_far]}

    def context(k, before):
        at = jnp.stack([host * groups + group, group ^ k, host % 2])
        return context_attend(at, lengths, queries, keys_values, bias, *held[k], before)

    context_out = context(0, None)
    for k in range(1, cores):
        held[k] = by_core[k - 1]
        context_out = context(k, context_out)
    other = after(held[cores], context_out)
    for k in range(1, cores):
        held[cores ^ k] = [swap(x, "grp", k) for x in other]
    for k in range(cores, groups):
        context_out = context(k, context_out)
    return (context_out, combine(coded.astype(jnp.float32)))


def solution(mesh):
    return jax.shard_map(
        per_device,
        mesh=mesh,
        in_specs=(
            P(("hst", "grp"), None),
            P(None, ("hst", "grp"), None),
            P(),
            P(),
            P("hst", "grp"),
            P(None, "hst", "grp"),
        ),
        out_specs=(P(("hst", "grp"), None), P("hst", "grp")),
        check_vma=False,
    )
```
